128 devices in a mesh: sec: 2 (over x_lo), grp: 16 (over y, x_hi, core), head: 4 (over z).
Axes of the slice: x: 4 (x_hi: 2, x_lo: 2; x = x_hi * 2 + x_lo), y: 4, z: 4, core: 2. Of those that a mesh axis runs over, the one named last changes fastest.
Arguments:
- turn_hidden: bfloat16 [16384, 8192], P(('sec', 'grp')), may hold values from -6 to 6
- w_key: bfloat16 [8192, 1024], P(None, 'head'), may hold values from -0.0625 to 0.0625
- w_value: bfloat16 [8192, 1024], P(None, 'head'), may hold values from -0.0625 to 0.0625
- turn_queries: bfloat16 [16384, 8192], P(('sec', 'grp'), 'head'), may hold values from -480 to 480
- turn_speaker: int32 [16384], replicated, may hold values from 0 to 3
- speaker_mask: int32 [8, 4, 4], replicated, may hold values from 0 to 1, as said below
- shard_block: int32 [32], replicated, may hold values from 0 to 3, as said below
- context_keys: bfloat16 [65536, 1024], P(('sec', 'grp'), 'head'), may hold values from -6 to 6
- context_values: bfloat16 [65536, 1024], P(('sec', 'grp'), 'head'), may hold values from -6 to 6
- context_length: int32 [8], replicated, may hold values from 512 to 2048, as said below
- decode_home: int32 [32], replicated, may hold values from 0 to 7, as said below
- step_hidden: bfloat16 [512, 4, 8192], P(('sec', 'grp')), may hold values from -6 to 6
- step_queries: bfloat16 [512, 4, 8192], P(('sec', 'grp'), None, 'head'), may hold values from -480 to 480
- row_speaker: int32 [512], P(('sec', 'grp')), may hold values from 0 to 3
Outputs:
- turn_attention: bfloat16 [16384, 8192], P(('sec', 'grp'), 'head')
- step_attention: bfloat16 [512, 4, 8192], P(('sec', 'grp'), None, 'head')
The draws below stay inside these ranges and needn't reach their ends.
Inputs may be any that keep to these rules, and one draw needn't show every extreme that they name: Every speaker may read its own tokens: speaker_mask[d, a, a] = 1. `shard_block`: each aligned group of 4 entries (the 4 shards of one dialogue, shards 4 d to 4 d + 3) is a permutation of 0 to 3. `context_length`: some dialogue has exactly 2048 live positions. `decode_home`: every dialogue is served by at least one decode group.
All inputs are finite; a program needn't handle non-finite values.
Results may differ from the reference program's by a relative error of at most 0.012.
The reference program's roundings to bfloat16 on the way count: a program that leaves them out, or rounds other values in their place, can miss the bound.
Values may be sent and summed in bfloat16 or wider, within the bound.
No kernel may reach another device: no remote copies, remote signals or barrier semaphores. Data moves between devices by JAX's collectives and lax.ppermute only.
A program may use at most 192 MiB of HBM per device.

```python
import math
import jax
import jax.numpy as jnp
from jax import lax

D = 8192
HQ = 64
KVH = 8
HD = 128
SPK = 4
TURN = 2048
STEPS = 4
CTX = 2048
ROWS_DG = 16
SHARD = 512
SHARDS = 32
DIALOGS = 8
ROWS = 512


def scaled_queries(key, shape):
    base = jnp.clip(jax.random.normal(key, shape, jnp.float32), -8.0, 8.0)
    return base.astype(jnp.bfloat16)


def draw_turn_queries(key, part):
    key = jax.random.fold_in(key, 11)
    return scaled_queries(key, (SHARDS * SHARD, HQ * HD))


def draw_step_queries(key, part):
    key = jax.random.fold_in(key, 12)
    return scaled_queries(key, (ROWS, STEPS, HQ * HD))


def draw_speaker_mask(key, part):
    key = jax.random.fold_in(key, 13)
    bits = jax.random.randint(key, (DIALOGS, SPK, SPK), 0, 2, dtype=jnp.int32)
    diagonal = jnp.arange(SPK)[:, None] == jnp.arange(SPK)[None, :]
    return jnp.where(diagonal[None], 1, bits).astype(jnp.int32)


def draw_shard_block(key, part):
    key = jax.random.fold_in(key, 14)
    subkeys = jax.random.split(key, DIALOGS)
    orders = jax.vmap(lambda sub_key: jax.random.permutation(sub_key, 4))(subkeys)
    return orders.reshape(-1).astype(jnp.int32)


def draw_context_length(key, part):
    key = jax.random.fold_in(key, 15)
    lengths = jax.random.randint(jax.random.fold_in(key, 1), (DIALOGS,), CTX // 4, CTX + 1, dtype=jnp.int32)
    chosen = jax.random.randint(jax.random.fold_in(key, 2), (), 0, DIALOGS, dtype=jnp.int32)
    return jnp.where(jnp.arange(DIALOGS, dtype=jnp.int32) == chosen, CTX, lengths).astype(jnp.int32)


def draw_decode_home(key, part):
    key = jax.random.fold_in(key, 16)
    first = jax.random.permutation(jax.random.fold_in(key, 1), DIALOGS).astype(jnp.int32)
    others = jax.random.randint(jax.random.fold_in(key, 2), (SHARDS - DIALOGS,), 0, DIALOGS, dtype=jnp.int32)
    joined = jnp.concatenate([first, others])
    order = jax.random.permutation(jax.random.fold_in(key, 3), SHARDS)
    return joined[order].astype(jnp.int32)


def set_ends(entries, key, least, top_value):
    longest = entries.shape.index(max(entries.shape))
    spots = []
    for shift in (0, 1):
        where = [jax.random.randint(jax.random.fold_in(key, axis), (), 0, length) for axis, length in enumerate(entries.shape)]
        where[longest] = (where[longest] + shift) % entries.shape[longest]
        spots.append(tuple(where))
    return entries.at[spots[0]].set(least).at[spots[1]].set(top_value)


def block_levels(own_key, dims, cuts, smallest, top_value):
    factor_of, own = 1.0, jax.random.fold_in(own_key, 6)
    for axis_at, parts in cuts:
        draws = jnp.exp(jax.random.uniform(jax.random.fold_in(own, axis_at), (parts,), jnp.float32, smallest / len(cuts), top_value / len(cuts)))
        factor_of = factor_of * jnp.repeat(draws, dims[axis_at] // parts).reshape([-1 if axis == axis_at else 1 for axis in range(len(dims))])
    return factor_of


def gaussian(stream_key, shape, deviation, most, shards=(), kind=jnp.bfloat16):
    drawn = jax.random.normal(stream_key, shape, jnp.float32) * deviation
    if len(shards) > 0:
        drawn = block_levels(stream_key, shape, shards, -0.22, 0.18) * drawn
    return jnp.clip(drawn, min=-most, max=most).astype(kind)


def setup_inputs(seed: int = 0) -> dict:
    key_list = jax.random.split(jax.random.key(seed), 15)
    turn_hidden = gaussian(key_list[0], (SHARDS * SHARD, D), 1.0, 6.0, ((0, 32),))
    w_key = gaussian(key_list[1], (D, KVH * HD), D ** -0.5, 0.0625, ((1, 4),))
    w_value = gaussian(key_list[2], (D, KVH * HD), D ** -0.5, 0.0625, ((1, 4),))
    turn_queries = draw_turn_queries(jax.random.fold_in(key_list[14], 71), 0)
    turn_speaker = set_ends(jax.random.randint(key_list[4], (SHARDS * SHARD,), 0, SPK), jax.random.fold_in(key_list[4], 1), 0, SPK - 1).astype(jnp.int32)
    speaker_mask = draw_speaker_mask(jax.random.fold_in(key_list[14], 71), 0)
    shard_block = draw_shard_block(jax.random.fold_in(key_list[14], 71), 0)
    context_keys = gaussian(key_list[7], (SHARDS * CTX, KVH * HD), 1.0, 6.0, ((0, 32), (1, 4)))
    context_values = gaussian(key_list[8], (SHARDS * CTX, KVH * HD), 1.0, 6.0, ((0, 32), (1, 4)))
    context_length = draw_context_length(jax.random.fold_in(key_list[14], 71), 0)
    decode_home = draw_decode_home(jax.random.fold_in(key_list[14], 71), 0)
    step_hidden = gaussian(key_list[11], (ROWS, STEPS, D), 1.0, 6.0, ((0, 32),))
    step_queries = draw_step_queries(jax.random.fold_in(key_list[14], 71), 0)
    row_speaker = set_ends(jax.random.randint(key_list[13], (ROWS,), 0, SPK), jax.random.fold_in(key_list[13], 1), 0, SPK - 1).astype(jnp.int32)
    return {"turn_hidden": turn_hidden, "w_key": w_key, "w_value": w_value, "turn_queries": turn_queries, "turn_speaker": turn_speaker, "speaker_mask": speaker_mask, "shard_block": shard_block, "context_keys": context_keys, "context_values": context_values, "context_length": context_length, "decode_home": decode_home, "step_hidden": step_hidden, "step_queries": step_queries, "row_speaker": row_speaker}


big_negative = -1e+30

def lookup_allowed(table, speakers_a, speakers_b):
    return table[speakers_a][:, speakers_b] == 1

def rounded_weights(weights):
    return lax.optimization_barrier(weights.astype(jnp.bfloat16)).astype(jnp.float32)

def reference(turn_hidden, w_key, w_value, turn_queries, turn_speaker, speaker_mask, shard_block, context_keys, context_values, context_length, decode_home, step_hidden, step_queries, row_speaker):
    q_per_kv = HQ // KVH
    score_scale = 1.0 / math.sqrt(HD)
    new_keys = jnp.dot(turn_hidden, w_key, preferred_element_type=jnp.float32).astype(jnp.bfloat16)
    new_values = jnp.dot(turn_hidden, w_value, preferred_element_type=jnp.float32).astype(jnp.bfloat16)
    positions = (shard_block[:, None] * SHARD + jnp.arange(SHARD, dtype=jnp.int32)[None, :]).reshape(-1)

    def prefill_dialog(dialog_id):
        first = (dialog_id * TURN).astype(jnp.int32)
        queries = lax.dynamic_slice_in_dim(turn_queries, first, TURN, 0).astype(jnp.float32)
        queries = queries.reshape(TURN, KVH, q_per_kv, HD).transpose(1, 0, 2, 3)
        key_block = lax.dynamic_slice_in_dim(new_keys, first, TURN, 0).astype(jnp.float32).reshape(TURN, KVH, HD).transpose(1, 0, 2)
        value_block = lax.dynamic_slice_in_dim(new_values, first, TURN, 0).astype(jnp.float32).reshape(TURN, KVH, HD).transpose(1, 0, 2)
        spk = lax.dynamic_slice_in_dim(turn_speaker, first, TURN, 0)
        pos = lax.dynamic_slice_in_dim(positions, first, TURN, 0)
        visible = lookup_allowed(speaker_mask[dialog_id], spk, spk) & (pos[None, :] <= pos[:, None])

        def per_head(items):
            q_head, k_head, v_head = items
            scores = jnp.einsum('qgd,td->gqt', q_head, k_head) * score_scale
            top = lax.optimization_barrier(jnp.max(jnp.where(visible[None], scores, big_negative), axis=-1, keepdims=True))
            weights = jnp.where(visible[None], jnp.exp(scores - top), 0.0)
            totals = lax.optimization_barrier(jnp.sum(weights, axis=-1, keepdims=True))
            mixed = jnp.einsum('gqt,td->gqd', rounded_weights(weights), v_head) / totals
            return mixed
        outputs = lax.map(per_head, (queries, key_block, value_block))
        return outputs.transpose(2, 0, 1, 3).reshape(TURN, HQ * HD).astype(jnp.bfloat16)
    turn_attention = lax.map(prefill_dialog, jnp.arange(DIALOGS, dtype=jnp.int32)).reshape(SHARDS * SHARD, HQ * HD)
    flat_steps = step_hidden.reshape(ROWS * STEPS, D)
    step_keys = jnp.dot(flat_steps, w_key, preferred_element_type=jnp.float32).astype(jnp.bfloat16).reshape(ROWS, STEPS, KVH, HD)
    step_values = jnp.dot(flat_steps, w_value, preferred_element_type=jnp.float32).astype(jnp.bfloat16).reshape(ROWS, STEPS, KVH, HD)

    def decode_group(group_id):
        dialog_id = decode_home[group_id]
        length = context_length[dialog_id]
        row_first = (group_id * ROWS_DG).astype(jnp.int32)
        queries = lax.dynamic_slice_in_dim(step_queries, row_first, ROWS_DG, 0).astype(jnp.float32).reshape(ROWS_DG, STEPS, KVH, q_per_kv, HD)
        ctx_k = lax.dynamic_slice_in_dim(context_keys, (group_id * CTX).astype(jnp.int32), CTX, 0).astype(jnp.float32).reshape(CTX, KVH, HD)
        ctx_v = lax.dynamic_slice_in_dim(context_values, (group_id * CTX).astype(jnp.int32), CTX, 0).astype(jnp.float32).reshape(CTX, KVH, HD)
        turn_first = (dialog_id * TURN).astype(jnp.int32)
        turn_k = lax.dynamic_slice_in_dim(new_keys, turn_first, TURN, 0).astype(jnp.float32).reshape(TURN, KVH, HD)
        turn_v = lax.dynamic_slice_in_dim(new_values, turn_first, TURN, 0).astype(jnp.float32).reshape(TURN, KVH, HD)
        own_k = lax.dynamic_slice_in_dim(step_keys, row_first, ROWS_DG, 0).astype(jnp.float32)
        own_v = lax.dynamic_slice_in_dim(step_values, row_first, ROWS_DG, 0).astype(jnp.float32)
        spk_rows = lax.dynamic_slice_in_dim(row_speaker, row_first, ROWS_DG, 0)
        spk_turn = lax.dynamic_slice_in_dim(turn_speaker, turn_first, TURN, 0)
        mask_ctx = (jnp.arange(CTX, dtype=jnp.int32) < length)[None, None, None, None, :]
        mask_turn = lookup_allowed(speaker_mask[dialog_id], spk_rows, spk_turn)[:, None, None, None, :]
        mask_own = (jnp.arange(STEPS)[None, :] <= jnp.arange(STEPS)[:, None])[None, :, None, None, :]
        s_ctx = jnp.einsum('rskgd,ckd->rskgc', queries, ctx_k) * score_scale
        s_turn = jnp.einsum('rskgd,tkd->rskgt', queries, turn_k) * score_scale
        s_own = jnp.einsum('rskgd,rukd->rskgu', queries, own_k) * score_scale
        top = jnp.maximum(lax.optimization_barrier(jnp.max(jnp.where(mask_ctx, s_ctx, big_negative), axis=-1, keepdims=True)), lax.optimization_barrier(jnp.max(jnp.where(mask_turn, s_turn, big_negative), axis=-1, keepdims=True)))
        top = jnp.maximum(top, lax.optimization_barrier(jnp.max(jnp.where(mask_own, s_own, big_negative), axis=-1, keepdims=True)))
        p_ctx = jnp.where(mask_ctx, jnp.exp(s_ctx - top), 0.0)
        p_turn = jnp.where(mask_turn, jnp.exp(s_turn - top), 0.0)
        p_own = jnp.where(mask_own, jnp.exp(s_own - top), 0.0)
        totals = lax.optimization_barrier(jnp.sum(p_ctx, axis=-1, keepdims=True)) + lax.optimization_barrier(jnp.sum(p_turn, axis=-1, keepdims=True)) + lax.optimization_barrier(jnp.sum(p_own, axis=-1, keepdims=True))
        mixed = jnp.einsum('rskgc,ckd->rskgd', rounded_weights(p_ctx), ctx_v)
        mixed = mixed + jnp.einsum('rskgt,tkd->rskgd', rounded_weights(p_turn), turn_v)
        mixed = mixed + jnp.einsum('rskgu,rukd->rskgd', rounded_weights(p_own), own_v)
        return (mixed / totals).reshape(ROWS_DG, STEPS, HQ * HD).astype(jnp.bfloat16)
    step_attention = lax.map(decode_group, jnp.arange(SHARDS, dtype=jnp.int32)).reshape(ROWS, STEPS, HQ * HD)
    return (turn_attention, step_attention)
```

```python
import functools
import math

import jax
import jax.numpy as jnp
from jax import lax
from jax.experimental import pallas as pl
from jax.experimental.pallas import tpu as pltpu
from jax.sharding import Mesh
from jax.sharding import PartitionSpec as P

HQ = 64
KVH = 8
HD = 128
SPK = 4
GQ = HQ // KVH

HIDE = -1e30
SCALE = math.log2(math.e) / math.sqrt(HD)
NT = (((1,), (1,)), ((), ()))
F32 = jnp.float32
BF16 = jnp.bfloat16
VMEM_LIMIT = 56 * 2**20

S_OWN, S_SIB, S_FAR, S_FARSIB, S_REL, S_WHICH, S_SEL, S_LEN, S_XP = 0, 1, 2, 3, 4, 8, 12, 13, 14


def params():
    return pltpu.CompilerParams(vmem_limit_bytes=VMEM_LIMIT)


def absorb(state, q, k, v, mask=None):
    s = lax.dot_general(q, k, NT, preferred_element_type=F32)
    if mask is not None:
        s = jnp.where(mask, s, HIDE)
    m = jnp.max(s, axis=1, keepdims=True)
    if state is not None:
        m = jnp.maximum(m, state[0])
    p = jnp.exp2((s - m) * SCALE).astype(BF16)
    acc = jnp.dot(p, v, preferred_element_type=F32)
    if state is not None:
        acc = acc + state[1] * jnp.exp2((state[0] - m) * SCALE)
    return m, acc


def with_ones(v):
    return jnp.concatenate([v, jnp.ones(v.shape, BF16)], 1)


def project_kernel(x_ref, s_ref, wk_ref, wv_ref, kv_ref, skv_ref, acc, sacc):
    step = pl.program_id(0)
    w = jnp.concatenate([wk_ref[...], wv_ref[...]], 1)
    part = jnp.dot(x_ref[...], w, preferred_element_type=F32)
    spart = jnp.dot(s_ref[...], w, preferred_element_type=F32)

    @pl.when(step == 0)
    def _():
        acc[...] = part
        sacc[...] = spart

    @pl.when(step > 0)
    def _():
        acc[...] += part
        sacc[...] += spart

    @pl.when(step == pl.num_programs(0) - 1)
    def _():
        kv_ref[...] = acc[...].astype(BF16)
        skv_ref[...] = sacc[...].astype(BF16)


def project(x, steps, w_key, w_value, head):
    rows, depth = x.shape
    srows = steps.shape[0]
    kc = 1024
    return pl.pallas_call(
        project_kernel,
        grid=(depth // kc,),
        in_specs=[
            pl.BlockSpec((rows, kc), lambda i: (0, i)),
            pl.BlockSpec((srows, kc), lambda i: (0, i)),
            pl.BlockSpec((kc, HD), lambda i: (i, head)),
            pl.BlockSpec((kc, HD), lambda i: (i, head)),
        ],
        out_specs=[
            pl.BlockSpec((rows, 2 * HD), lambda i: (0, 0)),
            pl.BlockSpec((srows, 2 * HD), lambda i: (0, 0)),
        ],
        out_shape=[
            jax.ShapeDtypeStruct((rows, 2 * HD), BF16),
            jax.ShapeDtypeStruct((srows, 2 * HD), BF16),
        ],
        scratch_shapes=[pltpu.VMEM((rows, 2 * HD), F32), pltpu.VMEM((srows, 2 * HD), F32)],
        compiler_params=params(),
        cost_estimate=pl.CostEstimate(
            flops=2 * (rows + srows) * depth * 2 * HD,
            bytes_accessed=2 * depth * (rows + srows + 2 * HD),
            transcendentals=0,
        ),
        name="project",
    )(x, steps, w_key, w_value)


def stack_heads(q_ref, feat, heads):
    half = q_ref.shape[0] // 2
    parts = []
    for first in (0, half):
        for h in range(heads):
            q = q_ref[first : first + half, h * HD : (h + 1) * HD]
            parts.append(jnp.concatenate([q, feat[first : first + half, :]], 1))
    return jnp.concatenate(parts, 0)


def unstack(x, h, heads, half):
    return x[h * half : (h + 1) * half], x[(heads + h) * half : (heads + h + 1) * half]


def keys_of(kv_ref, kf):
    return jnp.concatenate([kv_ref[:, :HD], kf], 1)


def near_kernel(sc, q_ref, qf_ref, own_ref, sib_ref, kf_ref, acc_ref, ml_ref, *, heads):
    rows = q_ref.shape[0]
    half = rows // 2
    own = pl.multiple_of(sc[S_OWN] * rows, rows)
    sib = pl.multiple_of((sc[S_OWN] ^ 1) * rows, rows)

    def diagonal(q):
        k = keys_of(own_ref, kf_ref[pl.ds(own, rows), :])
        v = with_ones(own_ref[:, HD:])
        top, low = q[: heads * half], q[heads * half :]
        at_row = lax.broadcasted_iota(jnp.int32, (heads * half, half), 0) % half
        at_col = lax.broadcasted_iota(jnp.int32, (heads * half, half), 1)
        mt, at = absorb(None, top, k[:half], v[:half], at_col <= at_row)
        at_row = lax.broadcasted_iota(jnp.int32, (heads * half, rows), 0) % half + half
        at_col = lax.broadcasted_iota(jnp.int32, (heads * half, rows), 1)
        mb, ab = absorb(None, low, k, v, at_col <= at_row)
        return jnp.concatenate([mt, mb], 0), jnp.concatenate([at, ab], 0)

    def put(state):
        m, acc = state
        lane = lax.broadcasted_iota(jnp.int32, (half, HD), 1)
        top = jnp.zeros((half, HD), F32)
        low = jnp.zeros((half, HD), F32)
        for h in range(heads):
            at, ab = unstack(acc, h, heads, half)
            mt, mb = unstack(m, h, heads, half)
            acc_ref[:half, h * HD : (h + 1) * HD] = at[:, :HD]
            acc_ref[half:, h * HD : (h + 1) * HD] = ab[:, :HD]
            top = jnp.where(lane == h, mt, jnp.where(lane == heads + h, at[:, HD:], top))
            low = jnp.where(lane == h, mb, jnp.where(lane == heads + h, ab[:, HD:], low))
        ml_ref[0, :half, :] = top
        ml_ref[0, half:, :] = low

    @pl.when(sc[S_SIB] == 0)
    def _():
        put(diagonal(stack_heads(q_ref, qf_ref[...], heads)))

    @pl.when(sc[S_SIB] != 0)
    def _():
        q = stack_heads(q_ref, qf_ref[...], heads)
        state = diagonal(q)
        k = keys_of(sib_ref, kf_ref[pl.ds(sib, rows), :])
        put(absorb(state, q, k, with_ones(sib_ref[:, HD:])))


def far_kernel(sc, q_ref, qf_ref, far_ref, farsib_ref, kf_ref, acc_ref, ml_ref, o_ref, *, heads):
    rows = q_ref.shape[0]
    half = rows // 2
    far = pl.multiple_of((sc[S_OWN] ^ 2) * rows, rows)
    farsib = pl.multiple_of((sc[S_OWN] ^ 3) * rows, rows)

    def load():
        ms, accs = [], []
        for first in (0, half):
            ml = ml_ref[0, first : first + half, :]
            for h in range(heads):
                ms.append(ml[:, h : h + 1])
                a = acc_ref[first : first + half, h * HD : (h + 1) * HD]
                l = jnp.broadcast_to(ml[:, heads + h : heads + h + 1], (half, HD))
                accs.append(jnp.concatenate([a, l], 1))
        return jnp.concatenate(ms, 0), jnp.concatenate(accs, 0)

    def put(state):
        acc = state[1]
        out = (acc[:, :HD] / acc[:, HD:]).astype(BF16)
        for h in range(heads):
            t, b = unstack(out, h, heads, half)
            o_ref[:half, h * HD : (h + 1) * HD] = t
            o_ref[half:, h * HD : (h + 1) * HD] = b

    def run(with_far, with_farsib):
        state = load()
        if with_far or with_farsib:
            q = stack_heads(q_ref, qf_ref[...], heads)
        if with_far:
            k = keys_of(far_ref, kf_ref[pl.ds(far, rows), :])
            state = absorb(state, q, k, with_ones(far_ref[:, HD:]))
        if with_farsib:
            k = keys_of(farsib_ref, kf_ref[pl.ds(farsib, rows), :])
            state = absorb(state, q, k, with_ones(farsib_ref[:, HD:]))
        put(state)

    for a in (0, 1):
        for b in (0, 1):
            pl.when((sc[S_FAR] == a) & (sc[S_FARSIB] == b))(functools.partial(run, a, b))


PF_HEADS = 2


def prefill_specs(rows, head):
    groups = GQ // PF_HEADS
    wide = PF_HEADS * HD
    q_spec = pl.BlockSpec((rows, wide), lambda g, sc: (0, head * groups + g))
    whole = pl.BlockSpec((rows, 2 * HD), lambda g, sc: (0, 0))
    qf_spec = pl.BlockSpec((rows, HD), lambda g, sc: (0, 0))
    kf_spec = pl.BlockSpec((4 * rows, HD), lambda g, sc: (0, 0))
    acc_spec = pl.BlockSpec((rows, wide), lambda g, sc: (0, g))
    ml_spec = pl.BlockSpec((1, rows, HD), lambda g, sc: (g, 0, 0))
    return groups, [q_spec, qf_spec, whole, whole, kf_spec], acc_spec, ml_spec


def prefill_near(scalars, q, qf, own, sib, kf, head):
    rows = q.shape[0]
    groups, ins, acc_spec, ml_spec = prefill_specs(rows, head)
    return pl.pallas_call(
        functools.partial(near_kernel, heads=PF_HEADS),
        grid_spec=pltpu.PrefetchScalarGridSpec(
            num_scalar_prefetch=1, grid=(groups,), in_specs=ins, out_specs=[acc_spec, ml_spec]
        ),
        out_shape=[
            jax.ShapeDtypeStruct((rows, GQ * HD), F32),
            jax.ShapeDtypeStruct((groups, rows, HD), F32),
        ],
        compiler_params=params(),
        cost_estimate=pl.CostEstimate(
            flops=4 * GQ * rows * rows * 2 * 2 * HD, bytes_accessed=5 * 2**20, transcendentals=0
        ),
        name="prefill_near",
    )(scalars, q, qf, own, sib, kf)


def prefill_far(scalars, q, qf, far, farsib, kf, acc, ml, head):
    rows = q.shape[0]
    groups, ins, acc_spec, ml_spec = prefill_specs(rows, head)
    return pl.pallas_call(
        functools.partial(far_kernel, heads=PF_HEADS),
        grid_spec=pltpu.PrefetchScalarGridSpec(
            num_scalar_prefetch=1,
            grid=(groups,),
            in_specs=ins + [acc_spec, ml_spec],
            out_specs=pl.BlockSpec((rows, PF_HEADS * HD), lambda g, sc: (0, g)),
        ),
        out_shape=jax.ShapeDtypeStruct((rows, GQ * HD), BF16),
        compiler_params=params(),
        cost_estimate=pl.CostEstimate(
            flops=4 * GQ * rows * rows * 2 * 2 * HD, bytes_accessed=5 * 2**20, transcendentals=0
        ),
        name="prefill_far",
    )(scalars, q, qf, far, farsib, kf, acc, ml)


def context_kernel(sc, q_ref, ck_ref, cv_ref, s0_ref, s1_ref, acc_ref, ml_ref, *, steps):
    srows = q_ref.shape[0]
    n = ck_ref.shape[0]
    block = 1024
    live = sc[S_LEN]
    lane = lax.broadcasted_iota(jnp.int32, (srows, HD), 1)
    q_mark = jnp.where(lane == 0, 1.0, 0.0).astype(BF16)
    ml = jnp.zeros((srows, HD), F32)
    at_row = lax.broadcasted_iota(jnp.int32, (GQ * srows, srows), 0) % srows
    at_col = lax.broadcasted_iota(jnp.int32, (GQ * srows, srows), 1)
    own_mask = (at_row // steps == at_col // steps) & (at_col <= at_row)
    for kvh, s_ref in enumerate((s0_ref, s1_ref)):
        cols = slice(kvh * HD, (kvh + 1) * HD)
        q = jnp.concatenate(
            [
                jnp.concatenate([q_ref[:, (kvh * GQ + h) * HD : (kvh * GQ + h + 1) * HD], q_mark], 1)
                for h in range(GQ)
            ],
            0,
        )
        zero = jnp.zeros((srows, HD), BF16)
        state = absorb(
            None,
            q,
            jnp.concatenate([s_ref[:, :HD], zero], 1),
            with_ones(s_ref[:, HD:]),
            own_mask,
        )
        for first in range(0, n, block):
            pos = lax.broadcasted_iota(jnp.int32, (block, HD), 0) + first
            col = lax.broadcasted_iota(jnp.int32, (block, HD), 1)
            mark = jnp.where((pos >= live) & (col == 0), HIDE, 0.0).astype(BF16)
            k = jnp.concatenate([ck_ref[first : first + block, cols], mark], 1)
            state = absorb(state, q, k, with_ones(cv_ref[first : first + block, cols]))
        m, acc = state
        for h in range(GQ):
            at = kvh * GQ + h
            a = acc[h * srows : (h + 1) * srows]
            acc_ref[:, at * HD : (at + 1) * HD] = a[:, :HD]
            ml = jnp.where(lane == at, m[h * srows : (h + 1) * srows], ml)
            ml = jnp.where(lane == KVH * GQ + at, a[:, HD:], ml)
    ml_ref[...] = ml


def context_part(scalars, q, ck, cv, s0, s1, steps):
    srows, width = q.shape
    return pl.pallas_call(
        functools.partial(context_kernel, steps=steps),
        grid_spec=pltpu.PrefetchScalarGridSpec(
            num_scalar_prefetch=1,
            grid=(1,),
            in_specs=[pl.BlockSpec(a.shape, lambda i, sc: (0, 0)) for a in (q, ck, cv, s0, s1)],
            out_specs=[
                pl.BlockSpec((srows, width), lambda i, sc: (0, 0)),
                pl.BlockSpec((srows, HD), lambda i, sc: (0, 0)),
            ],
        ),
        out_shape=[
            jax.ShapeDtypeStruct((srows, width), F32),
            jax.ShapeDtypeStruct((srows, HD), F32),
        ],
        compiler_params=params(),
        cost_estimate=pl.CostEstimate(
            flops=4 * srows * width * 2048 * 2, bytes_accessed=3 * 2**20, transcendentals=0
        ),
        name="context_part",
    )(scalars, q, ck, cv, s0, s1)


def pieces(x):
    hi = x.astype(BF16)
    rest = x - hi.astype(F32)
    mid = rest.astype(BF16)
    return hi, mid, (rest - mid.astype(F32)).astype(BF16)


def turn_kernel(
    sc, p0, p1, p2, p3, own, sib, far, farsib, xp, xps, xm, xms, kfo, kfx, o0, o1, o2, o3, ks, vs, qs, os, *, head
):
    srows = p0.shape[0]
    rows = own.shape[0]
    keys = 4 * rows
    for which, refs, first, kf in ((0, (own, sib, far, farsib), S_OWN, kfo), (1, (xp, xps, xm, xms), S_XP, kfx)):
        ks[which, :, HD:] = kf[...]
        vs[which, :, HD:] = jnp.ones((keys, HD), BF16)
        for i, ref in enumerate(refs):
            at = pl.multiple_of((sc[first] ^ i) * rows, rows)
            ks[which, pl.ds(at, rows), :HD] = ref[:, :HD]
            vs[which, pl.ds(at, rows), :HD] = ref[:, HD:]
    wide = GQ * HD
    for j, p in enumerate((p0, p1, p2, p3)):
        qs[j, :, :wide] = p[:, head * wide : (head + 1) * wide]
        qs[j, :, wide:] = p[:, 2 * wide :]
    lane = lax.broadcasted_iota(jnp.int32, (srows, HD), 1)

    def one(j, carry):
        @pl.when(sc[S_REL + j] != 0)
        def _():
            which = sc[S_WHICH + j]
            feat = qs[j, :, wide:]
            half = GQ // 2
            q = [
                jnp.concatenate(
                    [
                        jnp.concatenate([qs[j, :, h * HD : (h + 1) * HD], feat], 1)
                        for h in range(g * half, (g + 1) * half)
                    ],
                    0,
                )
                for g in (0, 1)
            ]
            state = [None, None]
            block = 1024
            for first in range(0, keys, block):
                k = ks[which, first : first + block, :]
                v = vs[which, first : first + block, :]
                for g in (0, 1):
                    state[g] = absorb(state[g], q[g], k, v)
            ms = jnp.zeros((srows, HD), F32)
            ls = jnp.zeros((srows, HD), F32)
            for h in range(GQ):
                m, acc = state[h // half]
                r = slice(h % half * srows, (h % half + 1) * srows)
                os[j, :, h * HD : (h + 1) * HD] = acc[r, :HD].astype(BF16)
                for part in range(3):
                    ms = jnp.where(lane == part * GQ + h, m[r], ms)
                    ls = jnp.where(lane == (part + 3) * GQ + h, acc[r, HD:], ls)
            m3, l3 = pieces(ms), pieces(ls)
            ext = jnp.zeros((srows, HD), F32)
            for part in range(3):
                ext = jnp.where(lane // GQ == part, m3[part].astype(F32), ext)
                ext = jnp.where(lane // GQ == part + 3, l3[part].astype(F32), ext)
            os[j, :, wide:] = ext.astype(BF16)

        return carry

    lax.fori_loop(0, 4, one, 0)
    for j, o in enumerate((o0, o1, o2, o3)):
        o[...] = os[j]


def turn_part(scalars, packets, kvs, kf_own, kf_other, head):
    srows = packets[0].shape[0]
    rows = kvs[0].shape[0]
    wide = GQ * HD + HD
    args = (*packets, *kvs, kf_own, kf_other)
    return pl.pallas_call(
        functools.partial(turn_kernel, head=head),
        grid_spec=pltpu.PrefetchScalarGridSpec(
            num_scalar_prefetch=1,
            grid=(1,),
            in_specs=[pl.BlockSpec(a.shape, lambda i, sc: (0, 0)) for a in args],
            out_specs=[pl.BlockSpec((srows, wide), lambda i, sc: (0, 0))] * 4,
            scratch_shapes=[
                pltpu.VMEM((2, 4 * rows, 2 * HD), BF16),
                pltpu.VMEM((2, 4 * rows, 2 * HD), BF16),
                pltpu.VMEM((4, srows, wide), BF16),
                pltpu.VMEM((4, srows, wide), BF16),
            ],
        ),
        out_shape=[jax.ShapeDtypeStruct((srows, wide), BF16)] * 4,
        compiler_params=params(),
        cost_estimate=pl.CostEstimate(
            flops=2 * 4 * srows * GQ * 4 * rows * 2 * HD, bytes_accessed=4 * 2**20, transcendentals=0
        ),
        name="turn_part",
    )(scalars, *args)


def merge_kernel(sc, acc_ref, ml_ref, *refs):
    o_ref = refs[-1]
    sel = sc[S_SEL]
    srows = acc_ref.shape[0]
    ml = ml_ref[...]
    wide = GQ * HD
    for kvh in range(2):
        cand = refs[kvh * 4 : kvh * 4 + 4]

        def pick(cols):
            x = cand[0][:, cols]
            for j in (1, 2, 3):
                x = jnp.where(sel == j, cand[j][:, cols], x)
            return x.astype(F32)

        ext = pick(slice(wide, wide + HD))
        for h in range(GQ):
            at = kvh * GQ + h

            def column(first):
                c = [ext[:, (first + i) * GQ + h : (first + i) * GQ + h + 1] for i in range(3)]
                return c[0] + c[1] + c[2]

            m2, l2 = column(0), column(3)
            m1, l1 = ml[:, at : at + 1], ml[:, KVH * GQ + at : KVH * GQ + at + 1]
            m = jnp.maximum(m1, m2)
            w1, w2 = jnp.exp2((m1 - m) * SCALE), jnp.exp2((m2 - m) * SCALE)
            total = l1 * w1 + l2 * w2
            a1 = acc_ref[:, at * HD : (at + 1) * HD]
            a2 = pick(slice(h * HD, (h + 1) * HD))
            o_ref[:, at * HD : (at + 1) * HD] = ((a1 * w1 + a2 * w2) / total).astype(BF16)


def merge(scalars, acc, ml, back):
    args = (acc, ml, *back[0], *back[1])
    return pl.pallas_call(
        merge_kernel,
        grid_spec=pltpu.PrefetchScalarGridSpec(
            num_scalar_prefetch=1,
            grid=(1,),
            in_specs=[pl.BlockSpec(a.shape, lambda i, sc: (0, 0)) for a in args],
            out_specs=pl.BlockSpec(acc.shape, lambda i, sc: (0, 0)),
        ),
        out_shape=jax.ShapeDtypeStruct(acc.shape, BF16),
        compiler_params=params(),
        name="merge",
    )(scalars, *args)


ROW = ("xlo", "xhi")


def row_index(x):
    return x % 2 * 2 + x // 2


def from_x(a, shift):
    return lax.ppermute(a, ROW, [(row_index((x + shift) % 4), row_index(x)) for x in range(4)])


def from_y(a, shift):
    return lax.ppermute(a, "y", [((y + shift) % 4, y) for y in range(4)])


def from_core(a):
    return lax.ppermute(a, "core", [(0, 1), (1, 0)])


def body(
    turn_hidden,
    w_key,
    w_value,
    turn_queries,
    turn_speaker,
    speaker_mask,
    shard_block,
    context_keys,
    context_values,
    context_length,
    decode_home,
    step_hidden,
    step_queries,
    row_speaker,
):
    xlo, y, xhi, core = (lax.axis_index(a) for a in ("xlo", "y", "xhi", "core"))
    rows = turn_hidden.shape[0]
    rows_dg, steps = step_hidden.shape[:2]
    srows = rows_dg * steps
    dialog = xlo * 4 + y
    own_at = xhi * 2 + core
    shard = dialog * 4 + own_at

    pos = lax.dynamic_slice_in_dim(shard_block, dialog * 4, 4, 0)
    here = pos[own_at]
    shifts = jnp.arange(4, dtype=jnp.int32)
    groups = xlo * 16 + (y + shifts) % 4 * 4 + own_at
    homes = decode_home[groups]
    relevant = (homes % 4 == y).astype(jnp.int32)
    which = (homes // 4 != xlo).astype(jnp.int32)
    home = homes[0]
    sel = (y - home + 4) % 4
    xp_at = (xhi ^ xlo) * 2 + core
    scalars = jnp.concatenate(
        [
            jnp.stack([own_at] + [(pos[own_at ^ i] < here).astype(jnp.int32) for i in (1, 2, 3)]),
            relevant,
            which,
            jnp.stack([sel, context_length[home], xp_at, jnp.int32(0)]),
        ]
    ).astype(jnp.int32)

    lanes = jnp.arange(HD, dtype=jnp.int32)

    def query_marks(speakers):
        return (speakers[:, None] == lanes[None, :]).astype(BF16)

    def key_marks(d):
        table = lax.dynamic_slice(speaker_mask, (d, 0, 0), (1, SPK, SPK))[0]
        hidden = jnp.zeros((SPK, HD), F32).at[:, :SPK].set(jnp.where(table == 1, 0.0, HIDE).T)
        speakers = lax.dynamic_slice_in_dim(turn_speaker, d * 4 * rows, 4 * rows, 0)[:, None]
        marks = jnp.zeros((1, HD), F32)
        for b in range(SPK):
            marks = jnp.where(speakers == b, hidden[b][None, :], marks)
        return marks.astype(BF16)

    step_q = step_queries.reshape(srows, -1)
    packet = jnp.concatenate([step_q, query_marks(jnp.repeat(row_speaker, steps))], 1)
    packets = [packet] + [from_y(packet, j) for j in (1, 2, 3)]

    flat_steps = step_hidden.reshape(srows, -1)
    kv, step_kv = [], []
    for head in (0, 1):
        a, b = project(turn_hidden, flat_steps, w_key, w_value, head)
        kv.append(a)
        step_kv.append(b)

    qf = query_marks(lax.dynamic_slice_in_dim(turn_speaker, shard * rows, rows, 0))
    kf_own = key_marks(dialog)
    kf_other = key_marks((1 - xlo) * 4 + y)

    ctx_acc, ctx_ml = context_part(
        scalars, step_q, context_keys, context_values, step_kv[0], step_kv[1], steps
    )

    moved = []
    for head in (0, 1):
        sib = from_core(kv[head])
        far = from_x(kv[head], 2)
        xp = from_x(kv[head], 1)
        xm = from_x(kv[head], 3)
        moved.append((kv[head], sib, far, from_core(far), xp, from_core(xp), xm, from_core(xm)))

    near = [
        prefill_near(scalars, turn_queries, qf, moved[h][0], moved[h][1], kf_own, h) for h in (0, 1)
    ]
    outs, back = [], []
    for h in (0, 1):
        parts = turn_part(scalars, packets, moved[h], kf_own, kf_other, h)
        back.append([parts[0]] + [from_y(parts[j], -j) for j in (1, 2, 3)])
        outs.append(
            prefill_far(scalars, turn_queries, qf, moved[h][2], moved[h][3], kf_own, *near[h], h)
        )
    turn_attention = jnp.concatenate(outs, 1)
    step_attention = merge(scalars, ctx_acc, ctx_ml, back).reshape(rows_dg, steps, -1)
    return turn_attention, step_attention


def solution(mesh):
    heads = mesh.shape["head"]
    fine = Mesh(mesh.devices.reshape(2, 4, 2, 2, heads), ("xlo", "y", "xhi", "core", "head"))
    split = ("xlo", "y", "xhi", "core")
    return jax.shard_map(
        body,
        mesh=fine,
        in_specs=(
            P(split, None),
            P(None, "head"),
            P(None, "head"),
            P(split, "head"),
            P(),
            P(),
            P(),
            P(split, "head"),
            P(split, "head"),
            P(),
            P(),
            P(split, None, None),
            P(split, None, "head"),
            P(split),
        ),
        out_specs=(P(split, "head"), P(split, None, "head")),
        check_vma=False,
    )
```

```python
import functools
import math

import jax
import jax.numpy as jnp
from jax import lax
from jax.experimental import pallas as pl
from jax.experimental.pallas import tpu as pltpu
from jax.sharding import Mesh
from jax.sharding import PartitionSpec as P

HQ = 64
KVH = 8
HD = 128
SPK = 4
GQ = HQ // KVH

HIDE = -1e30
SCALE = math.log2(math.e) / math.sqrt(HD)
NT = (((1,), (1,)), ((), ()))
F32 = jnp.float32
BF16 = jnp.bfloat16

S_OWN, S_SIB, S_FAR, S_FARSIB, S_REL, S_WHICH, S_SEL, S_LEN, S_XP = 0, 1, 2, 3, 4, 8, 12, 13, 14


def params(mib):
    return pltpu.CompilerParams(vmem_limit_bytes=mib * 2**20)


def in_vmem(x):
    return pltpu.with_memory_space_constraint(x, pltpu.VMEM)


def in_hbm(x):
    return pltpu.with_memory_space_constraint(x, pltpu.HBM)


def with_ones(v):
    return jnp.concatenate([v, jnp.ones(v.shape, BF16)], 1)


def marks(table, speakers):
    row = lax.broadcasted_iota(jnp.int32, (8, HD), 0)
    hot = jnp.where(speakers == row, 1.0, 0.0).astype(BF16)
    out = lax.dot_general(hot, table, (((0,), (0,)), ((), ())), preferred_element_type=F32)
    return out.astype(BF16)


def prep_kernel(blocks, homes, lengths, mask, spk_ref, sc, qf_ref, kfo_ref, kfx_ref):
    xlo, y, xhi, core = (lax.axis_index(a) for a in ("xlo", "y", "xhi", "core"))
    own_at = xhi * 2 + core
    dialog = xlo * 4 + y
    here = blocks[dialog * 4 + own_at]
    sc[S_OWN] = own_at
    for i, at in ((1, S_SIB), (2, S_FAR), (3, S_FARSIB)):
        sc[at] = jnp.where(blocks[dialog * 4 + (own_at ^ i)] < here, 1, 0)
    for j in range(4):
        home = homes[xlo * 16 + (y + j) % 4 * 4 + own_at]
        sc[S_REL + j] = jnp.where(home % 4 == y, 1, 0)
        sc[S_WHICH + j] = jnp.where(home // 4 != xlo, 1, 0)
    home = homes[xlo * 16 + y * 4 + own_at]
    sc[S_SEL] = (y - home % 4 + 4) % 4
    sc[S_LEN] = lengths[home]
    sc[S_XP] = (xhi ^ xlo) * 2 + core
    sc[15] = 0

    row = lax.broadcasted_iota(jnp.int32, (8, HD), 0)
    lane = lax.broadcasted_iota(jnp.int32, (8, HD), 1)
    for d, out in ((dialog, kfo_ref), ((1 - xlo) * 4 + y, kfx_ref)):
        table = jnp.zeros((8, HD), F32)
        for a in range(SPK):
            for b in range(SPK):
                add = jnp.where(mask[a, b, d] == 1, 0.0, HIDE)
                table = jnp.where((row == b) & (lane == a), add, table)
        table = table.astype(BF16)
        for i in range(16):
            out[i * HD : (i + 1) * HD, :] = marks(table, spk_ref[d * 2 + i // 8, i % 8 : i % 8 + 1, :])
    eye = jnp.where((row == lane) & (row < SPK), 1.0, 0.0).astype(BF16)
    for i in range(4):
        at = (dialog * 4 + own_at) * 4 + i
        qf_ref[i * HD : (i + 1) * HD, :] = marks(eye, spk_ref[at // 8, pl.ds(at % 8, 1), :])


def prepare(blocks, homes, lengths, mask, spk):
    rows = spk.size // 32
    smem = pl.BlockSpec(memory_space=pltpu.SMEM)
    vmem = pl.BlockSpec(memory_space=pltpu.VMEM)
    return pl.pallas_call(
        prep_kernel,
        in_specs=[smem] * 4 + [vmem],
        out_specs=[smem] + [vmem] * 3,
        out_shape=[
            jax.ShapeDtypeStruct((16,), jnp.int32),
            pltpu.VMEM((rows, HD), BF16),
            pltpu.VMEM((4 * rows, HD), BF16),
            pltpu.VMEM((4 * rows, HD), BF16),
        ],
        compiler_params=params(6),
        name="prepare",
    )(blocks, homes, lengths, mask.transpose(1, 2, 0), spk.reshape(-1, 8, HD))


def packet_kernel(row_spk, q_ref, pk_ref, wide):
    groups, steps, width = q_ref.shape
    srows = groups * steps
    for r in range(groups):
        wide[r * steps : (r + 1) * steps, :] = q_ref[r].astype(F32)
    pk_ref[:, :width] = wide[...].astype(BF16)
    row = lax.broadcasted_iota(jnp.int32, (srows, HD), 0)
    lane = lax.broadcasted_iota(jnp.int32, (srows, HD), 1)
    speaker = jnp.zeros((srows, HD), jnp.int32)
    for r in range(groups):
        speaker = jnp.where(row // steps == r, row_spk[r], speaker)
    pk_ref[:, width:] = jnp.where(lane == speaker, 1.0, 0.0).astype(BF16)


def make_packet(row_spk, queries):
    groups, steps, width = queries.shape
    return pl.pallas_call(
        packet_kernel,
        in_specs=[pl.BlockSpec(memory_space=pltpu.SMEM), pl.BlockSpec(memory_space=pltpu.VMEM)],
        out_specs=pl.BlockSpec(memory_space=pltpu.VMEM),
        out_shape=jax.ShapeDtypeStruct((groups * steps, width + HD), BF16),
        scratch_shapes=[pltpu.VMEM((groups * steps, width), F32)],
        compiler_params=params(4),
        name="packet",
    )(row_spk, queries)


def project_kernel(x_hbm, s_hbm, wk_hbm, wv_hbm, after, kv_ref, skv_ref, xb, sb, wkb, wvb, wide, sem, *, chunk):
    groups, steps, depth = s_hbm.shape
    copies = []
    for i in range(depth // chunk):
        c = pl.ds(i * chunk, chunk)
        pairs = [
            (x_hbm.at[:, c], xb.at[:, c]),
            (wk_hbm.at[c, :], wkb.at[c, :]),
            (wv_hbm.at[c, :], wvb.at[c, :]),
        ]
        copies.append([pltpu.make_async_copy(a, b, sem.at[i, n]) for n, (a, b) in enumerate(pairs)])
        for copy in copies[-1]:
            copy.start()
        if i == 0:
            step_copy = pltpu.make_async_copy(s_hbm, sb, sem.at[0, 3])
            step_copy.start()
    acc = sacc = None
    for i, these in enumerate(copies):
        for copy in these:
            copy.wait()
        c = slice(i * chunk, (i + 1) * chunk)
        w = jnp.concatenate([wkb[c, :], wvb[c, :]], 1)
        if i == 0:
            step_copy.wait()
        for r in range(groups):
            wide[r * steps : (r + 1) * steps, c] = sb[r, :, c].astype(F32)
        part = jnp.dot(xb[:, c], w, preferred_element_type=F32)
        spart = jnp.dot(wide[:, c].astype(BF16), w, preferred_element_type=F32)
        acc = part if acc is None else acc + part
        sacc = spart if sacc is None else sacc + spart
    for at, first in enumerate((0, 2 * HD, HD, 3 * HD)):
        kv_ref[at] = acc[:, first : first + HD].astype(BF16)
        skv_ref[at] = sacc[:, first : first + HD].astype(BF16)


def project(x, steps, w_key, w_value, after):
    rows, depth = x.shape
    srows = steps.shape[0] * steps.shape[1]
    chunk = 1024
    hbm = pl.BlockSpec(memory_space=pl.ANY)
    vmem = pl.BlockSpec(memory_space=pltpu.VMEM)
    return pl.pallas_call(
        functools.partial(project_kernel, chunk=chunk),
        in_specs=[hbm] * 5,
        out_specs=[vmem] * 2,
        out_shape=[
            jax.ShapeDtypeStruct((4, rows, HD), BF16),
            jax.ShapeDtypeStruct((4, srows, HD), BF16),
        ],
        scratch_shapes=[
            pltpu.VMEM(x.shape, BF16),
            pltpu.VMEM(steps.shape, BF16),
            pltpu.VMEM(w_key.shape, BF16),
            pltpu.VMEM(w_value.shape, BF16),
            pltpu.VMEM((srows, depth), F32),
            pltpu.SemaphoreType.DMA((depth // chunk, 4)),
        ],
        compiler_params=params(28),
        cost_estimate=pl.CostEstimate(
            flops=2 * (rows + srows) * depth * 4 * HD,
            bytes_accessed=2 * depth * (rows + srows + 4 * HD),
            transcendentals=0,
        ),
        name="project",
    )(*map(in_hbm, (x, steps, w_key, w_value)), after)


def scores(q, k):
    return lax.dot_general(q, k, NT, preferred_element_type=F32)


def settle(s, v, state=None):
    m = jnp.max(s, axis=1, keepdims=True)
    if state is not None:
        m = jnp.maximum(m, state[0])
    p = jnp.exp2((s - m) * SCALE).astype(BF16)
    acc = jnp.dot(p, v, preferred_element_type=F32)
    if state is not None:
        acc = acc + state[1] * jnp.exp2((state[0] - m) * SCALE)
    return m, acc


def in_turn(items, score, finish):
    ahead = score(items[0])
    for i, item in enumerate(items):
        now = ahead
        if i + 1 < len(items):
            ahead = score(items[i + 1])
        finish(item, now)


def keys_of(k, kf):
    return jnp.concatenate([k, kf], 1)


def query_of(q_ref, qf_ref, h, first, count):
    q = q_ref[first : first + count, h * HD : (h + 1) * HD]
    return jnp.concatenate([q, qf_ref[first : first + count, :]], 1)


def near_kernel(sc, q_ref, qf_ref, own_ref, sib_ref, kf_ref, acc_ref, ml_ref):
    group = pl.program_id(0)
    kvh = group * STATE // GQ
    rows = q_ref.shape[0]
    half = rows // 2
    own = pl.multiple_of(sc[S_OWN] * rows, rows)
    sib = pl.multiple_of((sc[S_OWN] ^ 1) * rows, rows)
    lane = lax.broadcasted_iota(jnp.int32, (half, HD), 1)

    def run(with_sib):
        k = keys_of(own_ref[2 * kvh], kf_ref[pl.ds(own, rows), :])
        v = with_ones(own_ref[2 * kvh + 1])
        ks = [k[:half], k]
        vs = [v[:half], v]
        if with_sib:
            k = keys_of(sib_ref[2 * kvh], kf_ref[pl.ds(sib, rows), :])
            v = with_ones(sib_ref[2 * kvh + 1])
            ks = [jnp.concatenate([a, k], 0) for a in ks]
            vs = [jnp.concatenate([a, v], 0) for a in vs]
        ml = [jnp.zeros((half, HD), F32)] * 2

        def score(item):
            h, part = item
            q = [query_of(q_ref, qf_ref, h + i, part * half, half) for i in range(HN)]
            s = scores(jnp.concatenate(q, 0), ks[part])
            own_cols = (part + 1) * half
            at_row = lax.broadcasted_iota(jnp.int32, (HN * half, half), 0) % half
            at_col = lax.broadcasted_iota(jnp.int32, (HN * half, half), 1)
            corner = jnp.where(at_col <= at_row, s[:, own_cols - half : own_cols], HIDE)
            cut = [s[:, : own_cols - half]] * (part > 0) + [corner] + [s[:, own_cols:]] * with_sib
            return jnp.concatenate(cut, 1)

        def finish(item, s):
            h0, part = item
            ms, accs = settle(s, vs[part])
            for i in range(HN):
                h = h0 + i
                m, acc = ms[i * half : (i + 1) * half], accs[i * half : (i + 1) * half]
                acc_ref[group, part * half : (part + 1) * half, h * HD : (h + 1) * HD] = acc[:, :HD]
                ml[part] = jnp.where(lane == h, m, jnp.where(lane == STATE + h, acc[:, HD:], ml[part]))

        in_turn([(h, part) for h in range(0, STATE, HN) for part in (0, 1)], score, finish)
        for part in (0, 1):
            ml_ref[group, part * half : (part + 1) * half, :] = ml[part]

    @pl.when(sc[S_SIB] == 0)
    def _():
        run(0)

    @pl.when(sc[S_SIB] != 0)
    def _():
        run(1)


def far_kernel(sc, q_ref, qf_ref, far_ref, fs_ref, kf_ref, acc_ref, ml_ref, *rest):
    group = pl.program_id(0)
    kvh = group * STATE // GQ
    o_ref = rest[-1]
    rows = q_ref.shape[0]
    half = rows // 2
    far = pl.multiple_of((sc[S_OWN] ^ 2) * rows, rows)
    farsib = pl.multiple_of((sc[S_OWN] ^ 3) * rows, rows)

    def run(with_far, with_farsib):
        ks, vs = [], []
        if with_far:
            ks.append(keys_of(far_ref[2 * kvh], kf_ref[pl.ds(far, rows), :]))
            vs.append(with_ones(far_ref[2 * kvh + 1]))
        if with_farsib:
            ks.append(keys_of(fs_ref[2 * kvh], kf_ref[pl.ds(farsib, rows), :]))
            vs.append(with_ones(fs_ref[2 * kvh + 1]))
        if ks:
            k, v = jnp.concatenate(ks, 0), jnp.concatenate(vs, 0)

        def score(item):
            q = [query_of(q_ref, qf_ref, item + i, 0, rows) for i in range(HF)]
            return scores(jnp.concatenate(q, 0), k) if ks else None

        def finish(item, s):
            state = []
            for h in range(item, item + HF):
                ml = ml_ref[group]
                l = jnp.broadcast_to(ml[:, STATE + h : STATE + h + 1], (rows, HD))
                acc = jnp.concatenate([acc_ref[group, :, h * HD : (h + 1) * HD], l], 1)
                state.append((ml[:, h : h + 1], acc))
            m = jnp.concatenate([x[0] for x in state], 0)
            acc = jnp.concatenate([x[1] for x in state], 0)
            if ks:
                acc = settle(s, v, (m, acc))[1]
            out = (acc[:, :HD] / acc[:, HD:]).astype(BF16)
            for i in range(HF):
                o_ref[:, (item + i) * HD : (item + i + 1) * HD] = out[i * rows : (i + 1) * rows]

        in_turn(list(range(0, STATE, HF)), score, finish)

    for a in (0, 1):
        for b in (0, 1):
            pl.when((sc[S_FAR] == a) & (sc[S_FARSIB] == b))(functools.partial(run, a, b))


STATE = 4
HN = 2
HF = 1


def prefill(kernel, name, scalars, q, qf, one, two, kf, state=(), after=()):
    rows, width = q.shape
    wide = STATE * HD
    groups = width // wide
    columns = pl.BlockSpec((rows, wide), lambda g, sc: (0, g))
    vmem = pl.BlockSpec(memory_space=pltpu.VMEM)
    hbm = pl.BlockSpec(memory_space=pl.ANY)
    first = not state
    return pl.pallas_call(
        kernel,
        grid_spec=pltpu.PrefetchScalarGridSpec(
            num_scalar_prefetch=1,
            grid=(groups,),
            in_specs=[columns] + [vmem] * (4 + len(state))
            + [hbm] * len(after),
            out_specs=[vmem, vmem] if first else columns,
        ),
        out_shape=[
            pltpu.VMEM((groups, rows, wide), F32),
            pltpu.VMEM((groups, rows, HD), F32),
        ]
        if first
        else jax.ShapeDtypeStruct(q.shape, BF16),
        compiler_params=params(20),
        cost_estimate=pl.CostEstimate(
            flops=8 * GQ * rows * rows * 2 * 2 * HD, bytes_accessed=4 * 2**20, transcendentals=0
        ),
        name=name,
    )(scalars, in_vmem(q), in_vmem(qf), in_vmem(one), in_vmem(two), in_vmem(kf), *map(in_vmem, state), *after)


def context_kernel(sc, q_ref, ck_ref, cv_ref, own_ref, acc_ref, ml_ref, *, steps):
    srows = q_ref.shape[0]
    n = ck_ref.shape[0]
    block = 1024
    live = sc[S_LEN]
    lane = lax.broadcasted_iota(jnp.int32, (srows, HD), 1)
    q_mark = jnp.where(lane == 0, 1.0, 0.0).astype(BF16)
    zero = jnp.zeros((srows, HD), BF16)
    at_row = lax.broadcasted_iota(jnp.int32, (DEC * srows, srows), 0) % srows
    at_col = lax.broadcasted_iota(jnp.int32, (DEC * srows, srows), 1)
    own_mask = (at_row // steps == at_col // steps) & (at_col <= at_row)
    keys = {}
    for first in range(0, n, block):
        pos = lax.broadcasted_iota(jnp.int32, (block, HD), 0) + first
        col = lax.broadcasted_iota(jnp.int32, (block, HD), 1)
        mark = jnp.where((pos >= live) & (col == 0), HIDE, 0.0).astype(BF16)
        for kvh in (0, 1):
            r, c = slice(first, first + block), slice(kvh * HD, (kvh + 1) * HD)
            keys[kvh, first] = jnp.concatenate([ck_ref[r, c], mark], 1), with_ones(cv_ref[r, c])
    state = {}
    ml = [jnp.zeros((srows, HD), F32)]

    def query(g):
        cut = [q_ref[:, h * HD : (h + 1) * HD] for h in range(g * DEC, (g + 1) * DEC)]
        return jnp.concatenate([jnp.concatenate([q, q_mark], 1) for q in cut], 0)

    def score(item):
        g, first = item
        kvh = g * DEC // GQ
        if first < 0:
            s = scores(query(g), jnp.concatenate([own_ref[2 * kvh], zero], 1))
            return jnp.where(own_mask, s, HIDE)
        return scores(query(g), keys[kvh, first][0])

    def finish(item, s):
        g, first = item
        kvh = g * DEC // GQ
        v = with_ones(own_ref[2 * kvh + 1]) if first < 0 else keys[kvh, first][1]
        state[g] = settle(s, v, state.get(g))
        if first == n - block:
            m, acc = state[g]
            for i in range(DEC):
                at = g * DEC + i
                a = acc[i * srows : (i + 1) * srows]
                acc_ref[:, at * HD : (at + 1) * HD] = a[:, :HD]
                ml[0] = jnp.where(lane == at, m[i * srows : (i + 1) * srows], ml[0])
                ml[0] = jnp.where(lane == 2 * GQ + at, a[:, HD:], ml[0])

    groups = 2 * GQ // DEC
    in_turn([(g, first) for g in range(groups) for first in [-1, *range(0, n, block)]], score, finish)
    ml_ref[...] = ml[0]


def context_part(scalars, q, ck, cv, own, steps):
    srows, width = q.shape[0], q.shape[1] - HD
    return pl.pallas_call(
        functools.partial(context_kernel, steps=steps),
        grid_spec=pltpu.PrefetchScalarGridSpec(
            num_scalar_prefetch=1,
            grid=(1,),
            in_specs=[pl.BlockSpec(memory_space=pltpu.VMEM)] * 4,
            out_specs=[
                pl.BlockSpec((srows, width), lambda i, sc: (0, 0)),
                pl.BlockSpec((srows, HD), lambda i, sc: (0, 0)),
            ],
        ),
        out_shape=[
            jax.ShapeDtypeStruct((srows, width), F32),
            jax.ShapeDtypeStruct((srows, HD), F32),
        ],
        compiler_params=params(12),
        name="context_part",
    )(scalars, q, in_vmem(ck), in_vmem(cv), own)


DEC = 8


def pieces(x):
    hi = x.astype(BF16)
    rest = x - hi.astype(F32)
    mid = rest.astype(BF16)
    return hi, mid, (rest - mid.astype(F32)).astype(BF16)


def turn_kernel(sc, p0, p1, p2, p3, own, sib, far, fs, xp, xps, xm, xms, kfo, kfx, o0, o1, o2, o3, ks, vs, qs, os):
    head = pl.program_id(0)
    srows = p0.shape[0]
    rows = own.shape[1]
    keys = 4 * rows
    wide = GQ * HD
    for which, refs, first, kf in ((0, (own, sib, far, fs), S_OWN, kfo), (1, (xp, xps, xm, xms), S_XP, kfx)):
        wanted = [(sc[S_REL + j] != 0) & (sc[S_WHICH + j] == which) for j in range(4)]

        @pl.when(wanted[0] | wanted[1] | wanted[2] | wanted[3])
        def _():
            ks[which, :, HD:] = kf[...]
            vs[which, :, HD:] = jnp.ones((keys, HD), BF16)
            for i, ref in enumerate(refs):
                at = pl.multiple_of((sc[first] ^ i) * rows, rows)
                ks[which, pl.ds(at, rows), :HD] = ref[2 * head]
                vs[which, pl.ds(at, rows), :HD] = ref[2 * head + 1]

    for j, p in enumerate((p0, p1, p2, p3)):

        @pl.when(sc[S_REL + j] != 0)
        def _():
            qs[j, :, :wide] = p[:, pl.ds(pl.multiple_of(head * wide, wide), wide)]
            qs[j, :, wide:] = p[:, 2 * wide :]

    lane = lax.broadcasted_iota(jnp.int32, (srows, HD), 1)
    block = 1024

    def one(j, carry):
        @pl.when(sc[S_REL + j] != 0)
        def _():
            which = sc[S_WHICH + j]
            feat = qs[j, :, wide:]
            state = {}
            ml = [jnp.zeros((srows, HD), F32)] * 2

            def score(item):
                g, first = item
                cut = [qs[j, :, h * HD : (h + 1) * HD] for h in range(g * DEC, (g + 1) * DEC)]
                q = jnp.concatenate([jnp.concatenate([q, feat], 1) for q in cut], 0)
                return scores(q, ks[which, first : first + block, :])

            def finish(item, s):
                g, first = item
                state[g] = settle(s, vs[which, first : first + block, :], state.get(g))
                if first == keys - block:
                    m, acc = state[g]
                    for i in range(DEC):
                        h = g * DEC + i
                        r = slice(i * srows, (i + 1) * srows)
                        os[j, :, h * HD : (h + 1) * HD] = acc[r, :HD].astype(BF16)
                        for part in range(3):
                            ml[0] = jnp.where(lane == part * GQ + h, m[r], ml[0])
                            ml[1] = jnp.where(lane == (part + 3) * GQ + h, acc[r, HD:], ml[1])

            in_turn([(g, first) for first in range(0, keys, block) for g in range(GQ // DEC)], score, finish)
            m3, l3 = pieces(ml[0]), pieces(ml[1])
            ext = jnp.zeros((srows, HD), F32)
            for part in range(3):
                ext = jnp.where(lane // GQ == part, m3[part].astype(F32), ext)
                ext = jnp.where(lane // GQ == part + 3, l3[part].astype(F32), ext)
            os[j, :, wide:] = ext.astype(BF16)

        return carry

    lax.fori_loop(0, 4, one, 0)
    for j, o in enumerate((o0, o1, o2, o3)):
        o[...] = os[j]


def turn_part(scalars, packets, kvs, kf_own, kf_other, after):
    srows = packets[0].shape[0]
    rows = kvs[0].shape[1]
    wide = GQ * HD + HD

    def kernel(*refs):
        turn_kernel(*refs[:15], *refs[15 + len(after) :])

    return pl.pallas_call(
        kernel,
        grid_spec=pltpu.PrefetchScalarGridSpec(
            num_scalar_prefetch=1,
            grid=(2,),
            in_specs=[pl.BlockSpec(memory_space=pltpu.VMEM)] * 14
            + [pl.BlockSpec(memory_space=pl.ANY)] * len(after),
            out_specs=[pl.BlockSpec((srows, wide), lambda g, sc: (0, g))] * 4,
            scratch_shapes=[
                pltpu.VMEM((2, 4 * rows, 2 * HD), BF16),
                pltpu.VMEM((2, 4 * rows, 2 * HD), BF16),
                pltpu.VMEM((4, srows, wide), BF16),
                pltpu.VMEM((4, srows, wide), BF16),
            ],
        ),
        out_shape=[jax.ShapeDtypeStruct((srows, 2 * wide), BF16)] * 4,
        compiler_params=params(20),
        cost_estimate=pl.CostEstimate(
            flops=4 * 4 * srows * GQ * 4 * rows * 2 * HD, bytes_accessed=4 * 2**20, transcendentals=0
        ),
        name="turn_part",
    )(scalars, *map(in_vmem, packets), *map(in_vmem, kvs), in_vmem(kf_own), in_vmem(kf_other), *after)


def merge_kernel(sc, acc_ref, ml_ref, *refs):
    o_ref, wide = refs[-2:]
    sel = sc[S_SEL]
    groups, steps, _ = o_ref.shape
    ml = ml_ref[...]
    width = GQ * HD
    for kvh in range(2):
        first = kvh * (width + HD)

        def pick(cols):
            cols = slice(first + cols.start, first + cols.stop)
            x = refs[0][:, cols]
            for j in (1, 2, 3):
                x = jnp.where(sel == j, refs[j][:, cols], x)
            return x.astype(F32)

        ext = pick(slice(width, width + HD))
        whole = [
            ext[:, i * GQ : (i + 1) * GQ]
            + ext[:, (i + 1) * GQ : (i + 2) * GQ]
            + ext[:, (i + 2) * GQ : (i + 3) * GQ]
            for i in (0, 3)
        ]
        m2, l2 = whole
        m1 = ml[:, kvh * GQ : (kvh + 1) * GQ]
        l1 = ml[:, (2 + kvh) * GQ : (3 + kvh) * GQ]
        m = jnp.maximum(m1, m2)
        w1, w2 = jnp.exp2((m1 - m) * SCALE), jnp.exp2((m2 - m) * SCALE)
        total = l1 * w1 + l2 * w2
        w1, w2 = w1 / total, w2 / total
        for h in range(GQ):
            at = kvh * GQ + h
            a1 = acc_ref[:, at * HD : (at + 1) * HD]
            a2 = pick(slice(h * HD, (h + 1) * HD))
            wide[:, at * HD : (at + 1) * HD] = a1 * w1[:, h : h + 1] + a2 * w2[:, h : h + 1]
    for r in range(groups):
        o_ref[r] = wide[r * steps : (r + 1) * steps, :].astype(BF16)


def merge(scalars, acc, ml, back, steps):
    args = (acc, ml, *back)
    shape = (acc.shape[0] // steps, steps, acc.shape[1])
    return pl.pallas_call(
        merge_kernel,
        grid_spec=pltpu.PrefetchScalarGridSpec(
            num_scalar_prefetch=1,
            grid=(1,),
            in_specs=[pl.BlockSpec(a.shape, lambda i, sc: (0, 0)) for a in args],
            out_specs=pl.BlockSpec(shape, lambda i, sc: (0, 0, 0)),
            scratch_shapes=[pltpu.VMEM(acc.shape, F32)],
        ),
        out_shape=jax.ShapeDtypeStruct(shape, BF16),
        compiler_params=params(8),
        name="merge",
    )(scalars, *args)


ROW = ("xlo", "xhi")


def row_index(x):
    return x % 2 * 2 + x // 2


def from_x(a, shift):
    return lax.ppermute(a, ROW, [(row_index((x + shift) % 4), row_index(x)) for x in range(4)])


def from_y(a, shift):
    return lax.ppermute(a, "y", [((y + shift) % 4, y) for y in range(4)])


def from_core(a):
    return lax.ppermute(a, "core", [(0, 1), (1, 0)])


def body(
    turn_hidden,
    w_key,
    w_value,
    turn_queries,
    turn_speaker,
    speaker_mask,
    shard_block,
    context_keys,
    context_values,
    context_length,
    decode_home,
    step_hidden,
    step_queries,
    row_speaker,
):
    steps = step_hidden.shape[1]
    packet = make_packet(row_speaker, step_queries)
    packets = [packet, from_y(packet, 1), None, from_y(packet, 3)]
    own, step_kv = project(turn_hidden, step_hidden, w_key, w_value, packet)
    own, packet, packets[1], packets[3] = lax.optimization_barrier((own, packet, packets[1], packets[3]))
    sib, far, xp, xm = from_core(own), from_x(own, 2), from_x(own, 1), from_x(own, 3)
    packets[2] = from_y(packet, 2)
    shard_block, sib = lax.optimization_barrier((shard_block, sib))
    scalars, qf, kf_own, kf_other = prepare(
        shard_block, decode_home, context_length, speaker_mask, turn_speaker
    )
    near = prefill(near_kernel, "prefill_near", scalars, turn_queries, qf, own, sib, kf_own)
    far, xp, xm, packet = lax.optimization_barrier((far, xp, xm, packet, near[1]))[:4]
    farsib, xps, xms = from_core(far), from_core(xp), from_core(xm)
    ctx = context_part(scalars, packet, context_keys, context_values, step_kv, steps)
    moved = (own, sib, far, farsib, xp, xps, xm, xms)
    parts = turn_part(scalars, packets, moved, kf_own, kf_other, (ctx[1],))
    back = [parts[0]] + [from_y(parts[j], -j) for j in (1, 2, 3)]
    turn_attention = prefill(
        far_kernel, "prefill_far", scalars, turn_queries, qf, far, farsib, kf_own, near, (parts[0],)
    )
    step_attention = merge(scalars, *ctx, back, steps)
    return turn_attention, step_attention


def solution(mesh):
    heads = mesh.shape["head"]
    fine = Mesh(mesh.devices.reshape(2, 4, 2, 2, heads), ("xlo", "y", "xhi", "core", "head"))
    split = ("xlo", "y", "xhi", "core")
    return jax.shard_map(
        body,
        mesh=fine,
        in_specs=(
            P(split, None),
            P(None, "head"),
            P(None, "head"),
            P(split, "head"),
            P(),
            P(),
            P(),
            P(split, "head"),
            P(split, "head"),
            P(),
            P(),
            P(split, None, None),
            P(split, None, "head"),
            P(split),
        ),
        out_specs=(P(split, "head"), P(split, None, "head")),
        check_vma=False,
    )
```

```python
import functools
import math

import jax
import jax.numpy as jnp
from jax import lax
from jax.experimental import pallas as pl
from jax.experimental.pallas import tpu as pltpu
from jax.sharding import Mesh
from jax.sharding import PartitionSpec as P

HQ = 64
KVH = 8
HD = 128
SPK = 4
GQ = HQ // KVH

HIDE = -1e30
SCALE = math.log2(math.e) / math.sqrt(HD)
NT = (((1,), (1,)), ((), ()))
F32 = jnp.float32
BF16 = jnp.bfloat16

S_OWN, S_SIB, S_FAR, S_FARSIB, S_REL, S_WHICH, S_SEL, S_LEN, S_XP = 0, 1, 2, 3, 4, 8, 12, 13, 14


def params(mib):
    return pltpu.CompilerParams(vmem_limit_bytes=mib * 2**20)


def in_vmem(x):
    return pltpu.with_memory_space_constraint(x, pltpu.VMEM)


def in_hbm(x):
    return pltpu.with_memory_space_constraint(x, pltpu.HBM)


def with_ones(v):
    return jnp.concatenate([v, jnp.ones(v.shape, BF16)], 1)


def marks(table, speakers):
    row = lax.broadcasted_iota(jnp.int32, (8, HD), 0)
    hot = jnp.where(speakers == row, 1.0, 0.0).astype(BF16)
    out = lax.dot_general(hot, table, (((0,), (0,)), ((), ())), preferred_element_type=F32)
    return out.astype(BF16)


def prep_kernel(blocks, homes, lengths, mask, spk_ref, sc, qf_ref, kfo_ref, kfx_ref):
    xlo, y, xhi, core = (lax.axis_index(a) for a in ("xlo", "y", "xhi", "core"))
    own_at = xhi * 2 + core
    dialog = xlo * 4 + y
    here = blocks[dialog * 4 + own_at]
    sc[S_OWN] = own_at
    for i, at in ((1, S_SIB), (2, S_FAR), (3, S_FARSIB)):
        sc[at] = jnp.where(blocks[dialog * 4 + (own_at ^ i)] < here, 1, 0)
    for j in range(4):
        home = homes[xlo * 16 + (y + j) % 4 * 4 + own_at]
        sc[S_REL + j] = jnp.where(home % 4 == y, 1, 0)
        sc[S_WHICH + j] = jnp.where(home // 4 != xlo, 1, 0)
    home = homes[xlo * 16 + y * 4 + own_at]
    sc[S_SEL] = (y - home % 4 + 4) % 4
    sc[S_LEN] = lengths[home]
    sc[S_XP] = (xhi ^ xlo) * 2 + core
    sc[15] = 0

    row = lax.broadcasted_iota(jnp.int32, (8, HD), 0)
    lane = lax.broadcasted_iota(jnp.int32, (8, HD), 1)
    for d, out in ((dialog, kfo_ref), ((1 - xlo) * 4 + y, kfx_ref)):
        table = jnp.zeros((8, HD), F32)
        for a in range(SPK):
            for b in range(SPK):
                add = jnp.where(mask[a, b, d] == 1, 0.0, HIDE)
                table = jnp.where((row == b) & (lane == a), add, table)
        table = table.astype(BF16)
        for i in range(16):
            out[i * HD : (i + 1) * HD, :] = marks(table, spk_ref[d * 2 + i // 8, i % 8 : i % 8 + 1, :])
    eye = jnp.where((row == lane) & (row < SPK), 1.0, 0.0).astype(BF16)
    for i in range(4):
        at = (dialog * 4 + own_at) * 4 + i
        qf_ref[i * HD : (i + 1) * HD, :] = marks(eye, spk_ref[at // 8, pl.ds(at % 8, 1), :])


def prepare(blocks, homes, lengths, mask, spk):
    rows = spk.size // 32
    smem = pl.BlockSpec(memory_space=pltpu.SMEM)
    vmem = pl.BlockSpec(memory_space=pltpu.VMEM)
    return pl.pallas_call(
        prep_kernel,
        in_specs=[smem] * 4 + [vmem],
        out_specs=[smem] + [vmem] * 3,
        out_shape=[
            jax.ShapeDtypeStruct((16,), jnp.int32),
            pltpu.VMEM((rows, HD), BF16),
            pltpu.VMEM((4 * rows, HD), BF16),
            pltpu.VMEM((4 * rows, HD), BF16),
        ],
        compiler_params=params(6),
        name="prepare",
    )(blocks, homes, lengths, mask.transpose(1, 2, 0), spk.reshape(-1, 8, HD))


def packet_kernel(row_spk, q_ref, pk_ref, wide):
    groups, steps, width = q_ref.shape
    srows = groups * steps
    for r in range(groups):
        wide[r * steps : (r + 1) * steps, :] = q_ref[r].astype(F32)
    pk_ref[:, :width] = wide[...].astype(BF16)
    row = lax.broadcasted_iota(jnp.int32, (srows, HD), 0)
    lane = lax.broadcasted_iota(jnp.int32, (srows, HD), 1)
    speaker = jnp.zeros((srows, HD), jnp.int32)
    for r in range(groups):
        speaker = jnp.where(row // steps == r, row_spk[r], speaker)
    pk_ref[:, width:] = jnp.where(lane == speaker, 1.0, 0.0).astype(BF16)


def make_packet(row_spk, queries):
    groups, steps, width = queries.shape
    return pl.pallas_call(
        packet_kernel,
        in_specs=[pl.BlockSpec(memory_space=pltpu.SMEM), pl.BlockSpec(memory_space=pltpu.VMEM)],
        out_specs=pl.BlockSpec(memory_space=pltpu.VMEM),
        out_shape=jax.ShapeDtypeStruct((groups * steps, width + HD), BF16),
        scratch_shapes=[pltpu.VMEM((groups * steps, width), F32)],
        compiler_params=params(4),
        name="packet",
    )(row_spk, queries)


def project_kernel(x_hbm, s_hbm, wk_hbm, wv_hbm, kv_ref, skv_ref, xb, sb, wkb, wvb, wide, sem, *, chunk):
    groups, steps, depth = s_hbm.shape
    copies = []
    for i in range(depth // chunk):
        c = pl.ds(i * chunk, chunk)
        pairs = [
            (x_hbm.at[:, c], xb.at[:, c]),
            (wk_hbm.at[c, :], wkb.at[c, :]),
            (wv_hbm.at[c, :], wvb.at[c, :]),
        ]
        copies.append([pltpu.make_async_copy(a, b, sem.at[i, n]) for n, (a, b) in enumerate(pairs)])
        for copy in copies[-1]:
            copy.start()
        if i == 0:
            step_copy = pltpu.make_async_copy(s_hbm, sb, sem.at[0, 3])
            step_copy.start()
    acc = sacc = None
    for i, these in enumerate(copies):
        for copy in these:
            copy.wait()
        c = slice(i * chunk, (i + 1) * chunk)
        w = jnp.concatenate([wkb[c, :], wvb[c, :]], 1)
        if i == 0:
            step_copy.wait()
        for r in range(groups):
            wide[r * steps : (r + 1) * steps, c] = sb[r, :, c].astype(F32)
        part = jnp.dot(xb[:, c], w, preferred_element_type=F32)
        spart = jnp.dot(wide[:, c].astype(BF16), w, preferred_element_type=F32)
        acc = part if acc is None else acc + part
        sacc = spart if sacc is None else sacc + spart
    for at, first in enumerate((0, 2 * HD, HD, 3 * HD)):
        kv_ref[at] = acc[:, first : first + HD].astype(BF16)
        skv_ref[at] = sacc[:, first : first + HD].astype(BF16)


def project(x, steps, w_key, w_value):
    rows, depth = x.shape
    srows = steps.shape[0] * steps.shape[1]
    chunk = 1024
    hbm = pl.BlockSpec(memory_space=pl.ANY)
    vmem = pl.BlockSpec(memory_space=pltpu.VMEM)
    return pl.pallas_call(
        functools.partial(project_kernel, chunk=chunk),
        in_specs=[hbm] * 4,
        out_specs=[vmem] * 2,
        out_shape=[
            jax.ShapeDtypeStruct((4, rows, HD), BF16),
            jax.ShapeDtypeStruct((4, srows, HD), BF16),
        ],
        scratch_shapes=[
            pltpu.VMEM(x.shape, BF16),
            pltpu.VMEM(steps.shape, BF16),
            pltpu.VMEM(w_key.shape, BF16),
            pltpu.VMEM(w_value.shape, BF16),
            pltpu.VMEM((srows, depth), F32),
            pltpu.SemaphoreType.DMA((depth // chunk, 4)),
        ],
        compiler_params=params(28),
        cost_estimate=pl.CostEstimate(
            flops=2 * (rows + srows) * depth * 4 * HD,
            bytes_accessed=2 * depth * (rows + srows + 4 * HD),
            transcendentals=0,
        ),
        name="project",
    )(*map(in_hbm, (x, steps, w_key, w_value)))


def scores(q, k):
    return lax.dot_general(q, k, NT, preferred_element_type=F32)


def settle(s, v, state=None):
    m = jnp.max(s, axis=1, keepdims=True)
    if state is not None:
        m = jnp.maximum(m, state[0])
    p = jnp.exp2((s - m) * SCALE).astype(BF16)
    acc = jnp.dot(p, v, preferred_element_type=F32)
    if state is not None:
        acc = acc + state[1] * jnp.exp2((state[0] - m) * SCALE)
    return m, acc


def in_turn(items, score, finish):
    ahead = score(items[0])
    for i, item in enumerate(items):
        now = ahead
        if i + 1 < len(items):
            ahead = score(items[i + 1])
        finish(item, now)


def keys_of(k, kf):
    return jnp.concatenate([k, kf], 1)


def query_of(q_ref, qf_ref, h, first, count):
    q = q_ref[first : first + count, h * HD : (h + 1) * HD]
    return jnp.concatenate([q, qf_ref[first : first + count, :]], 1)


def near_kernel(sc, q_ref, qf_ref, own_ref, sib_ref, kf_ref, acc_ref, ml_ref):
    group = pl.program_id(0)
    kvh = group * STATE // GQ
    rows = q_ref.shape[0]
    half = rows // 2
    own = pl.multiple_of(sc[S_OWN] * rows, rows)
    sib = pl.multiple_of((sc[S_OWN] ^ 1) * rows, rows)
    lane = lax.broadcasted_iota(jnp.int32, (half, HD), 1)

    def run(with_sib):
        k = keys_of(own_ref[2 * kvh], kf_ref[pl.ds(own, rows), :])
        v = with_ones(own_ref[2 * kvh + 1])
        ks = [k[:half], k]
        vs = [v[:half], v]
        if with_sib:
            k = keys_of(sib_ref[2 * kvh], kf_ref[pl.ds(sib, rows), :])
            v = with_ones(sib_ref[2 * kvh + 1])
            ks = [jnp.concatenate([a, k], 0) for a in ks]
            vs = [jnp.concatenate([a, v], 0) for a in vs]
        ml = [jnp.zeros((half, HD), F32)] * 2

        def score(item):
            h, part = item
            q = [query_of(q_ref, qf_ref, h + i, part * half, half) for i in range(HN)]
            s = scores(jnp.concatenate(q, 0), ks[part])
            own_cols = (part + 1) * half
            at_row = lax.broadcasted_iota(jnp.int32, (HN * half, half), 0) % half
            at_col = lax.broadcasted_iota(jnp.int32, (HN * half, half), 1)
            corner = jnp.where(at_col <= at_row, s[:, own_cols - half : own_cols], HIDE)
            cut = [s[:, : own_cols - half]] * (part > 0) + [corner] + [s[:, own_cols:]] * with_sib
            return jnp.concatenate(cut, 1)

        def finish(item, s):
            h0, part = item
            ms, accs = settle(s, vs[part])
            for i in range(HN):
                h = h0 + i
                m, acc = ms[i * half : (i + 1) * half], accs[i * half : (i + 1) * half]
                acc_ref[group, part * half : (part + 1) * half, h * HD : (h + 1) * HD] = acc[:, :HD]
                ml[part] = jnp.where(lane == h, m, jnp.where(lane == STATE + h, acc[:, HD:], ml[part]))

        in_turn([(h, part) for h in range(0, STATE, HN) for part in (0, 1)], score, finish)
        for part in (0, 1):
            ml_ref[group, part * half : (part + 1) * half, :] = ml[part]

    @pl.when(sc[S_SIB] == 0)
    def _():
        run(0)

    @pl.when(sc[S_SIB] != 0)
    def _():
        run(1)


def far_kernel(sc, q_ref, qf_ref, far_ref, fs_ref, kf_ref, acc_ref, ml_ref, *rest):
    group = pl.program_id(0)
    kvh = group * STATE // GQ
    o_ref = rest[-1]
    rows = q_ref.shape[0]
    half = rows // 2
    far = pl.multiple_of((sc[S_OWN] ^ 2) * rows, rows)
    farsib = pl.multiple_of((sc[S_OWN] ^ 3) * rows, rows)

    def run(with_far, with_farsib):
        ks, vs = [], []
        if with_far:
            ks.append(keys_of(far_ref[2 * kvh], kf_ref[pl.ds(far, rows), :]))
            vs.append(with_ones(far_ref[2 * kvh + 1]))
        if with_farsib:
            ks.append(keys_of(fs_ref[2 * kvh], kf_ref[pl.ds(farsib, rows), :]))
            vs.append(with_ones(fs_ref[2 * kvh + 1]))
        if ks:
            k, v = jnp.concatenate(ks, 0), jnp.concatenate(vs, 0)

        def score(item):
            q = [query_of(q_ref, qf_ref, item + i, 0, rows) for i in range(HF)]
            return scores(jnp.concatenate(q, 0), k) if ks else None

        def finish(item, s):
            state = []
            for h in range(item, item + HF):
                ml = ml_ref[group]
                l = jnp.broadcast_to(ml[:, STATE + h : STATE + h + 1], (rows, HD))
                acc = jnp.concatenate([acc_ref[group, :, h * HD : (h + 1) * HD], l], 1)
                state.append((ml[:, h : h + 1], acc))
            m = jnp.concatenate([x[0] for x in state], 0)
            acc = jnp.concatenate([x[1] for x in state], 0)
            if ks:
                acc = settle(s, v, (m, acc))[1]
            out = (acc[:, :HD] / acc[:, HD:]).astype(BF16)
            for i in range(HF):
                o_ref[:, (item + i) * HD : (item + i + 1) * HD] = out[i * rows : (i + 1) * rows]

        in_turn(list(range(0, STATE, HF)), score, finish)

    for a in (0, 1):
        for b in (0, 1):
            pl.when((sc[S_FAR] == a) & (sc[S_FARSIB] == b))(functools.partial(run, a, b))


STATE = 4
HN = 2
HF = 1


def prefill(kernel, name, scalars, q, qf, one, two, kf, state=(), after=()):
    rows, width = q.shape
    wide = STATE * HD
    groups = width // wide
    columns = pl.BlockSpec((rows, wide), lambda g, sc: (0, g))
    vmem = pl.BlockSpec(memory_space=pltpu.VMEM)
    hbm = pl.BlockSpec(memory_space=pl.ANY)
    first = not state
    return pl.pallas_call(
        kernel,
        grid_spec=pltpu.PrefetchScalarGridSpec(
            num_scalar_prefetch=1,
            grid=(groups,),
            in_specs=[columns] + [vmem] * (4 + len(state))
            + [hbm] * len(after),
            out_specs=[vmem, vmem] if first else columns,
        ),
        out_shape=[
            pltpu.VMEM((groups, rows, wide), F32),
            pltpu.VMEM((groups, rows, HD), F32),
        ]
        if first
        else jax.ShapeDtypeStruct(q.shape, BF16),
        compiler_params=params(20),
        cost_estimate=pl.CostEstimate(
            flops=8 * GQ * rows * rows * 2 * 2 * HD, bytes_accessed=4 * 2**20, transcendentals=0
        ),
        name=name,
    )(scalars, in_vmem(q), in_vmem(qf), in_vmem(one), in_vmem(two), in_vmem(kf), *map(in_vmem, state), *after)


def context_kernel(sc, q_ref, ck_ref, cv_ref, own_ref, acc_ref, ml_ref, *, steps):
    srows = q_ref.shape[0]
    n = ck_ref.shape[0]
    block = 1024
    live = sc[S_LEN]
    lane = lax.broadcasted_iota(jnp.int32, (srows, HD), 1)
    q_mark = jnp.where(lane == 0, 1.0, 0.0).astype(BF16)
    zero = jnp.zeros((srows, HD), BF16)
    at_row = lax.broadcasted_iota(jnp.int32, (DEC * srows, srows), 0) % srows
    at_col = lax.broadcasted_iota(jnp.int32, (DEC * srows, srows), 1)
    own_mask = (at_row // steps == at_col // steps) & (at_col <= at_row)
    keys = {}
    for first in range(0, n, block):
        pos = lax.broadcasted_iota(jnp.int32, (block, HD), 0) + first
        col = lax.broadcasted_iota(jnp.int32, (block, HD), 1)
        mark = jnp.where((pos >= live) & (col == 0), HIDE, 0.0).astype(BF16)
        for kvh in (0, 1):
            r, c = slice(first, first + block), slice(kvh * HD, (kvh + 1) * HD)
            keys[kvh, first] = jnp.concatenate([ck_ref[r, c], mark], 1), with_ones(cv_ref[r, c])
    state = {}
    ml = [jnp.zeros((srows, HD), F32)]

    def query(g):
        cut = [q_ref[:, h * HD : (h + 1) * HD] for h in range(g * DEC, (g + 1) * DEC)]
        return jnp.concatenate([jnp.concatenate([q, q_mark], 1) for q in cut], 0)

    def score(item):
        g, first = item
        kvh = g * DEC // GQ
        if first < 0:
            s = scores(query(g), jnp.concatenate([own_ref[2 * kvh], zero], 1))
            return jnp.where(own_mask, s, HIDE)
        return scores(query(g), keys[kvh, first][0])

    def finish(item, s):
        g, first = item
        kvh = g * DEC // GQ
        v = with_ones(own_ref[2 * kvh + 1]) if first < 0 else keys[kvh, first][1]
        state[g] = settle(s, v, state.get(g))
        if first == n - block:
            m, acc = state[g]
            for i in range(DEC):
                at = g * DEC + i
                a = acc[i * srows : (i + 1) * srows]
                acc_ref[:, at * HD : (at + 1) * HD] = a[:, :HD]
                ml[0] = jnp.where(lane == at, m[i * srows : (i + 1) * srows], ml[0])
                ml[0] = jnp.where(lane == 2 * GQ + at, a[:, HD:], ml[0])

    groups = 2 * GQ // DEC
    in_turn([(g, first) for g in range(groups) for first in [-1, *range(0, n, block)]], score, finish)
    ml_ref[...] = ml[0]


def context_part(scalars, q, ck, cv, own, steps):
    srows, width = q.shape[0], q.shape[1] - HD
    return pl.pallas_call(
        functools.partial(context_kernel, steps=steps),
        grid_spec=pltpu.PrefetchScalarGridSpec(
            num_scalar_prefetch=1,
            grid=(1,),
            in_specs=[pl.BlockSpec(memory_space=pltpu.VMEM)] * 4,
            out_specs=[
                pl.BlockSpec((srows, width), lambda i, sc: (0, 0)),
                pl.BlockSpec((srows, HD), lambda i, sc: (0, 0)),
            ],
        ),
        out_shape=[
            jax.ShapeDtypeStruct((srows, width), F32),
            jax.ShapeDtypeStruct((srows, HD), F32),
        ],
        compiler_params=params(12),
        name="context_part",
    )(scalars, q, in_vmem(ck), in_vmem(cv), own)


DEC = 8


def pieces(x):
    hi = x.astype(BF16)
    rest = x - hi.astype(F32)
    mid = rest.astype(BF16)
    return hi, mid, (rest - mid.astype(F32)).astype(BF16)


def turn_kernel(sc, p0, p1, p2, p3, own, sib, far, fs, xp, xps, xm, xms, kfo, kfx, o0, o1, o2, o3, ks, vs, qs, os):
    head = pl.program_id(0)
    srows = p0.shape[0]
    rows = own.shape[1]
    keys = 4 * rows
    wide = GQ * HD
    for which, refs, first, kf in ((0, (own, sib, far, fs), S_OWN, kfo), (1, (xp, xps, xm, xms), S_XP, kfx)):
        wanted = [(sc[S_REL + j] != 0) & (sc[S_WHICH + j] == which) for j in range(4)]

        @pl.when(wanted[0] | wanted[1] | wanted[2] | wanted[3])
        def _():
            ks[which, :, HD:] = kf[...]
            vs[which, :, HD:] = jnp.ones((keys, HD), BF16)
            for i, ref in enumerate(refs):
                at = pl.multiple_of((sc[first] ^ i) * rows, rows)
                ks[which, pl.ds(at, rows), :HD] = ref[2 * head]
                vs[which, pl.ds(at, rows), :HD] = ref[2 * head + 1]

    for j, p in enumerate((p0, p1, p2, p3)):

        @pl.when(sc[S_REL + j] != 0)
        def _():
            qs[j, :, :wide] = p[:, pl.ds(pl.multiple_of(head * wide, wide), wide)]
            qs[j, :, wide:] = p[:, 2 * wide :]

    lane = lax.broadcasted_iota(jnp.int32, (srows, HD), 1)
    block = 1024

    def one(j, carry):
        @pl.when(sc[S_REL + j] != 0)
        def _():
            which = sc[S_WHICH + j]
            feat = qs[j, :, wide:]
            state = {}
            ml = [jnp.zeros((srows, HD), F32)] * 2

            def score(item):
                g, first = item
                cut = [qs[j, :, h * HD : (h + 1) * HD] for h in range(g * DEC, (g + 1) * DEC)]
                q = jnp.concatenate([jnp.concatenate([q, feat], 1) for q in cut], 0)
                return scores(q, ks[which, first : first + block, :])

            def finish(item, s):
                g, first = item
                state[g] = settle(s, vs[which, first : first + block, :], state.get(g))
                if first == keys - block:
                    m, acc = state[g]
                    for i in range(DEC):
                        h = g * DEC + i
                        r = slice(i * srows, (i + 1) * srows)
                        os[j, :, h * HD : (h + 1) * HD] = acc[r, :HD].astype(BF16)
                        for part in range(3):
                            ml[0] = jnp.where(lane == part * GQ + h, m[r], ml[0])
                            ml[1] = jnp.where(lane == (part + 3) * GQ + h, acc[r, HD:], ml[1])

            in_turn([(g, first) for first in range(0, keys, block) for g in range(GQ // DEC)], score, finish)
            m3, l3 = pieces(ml[0]), pieces(ml[1])
            ext = jnp.zeros((srows, HD), F32)
            for part in range(3):
                ext = jnp.where(lane // GQ == part, m3[part].astype(F32), ext)
                ext = jnp.where(lane // GQ == part + 3, l3[part].astype(F32), ext)
            os[j, :, wide:] = ext.astype(BF16)

        return carry

    lax.fori_loop(0, 4, one, 0)
    for j, o in enumerate((o0, o1, o2, o3)):
        o[...] = os[j]


def turn_part(scalars, packets, kvs, kf_own, kf_other, after):
    srows = packets[0].shape[0]
    rows = kvs[0].shape[1]
    wide = GQ * HD + HD

    def kernel(*refs):
        turn_kernel(*refs[:15], *refs[15 + len(after) :])

    return pl.pallas_call(
        kernel,
        grid_spec=pltpu.PrefetchScalarGridSpec(
            num_scalar_prefetch=1,
            grid=(2,),
            in_specs=[pl.BlockSpec(memory_space=pltpu.VMEM)] * 14
            + [pl.BlockSpec(memory_space=pl.ANY)] * len(after),
            out_specs=[pl.BlockSpec((srows, wide), lambda g, sc: (0, g))] * 4,
            scratch_shapes=[
                pltpu.VMEM((2, 4 * rows, 2 * HD), BF16),
                pltpu.VMEM((2, 4 * rows, 2 * HD), BF16),
                pltpu.VMEM((4, srows, wide), BF16),
                pltpu.VMEM((4, srows, wide), BF16),
            ],
        ),
        out_shape=[jax.ShapeDtypeStruct((srows, 2 * wide), BF16)] * 4,
        compiler_params=params(20),
        cost_estimate=pl.CostEstimate(
            flops=4 * 4 * srows * GQ * 4 * rows * 2 * HD, bytes_accessed=4 * 2**20, transcendentals=0
        ),
        name="turn_part",
    )(scalars, *map(in_vmem, packets), *map(in_vmem, kvs), in_vmem(kf_own), in_vmem(kf_other), *after)


def merge_kernel(sc, acc_ref, ml_ref, *refs):
    o_ref, wide = refs[-2:]
    sel = sc[S_SEL]
    groups, steps, _ = o_ref.shape
    ml = ml_ref[...]
    width = GQ * HD
    for kvh in range(2):
        first = kvh * (width + HD)

        def pick(cols):
            cols = slice(first + cols.start, first + cols.stop)
            x = refs[0][:, cols]
            for j in (1, 2, 3):
                x = jnp.where(sel == j, refs[j][:, cols], x)
            return x.astype(F32)

        ext = pick(slice(width, width + HD))
        whole = [
            ext[:, i * GQ : (i + 1) * GQ]
            + ext[:, (i + 1) * GQ : (i + 2) * GQ]
            + ext[:, (i + 2) * GQ : (i + 3) * GQ]
            for i in (0, 3)
        ]
        m2, l2 = whole
        m1 = ml[:, kvh * GQ : (kvh + 1) * GQ]
        l1 = ml[:, (2 + kvh) * GQ : (3 + kvh) * GQ]
        m = jnp.maximum(m1, m2)
        w1, w2 = jnp.exp2((m1 - m) * SCALE), jnp.exp2((m2 - m) * SCALE)
        total = l1 * w1 + l2 * w2
        w1, w2 = w1 / total, w2 / total
        for h in range(GQ):
            at = kvh * GQ + h
            a1 = acc_ref[:, at * HD : (at + 1) * HD]
            a2 = pick(slice(h * HD, (h + 1) * HD))
            wide[:, at * HD : (at + 1) * HD] = a1 * w1[:, h : h + 1] + a2 * w2[:, h : h + 1]
    for r in range(groups):
        o_ref[r] = wide[r * steps : (r + 1) * steps, :].astype(BF16)


def merge(scalars, acc, ml, back, steps):
    args = (acc, ml, *back)
    shape = (acc.shape[0] // steps, steps, acc.shape[1])
    return pl.pallas_call(
        merge_kernel,
        grid_spec=pltpu.PrefetchScalarGridSpec(
            num_scalar_prefetch=1,
            grid=(1,),
            in_specs=[pl.BlockSpec(a.shape, lambda i, sc: (0, 0)) for a in args],
            out_specs=pl.BlockSpec(shape, lambda i, sc: (0, 0, 0)),
            scratch_shapes=[pltpu.VMEM(acc.shape, F32)],
        ),
        out_shape=jax.ShapeDtypeStruct(shape, BF16),
        compiler_params=params(8),
        name="merge",
    )(scalars, *args)


ROW = ("xlo", "xhi")


def row_index(x):
    return x % 2 * 2 + x // 2


def from_x(a, shift):
    return lax.ppermute(a, ROW, [(row_index((x + shift) % 4), row_index(x)) for x in range(4)])


def from_y(a, shift):
    return lax.ppermute(a, "y", [((y + shift) % 4, y) for y in range(4)])


def from_core(a):
    return lax.ppermute(a, "core", [(0, 1), (1, 0)])


def body(
    turn_hidden,
    w_key,
    w_value,
    turn_queries,
    turn_speaker,
    speaker_mask,
    shard_block,
    context_keys,
    context_values,
    context_length,
    decode_home,
    step_hidden,
    step_queries,
    row_speaker,
):
    steps = step_hidden.shape[1]
    tie = lax.optimization_barrier
    own, step_kv = project(turn_hidden, step_hidden, w_key, w_value)
    sib, far, xp, xm = from_core(own), from_x(own, 2), from_x(own, 1), from_x(own, 3)
    sib, row_speaker, shard_block = tie((sib, row_speaker, shard_block))
    packet = make_packet(row_speaker, step_queries)
    packets = [packet, from_y(packet, 1), from_y(packet, 2), None]
    scalars, qf, kf_own, kf_other = prepare(
        shard_block, decode_home, context_length, speaker_mask, turn_speaker
    )
    near = prefill(near_kernel, "prefill_near", scalars, turn_queries, qf, own, sib, kf_own)
    packets[0], packets[1], packets[2], _ = tie((*packets[:3], near[1]))
    packets[3] = from_y(packets[0], 3)
    ctx = context_part(scalars, packets[0], context_keys, context_values, step_kv, steps)
    far, xp, xm, packets[3], _ = tie((far, xp, xm, packets[3], ctx[1]))
    farsib, xps, xms = from_core(far), from_core(xp), from_core(xm)
    moved = (own, sib, far, farsib, xp, xps, xm, xms)
    parts = turn_part(scalars, packets, moved, kf_own, kf_other, (ctx[1],))
    back = [parts[0]] + [from_y(parts[j], -j) for j in (1, 2, 3)]
    turn_attention = prefill(
        far_kernel, "prefill_far", scalars, turn_queries, qf, far, farsib, kf_own, near, (parts[0],)
    )
    step_attention = merge(scalars, *ctx, back, steps)
    return turn_attention, step_attention


def solution(mesh):
    heads = mesh.shape["head"]
    fine = Mesh(mesh.devices.reshape(2, 4, 2, 2, heads), ("xlo", "y", "xhi", "core", "head"))
    split = ("xlo", "y", "xhi", "core")
    return jax.shard_map(
        body,
        mesh=fine,
        in_specs=(
            P(split, None),
            P(None, "head"),
            P(None, "head"),
            P(split, "head"),
            P(),
            P(),
            P(),
            P(split, "head"),
            P(split, "head"),
            P(),
            P(),
            P(split, None, None),
            P(split, None, "head"),
            P(split),
        ),
        out_specs=(P(split, "head"), P(split, None, "head")),
        check_vma=False,
    )
```

```python
import functools
import math

import jax
import jax.numpy as jnp
from jax import lax
from jax.experimental import pallas as pl
from jax.experimental.pallas import tpu as pltpu
from jax.sharding import Mesh
from jax.sharding import PartitionSpec as P

HQ = 64
KVH = 8
HD = 128
SPK = 4
GQ = HQ // KVH

HIDE = -1e30
SCALE = math.log2(math.e) / math.sqrt(HD)
NT = (((1,), (1,)), ((), ()))
F32 = jnp.float32
BF16 = jnp.bfloat16

S_OWN, S_SIB, S_FAR, S_FARSIB, S_REL, S_WHICH, S_SEL, S_LEN, S_XP, S_EARLY = 0, 1, 2, 3, 4, 8, 12, 13, 14, 15


def params(mib):
    return pltpu.CompilerParams(vmem_limit_bytes=mib * 2**20)


def in_vmem(x):
    return pltpu.with_memory_space_constraint(x, pltpu.VMEM)


def in_hbm(x):
    return pltpu.with_memory_space_constraint(x, pltpu.HBM)


def with_ones(v):
    return jnp.concatenate([v, jnp.ones(v.shape, BF16)], 1)


def marks(table, speakers):
    row = lax.broadcasted_iota(jnp.int32, (8, HD), 0)
    hot = jnp.where(speakers == row, 1.0, 0.0).astype(BF16)
    out = lax.dot_general(hot, table, (((0,), (0,)), ((), ())), preferred_element_type=F32)
    return out.astype(BF16)


def prep_kernel(blocks, homes, lengths, mask, spk_ref, sc, qf_ref, kfo_ref, kfx_ref):
    xlo, y, xhi, core = (lax.axis_index(a) for a in ("xlo", "y", "xhi", "core"))
    own_at = xhi * 2 + core
    dialog = xlo * 4 + y
    here = blocks[dialog * 4 + own_at]
    sc[S_OWN] = own_at
    for i, at in ((1, S_SIB), (2, S_FAR), (3, S_FARSIB)):
        sc[at] = jnp.where(blocks[dialog * 4 + (own_at ^ i)] < here, 1, 0)
    for j in range(4):
        home = homes[xlo * 16 + (y + j) % 4 * 4 + own_at]
        sc[S_REL + j] = jnp.where(home % 4 == y, 1, 0)
        sc[S_WHICH + j] = jnp.where(home // 4 != xlo, 1, 0)
    home = homes[xlo * 16 + y * 4 + own_at]
    sc[S_SEL] = (y - home % 4 + 4) % 4
    sc[S_LEN] = lengths[home]
    sc[S_XP] = (xhi ^ xlo) * 2 + core

    most = jnp.int32(0)
    mine = jnp.int32(0)
    for c in range(8):
        rows_of = [homes[c // 4 * 16 + at * 4 + c % 4] % 4 for at in range(4)]
        for at in range(4):
            count = sum(jnp.where(r == at, 1, 0) for r in rows_of)
            most = jnp.maximum(most, count)
            mine = jnp.where((c == xlo * 4 + own_at) & (y == at), count, mine)
    sc[S_EARLY] = jnp.minimum((most - mine) * 2 // 3, 3)

    row = lax.broadcasted_iota(jnp.int32, (8, HD), 0)
    lane = lax.broadcasted_iota(jnp.int32, (8, HD), 1)
    for d, out in ((dialog, kfo_ref), ((1 - xlo) * 4 + y, kfx_ref)):
        table = jnp.zeros((8, HD), F32)
        for a in range(SPK):
            for b in range(SPK):
                add = jnp.where(mask[a, b, d] == 1, 0.0, HIDE)
                table = jnp.where((row == b) & (lane == a), add, table)
        table = table.astype(BF16)
        for i in range(16):
            out[i * HD : (i + 1) * HD, :] = marks(table, spk_ref[d * 2 + i // 8, i % 8 : i % 8 + 1, :])
    eye = jnp.where((row == lane) & (row < SPK), 1.0, 0.0).astype(BF16)
    for i in range(4):
        at = (dialog * 4 + own_at) * 4 + i
        qf_ref[i * HD : (i + 1) * HD, :] = marks(eye, spk_ref[at // 8, pl.ds(at % 8, 1), :])


def prepare(blocks, homes, lengths, mask, spk):
    rows = spk.size // 32
    smem = pl.BlockSpec(memory_space=pltpu.SMEM)
    vmem = pl.BlockSpec(memory_space=pltpu.VMEM)
    return pl.pallas_call(
        prep_kernel,
        in_specs=[smem] * 4 + [vmem],
        out_specs=[smem] + [vmem] * 3,
        out_shape=[
            jax.ShapeDtypeStruct((16,), jnp.int32),
            pltpu.VMEM((rows, HD), BF16),
            pltpu.VMEM((4 * rows, HD), BF16),
            pltpu.VMEM((4 * rows, HD), BF16),
        ],
        compiler_params=params(6),
        name="prepare",
    )(blocks, homes, lengths, mask.transpose(1, 2, 0), spk.reshape(-1, 8, HD))


def packet_kernel(row_spk, q_ref, pk_ref, wide):
    groups, steps, width = q_ref.shape
    srows = groups * steps
    for r in range(groups):
        wide[r * steps : (r + 1) * steps, :] = q_ref[r].astype(F32)
    pk_ref[:, :width] = wide[...].astype(BF16)
    row = lax.broadcasted_iota(jnp.int32, (srows, HD), 0)
    lane = lax.broadcasted_iota(jnp.int32, (srows, HD), 1)
    speaker = jnp.zeros((srows, HD), jnp.int32)
    for r in range(groups):
        speaker = jnp.where(row // steps == r, row_spk[r], speaker)
    pk_ref[:, width:] = jnp.where(lane == speaker, 1.0, 0.0).astype(BF16)


def make_packet(row_spk, queries):
    groups, steps, width = queries.shape
    return pl.pallas_call(
        packet_kernel,
        in_specs=[pl.BlockSpec(memory_space=pltpu.SMEM), pl.BlockSpec(memory_space=pltpu.VMEM)],
        out_specs=pl.BlockSpec(memory_space=pltpu.VMEM),
        out_shape=jax.ShapeDtypeStruct((groups * steps, width + HD), BF16),
        scratch_shapes=[pltpu.VMEM((groups * steps, width), F32)],
        compiler_params=params(4),
        name="packet",
    )(row_spk, queries)


def project_kernel(x_hbm, s_hbm, wk_hbm, wv_hbm, kv_ref, skv_ref, xb, sb, wkb, wvb, wide, sem, *, chunk):
    groups, steps, depth = s_hbm.shape
    copies = []
    for i in range(depth // chunk):
        c = pl.ds(i * chunk, chunk)
        pairs = [
            (x_hbm.at[:, c], xb.at[:, c]),
            (wk_hbm.at[c, :], wkb.at[c, :]),
            (wv_hbm.at[c, :], wvb.at[c, :]),
        ]
        copies.append([pltpu.make_async_copy(a, b, sem.at[i, n]) for n, (a, b) in enumerate(pairs)])
        for copy in copies[-1]:
            copy.start()
        if i == 0:
            step_copy = pltpu.make_async_copy(s_hbm, sb, sem.at[0, 3])
            step_copy.start()
    acc = None
    for i, these in enumerate(copies):
        for copy in these:
            copy.wait()
        c = slice(i * chunk, (i + 1) * chunk)
        w = jnp.concatenate([wkb[c, :], wvb[c, :]], 1)
        if i == 0:
            step_copy.wait()
        for r in range(groups):
            wide[r * steps : (r + 1) * steps, c] = sb[r, :, c].astype(F32)
        both = jnp.concatenate([xb[:, c], wide[:, c].astype(BF16)], 0)
        part = jnp.dot(both, w, preferred_element_type=F32)
        acc = part if acc is None else acc + part
    rows = xb.shape[0]
    for at, first in enumerate((0, 2 * HD, HD, 3 * HD)):
        kv_ref[at] = acc[:rows, first : first + HD].astype(BF16)
        skv_ref[at] = acc[rows:, first : first + HD].astype(BF16)


def project(x, steps, w_key, w_value):
    rows, depth = x.shape
    srows = steps.shape[0] * steps.shape[1]
    chunk = 1024
    hbm = pl.BlockSpec(memory_space=pl.ANY)
    vmem = pl.BlockSpec(memory_space=pltpu.VMEM)
    return pl.pallas_call(
        functools.partial(project_kernel, chunk=chunk),
        in_specs=[hbm] * 4,
        out_specs=[vmem] * 2,
        out_shape=[
            jax.ShapeDtypeStruct((4, rows, HD), BF16),
            jax.ShapeDtypeStruct((4, srows, HD), BF16),
        ],
        scratch_shapes=[
            pltpu.VMEM(x.shape, BF16),
            pltpu.VMEM(steps.shape, BF16),
            pltpu.VMEM(w_key.shape, BF16),
            pltpu.VMEM(w_value.shape, BF16),
            pltpu.VMEM((srows, depth), F32),
            pltpu.SemaphoreType.DMA((depth // chunk, 4)),
        ],
        compiler_params=params(28),
        cost_estimate=pl.CostEstimate(
            flops=2 * (rows + srows) * depth * 4 * HD,
            bytes_accessed=2 * depth * (rows + srows + 4 * HD),
            transcendentals=0,
        ),
        name="project",
    )(*map(in_hbm, (x, steps, w_key, w_value)))


def scores(q, k):
    return lax.dot_general(q, k, NT, preferred_element_type=F32)


def settle(s, v, state=None):
    m = jnp.max(s, axis=1, keepdims=True)
    if state is not None:
        m = jnp.maximum(m, state[0])
    p = jnp.exp2((s - m) * SCALE).astype(BF16)
    acc = jnp.dot(p, v, preferred_element_type=F32)
    if state is not None:
        acc = acc + state[1] * jnp.exp2((state[0] - m) * SCALE)
    return m, acc


def in_turn(items, score, finish):
    ahead = score(items[0])
    for i, item in enumerate(items):
        now = ahead
        if i + 1 < len(items):
            ahead = score(items[i + 1])
        finish(item, now)


def keys_of(k, kf):
    return jnp.concatenate([k, kf], 1)


def query_of(q_ref, qf_ref, h, first, count):
    q = q_ref[first : first + count, h * HD : (h + 1) * HD]
    return jnp.concatenate([q, qf_ref[first : first + count, :]], 1)


def near_kernel(sc, q_ref, qf_ref, own_ref, sib_ref, kf_ref, *refs, first):
    acc_ref, ml_ref = refs[-2:]
    group = pl.program_id(0) + first
    kvh = group * STATE // GQ
    rows = q_ref.shape[0]
    half = rows // 2
    own = pl.multiple_of(sc[S_OWN] * rows, rows)
    sib = pl.multiple_of((sc[S_OWN] ^ 1) * rows, rows)
    lane = lax.broadcasted_iota(jnp.int32, (half, HD), 1)

    def run(with_sib):
        k = keys_of(own_ref[2 * kvh], kf_ref[pl.ds(own, rows), :])
        v = with_ones(own_ref[2 * kvh + 1])
        ks = [k[:half], k]
        vs = [v[:half], v]
        if with_sib:
            k = keys_of(sib_ref[2 * kvh], kf_ref[pl.ds(sib, rows), :])
            v = with_ones(sib_ref[2 * kvh + 1])
            ks = [jnp.concatenate([a, k], 0) for a in ks]
            vs = [jnp.concatenate([a, v], 0) for a in vs]
        ml = [jnp.zeros((half, HD), F32)] * 2

        def score(item):
            h, part = item
            q = [query_of(q_ref, qf_ref, h + i, part * half, half) for i in range(HN)]
            s = scores(jnp.concatenate(q, 0), ks[part])
            own_cols = (part + 1) * half
            at_row = lax.broadcasted_iota(jnp.int32, (HN * half, half), 0) % half
            at_col = lax.broadcasted_iota(jnp.int32, (HN * half, half), 1)
            corner = jnp.where(at_col <= at_row, s[:, own_cols - half : own_cols], HIDE)
            cut = [s[:, : own_cols - half]] * (part > 0) + [corner] + [s[:, own_cols:]] * with_sib
            return jnp.concatenate(cut, 1)

        def finish(item, s):
            h0, part = item
            ms, accs = settle(s, vs[part])
            for i in range(HN):
                h = h0 + i
                m, acc = ms[i * half : (i + 1) * half], accs[i * half : (i + 1) * half]
                acc_ref[group, part * half : (part + 1) * half, h * HD : (h + 1) * HD] = acc[:, :HD]
                ml[part] = jnp.where(lane == h, m, jnp.where(lane == STATE + h, acc[:, HD:], ml[part]))

        in_turn([(h, part) for h in range(0, STATE, HN) for part in (0, 1)], score, finish)
        for part in (0, 1):
            ml_ref[group, part * half : (part + 1) * half, :] = ml[part]

    @pl.when(sc[S_SIB] == 0)
    def _():
        run(0)

    @pl.when(sc[S_SIB] != 0)
    def _():
        run(1)


def far_kernel(sc, q_ref, qf_ref, far_ref, fs_ref, kf_ref, acc_ref, ml_ref, *rest, early):
    group = pl.program_id(0)
    kvh = group * STATE // GQ
    o_ref = rest[-1]
    rows = q_ref.shape[0]
    half = rows // 2
    far = pl.multiple_of((sc[S_OWN] ^ 2) * rows, rows)
    farsib = pl.multiple_of((sc[S_OWN] ^ 3) * rows, rows)

    def run(with_far, with_farsib):
        ks, vs = [], []
        if with_far:
            ks.append(keys_of(far_ref[2 * kvh], kf_ref[pl.ds(far, rows), :]))
            vs.append(with_ones(far_ref[2 * kvh + 1]))
        if with_farsib:
            ks.append(keys_of(fs_ref[2 * kvh], kf_ref[pl.ds(farsib, rows), :]))
            vs.append(with_ones(fs_ref[2 * kvh + 1]))
        if ks:
            k, v = jnp.concatenate(ks, 0), jnp.concatenate(vs, 0)

        def score(item):
            q = [query_of(q_ref, qf_ref, item + i, 0, rows) for i in range(HF)]
            return scores(jnp.concatenate(q, 0), k) if ks else None

        def finish(item, s):
            state = []
            for h in range(item, item + HF):
                ml = ml_ref[group]
                l = jnp.broadcast_to(ml[:, STATE + h : STATE + h + 1], (rows, HD))
                acc = jnp.concatenate([acc_ref[group, :, h * HD : (h + 1) * HD], l], 1)
                state.append((ml[:, h : h + 1], acc))
            m = jnp.concatenate([x[0] for x in state], 0)
            acc = jnp.concatenate([x[1] for x in state], 0)
            if ks:
                acc = settle(s, v, (m, acc))[1]
            out = (acc[:, :HD] / acc[:, HD:]).astype(BF16)
            for i in range(HF):
                o_ref[:, (item + i) * HD : (item + i + 1) * HD] = out[i * rows : (i + 1) * rows]

        in_turn(list(range(0, STATE, HF)), score, finish)

    mine = (group < sc[S_EARLY]) == early
    for a in (0, 1):
        for b in (0, 1):
            pl.when(mine & (sc[S_FAR] == a) & (sc[S_FARSIB] == b))(functools.partial(run, a, b))


STATE = 4
HN = 2
HF = 1


def prefill_near(scalars, q, qf, own, sib, kf, first, count, state=()):
    rows, width = q.shape
    wide = STATE * HD
    groups = width // wide
    vmem = pl.BlockSpec(memory_space=pltpu.VMEM)
    return pl.pallas_call(
        functools.partial(near_kernel, first=first),
        grid_spec=pltpu.PrefetchScalarGridSpec(
            num_scalar_prefetch=1,
            grid=(count,),
            in_specs=[pl.BlockSpec((rows, wide), lambda g, sc: (0, first + g))] + [vmem] * (4 + len(state)),
            out_specs=[vmem, vmem],
        ),
        out_shape=[
            pltpu.VMEM((groups, rows, wide), F32),
            pltpu.VMEM((groups, rows, HD), F32),
        ],
        input_output_aliases={6: 0, 7: 1} if state else {},
        compiler_params=params(16),
        cost_estimate=pl.CostEstimate(
            flops=4 * GQ * rows * rows * 2 * 2 * HD, bytes_accessed=4 * 2**20, transcendentals=0
        ),
        name="prefill_near",
    )(scalars, *map(in_vmem, (q, qf, own, sib, kf, *state)))


def prefill_far(scalars, q, qf, far, farsib, kf, state, after, earlier=None):
    rows, width = q.shape
    wide = STATE * HD
    early = earlier is None
    if early:
        columns = pl.BlockSpec((rows, wide), lambda g, sc: (0, jnp.minimum(g, jnp.maximum(sc[S_EARLY], 1) - 1)))
    else:
        columns = pl.BlockSpec((rows, wide), lambda g, sc: (0, jnp.maximum(g, sc[S_EARLY])))
    vmem = pl.BlockSpec(memory_space=pltpu.VMEM)
    hbm = pl.BlockSpec(memory_space=pl.ANY)
    extra = list(after) + ([] if early else [earlier])
    return pl.pallas_call(
        functools.partial(far_kernel, early=early),
        grid_spec=pltpu.PrefetchScalarGridSpec(
            num_scalar_prefetch=1,
            grid=(width // wide,),
            in_specs=[columns] + [vmem] * 6 + [hbm] * len(extra),
            out_specs=columns,
        ),
        out_shape=pltpu.HBM(q.shape, BF16),
        input_output_aliases={} if early else {7 + len(extra): 0},
        compiler_params=params(16),
        cost_estimate=pl.CostEstimate(
            flops=4 * GQ * rows * rows * 2 * 2 * HD, bytes_accessed=4 * 2**20, transcendentals=0
        ),
        name="prefill_far",
    )(scalars, *map(in_vmem, (q, qf, far, farsib, kf, *state)), *extra)


def context_kernel(sc, q_ref, ck_ref, cv_ref, own_ref, acc_ref, ml_ref, *, steps):
    srows = q_ref.shape[0]
    n = ck_ref.shape[0]
    block = 1024
    live = sc[S_LEN]
    lane = lax.broadcasted_iota(jnp.int32, (srows, HD), 1)
    q_mark = jnp.where(lane == 0, 1.0, 0.0).astype(BF16)
    zero = jnp.zeros((srows, HD), BF16)
    at_row = lax.broadcasted_iota(jnp.int32, (DEC * srows, srows), 0) % srows
    at_col = lax.broadcasted_iota(jnp.int32, (DEC * srows, srows), 1)
    own_mask = (at_row // steps == at_col // steps) & (at_col <= at_row)
    keys = {}
    for first in range(0, n, block):
        pos = lax.broadcasted_iota(jnp.int32, (block, HD), 0) + first
        col = lax.broadcasted_iota(jnp.int32, (block, HD), 1)
        mark = jnp.where((pos >= live) & (col == 0), HIDE, 0.0).astype(BF16)
        for kvh in (0, 1):
            r, c = slice(first, first + block), slice(kvh * HD, (kvh + 1) * HD)
            keys[kvh, first] = jnp.concatenate([ck_ref[r, c], mark], 1), with_ones(cv_ref[r, c])
    state = {}
    ml = [jnp.zeros((srows, HD), F32)]

    def query(g):
        cut = [q_ref[:, h * HD : (h + 1) * HD] for h in range(g * DEC, (g + 1) * DEC)]
        return jnp.concatenate([jnp.concatenate([q, q_mark], 1) for q in cut], 0)

    def score(item):
        g, first = item
        kvh = g * DEC // GQ
        if first < 0:
            s = scores(query(g), jnp.concatenate([own_ref[2 * kvh], zero], 1))
            return jnp.where(own_mask, s, HIDE)
        return scores(query(g), keys[kvh, first][0])

    def finish(item, s):
        g, first = item
        kvh = g * DEC // GQ
        v = with_ones(own_ref[2 * kvh + 1]) if first < 0 else keys[kvh, first][1]
        state[g] = settle(s, v, state.get(g))
        if first == n - block:
            m, acc = state[g]
            for i in range(DEC):
                at = g * DEC + i
                a = acc[i * srows : (i + 1) * srows]
                acc_ref[:, at * HD : (at + 1) * HD] = a[:, :HD]
                ml[0] = jnp.where(lane == at, m[i * srows : (i + 1) * srows], ml[0])
                ml[0] = jnp.where(lane == 2 * GQ + at, a[:, HD:], ml[0])

    groups = 2 * GQ // DEC
    in_turn([(g, first) for g in range(groups) for first in [-1, *range(0, n, block)]], score, finish)
    ml_ref[...] = ml[0]


def context_part(scalars, q, ck, cv, own, steps):
    srows, width = q.shape[0], q.shape[1] - HD
    return pl.pallas_call(
        functools.partial(context_kernel, steps=steps),
        grid_spec=pltpu.PrefetchScalarGridSpec(
            num_scalar_prefetch=1,
            grid=(1,),
            in_specs=[pl.BlockSpec(memory_space=pltpu.VMEM)] * 4,
            out_specs=[
                pl.BlockSpec((srows, width), lambda i, sc: (0, 0)),
                pl.BlockSpec((srows, HD), lambda i, sc: (0, 0)),
            ],
        ),
        out_shape=[
            jax.ShapeDtypeStruct((srows, width), F32),
            jax.ShapeDtypeStruct((srows, HD), F32),
        ],
        compiler_params=params(12),
        name="context_part",
    )(scalars, q, in_vmem(ck), in_vmem(cv), own)


DEC = 8


def pieces(x):
    hi = x.astype(BF16)
    rest = x - hi.astype(F32)
    mid = rest.astype(BF16)
    return hi, mid, (rest - mid.astype(F32)).astype(BF16)


def turn_kernel(sc, p0, p1, p2, p3, own, sib, far, fs, xp, xps, xm, xms, kfo, kfx, o0, o1, o2, o3, ks, vs, qs, os):
    head = pl.program_id(0)
    srows = p0.shape[0]
    rows = own.shape[1]
    keys = 4 * rows
    wide = GQ * HD
    for which, refs, first, kf in ((0, (own, sib, far, fs), S_OWN, kfo), (1, (xp, xps, xm, xms), S_XP, kfx)):
        wanted = [(sc[S_REL + j] != 0) & (sc[S_WHICH + j] == which) for j in range(4)]

        @pl.when(wanted[0] | wanted[1] | wanted[2] | wanted[3])
        def _():
            ks[which, :, HD:] = kf[...]
            vs[which, :, HD:] = jnp.ones((keys, HD), BF16)
            for i, ref in enumerate(refs):
                at = pl.multiple_of((sc[first] ^ i) * rows, rows)
                ks[which, pl.ds(at, rows), :HD] = ref[2 * head]
                vs[which, pl.ds(at, rows), :HD] = ref[2 * head + 1]

    for j, p in enumerate((p0, p1, p2, p3)):

        @pl.when(sc[S_REL + j] != 0)
        def _():
            qs[j, :, :wide] = p[:, pl.ds(pl.multiple_of(head * wide, wide), wide)]
            qs[j, :, wide:] = p[:, 2 * wide :]

    lane = lax.broadcasted_iota(jnp.int32, (srows, HD), 1)
    block = 1024

    def one(j, carry):
        @pl.when(sc[S_REL + j] != 0)
        def _():
            which = sc[S_WHICH + j]
            feat = qs[j, :, wide:]
            state = {}
            ml = [jnp.zeros((srows, HD), F32)] * 2

            def score(item):
                g, first = item
                cut = [qs[j, :, h * HD : (h + 1) * HD] for h in range(g * DEC, (g + 1) * DEC)]
                q = jnp.concatenate([jnp.concatenate([q, feat], 1) for q in cut], 0)
                return scores(q, ks[which, first : first + block, :])

            def finish(item, s):
                g, first = item
                state[g] = settle(s, vs[which, first : first + block, :], state.get(g))
                if first == keys - block:
                    m, acc = state[g]
                    for i in range(DEC):
                        h = g * DEC + i
                        r = slice(i * srows, (i + 1) * srows)
                        os[j, :, h * HD : (h + 1) * HD] = acc[r, :HD].astype(BF16)
                        for part in range(3):
                            ml[0] = jnp.where(lane == part * GQ + h, m[r], ml[0])
                            ml[1] = jnp.where(lane == (part + 3) * GQ + h, acc[r, HD:], ml[1])

            in_turn([(g, first) for first in range(0, keys, block) for g in range(GQ // DEC)], score, finish)
            m3, l3 = pieces(ml[0]), pieces(ml[1])
            ext = jnp.zeros((srows, HD), F32)
            for part in range(3):
                ext = jnp.where(lane // GQ == part, m3[part].astype(F32), ext)
                ext = jnp.where(lane // GQ == part + 3, l3[part].astype(F32), ext)
            os[j, :, wide:] = ext.astype(BF16)

        return carry

    lax.fori_loop(0, 4, one, 0)
    for j, o in enumerate((o0, o1, o2, o3)):
        o[...] = os[j]


def turn_part(scalars, packets, kvs, kf_own, kf_other, after):
    srows = packets[0].shape[0]
    rows = kvs[0].shape[1]
    wide = GQ * HD + HD

    def kernel(*refs):
        turn_kernel(*refs[:15], *refs[15 + len(after) :])

    return pl.pallas_call(
        kernel,
        grid_spec=pltpu.PrefetchScalarGridSpec(
            num_scalar_prefetch=1,
            grid=(2,),
            in_specs=[pl.BlockSpec(memory_space=pltpu.VMEM)] * 14
            + [pl.BlockSpec(memory_space=pl.ANY)] * len(after),
            out_specs=[pl.BlockSpec((srows, wide), lambda g, sc: (0, g))] * 4,
            scratch_shapes=[
                pltpu.VMEM((2, 4 * rows, 2 * HD), BF16),
                pltpu.VMEM((2, 4 * rows, 2 * HD), BF16),
                pltpu.VMEM((4, srows, wide), BF16),
                pltpu.VMEM((4, srows, wide), BF16),
            ],
        ),
        out_shape=[jax.ShapeDtypeStruct((srows, 2 * wide), BF16)] * 4,
        compiler_params=params(20),
        cost_estimate=pl.CostEstimate(
            flops=4 * 4 * srows * GQ * 4 * rows * 2 * HD, bytes_accessed=4 * 2**20, transcendentals=0
        ),
        name="turn_part",
    )(scalars, *map(in_vmem, packets), *map(in_vmem, kvs), in_vmem(kf_own), in_vmem(kf_other), *after)


def merge_kernel(sc, acc_ref, ml_ref, *refs):
    o_ref, wide = refs[-2:]
    sel = sc[S_SEL]
    groups, steps, _ = o_ref.shape
    ml = ml_ref[...]
    width = GQ * HD
    for kvh in range(2):
        first = kvh * (width + HD)

        def pick(cols):
            cols = slice(first + cols.start, first + cols.stop)
            x = refs[0][:, cols]
            for j in (1, 2, 3):
                x = jnp.where(sel == j, refs[j][:, cols], x)
            return x.astype(F32)

        ext = pick(slice(width, width + HD))
        whole = [
            ext[:, i * GQ : (i + 1) * GQ]
            + ext[:, (i + 1) * GQ : (i + 2) * GQ]
            + ext[:, (i + 2) * GQ : (i + 3) * GQ]
            for i in (0, 3)
        ]
        m2, l2 = whole
        m1 = ml[:, kvh * GQ : (kvh + 1) * GQ]
        l1 = ml[:, (2 + kvh) * GQ : (3 + kvh) * GQ]
        m = jnp.maximum(m1, m2)
        w1, w2 = jnp.exp2((m1 - m) * SCALE), jnp.exp2((m2 - m) * SCALE)
        total = l1 * w1 + l2 * w2
        w1, w2 = w1 / total, w2 / total
        for h in range(GQ):
            at = kvh * GQ + h
            a1 = acc_ref[:, at * HD : (at + 1) * HD]
            a2 = pick(slice(h * HD, (h + 1) * HD))
            wide[:, at * HD : (at + 1) * HD] = a1 * w1[:, h : h + 1] + a2 * w2[:, h : h + 1]
    for r in range(groups):
        o_ref[r] = wide[r * steps : (r + 1) * steps, :].astype(BF16)


def merge(scalars, acc, ml, back, steps):
    args = (acc, ml, *back)
    shape = (acc.shape[0] // steps, steps, acc.shape[1])
    return pl.pallas_call(
        merge_kernel,
        grid_spec=pltpu.PrefetchScalarGridSpec(
            num_scalar_prefetch=1,
            grid=(1,),
            in_specs=[pl.BlockSpec(a.shape, lambda i, sc: (0, 0)) for a in args],
            out_specs=pl.BlockSpec(shape, lambda i, sc: (0, 0, 0)),
            scratch_shapes=[pltpu.VMEM(acc.shape, F32)],
        ),
        out_shape=jax.ShapeDtypeStruct(shape, BF16),
        compiler_params=params(8),
        name="merge",
    )(scalars, *args)


ROW = ("xlo", "xhi")


def row_index(x):
    return x % 2 * 2 + x // 2


def from_x(a, shift):
    return lax.ppermute(a, ROW, [(row_index((x + shift) % 4), row_index(x)) for x in range(4)])


def from_y(a, shift):
    return lax.ppermute(a, "y", [((y + shift) % 4, y) for y in range(4)])


def from_core(a):
    return lax.ppermute(a, "core", [(0, 1), (1, 0)])


def body(
    turn_hidden,
    w_key,
    w_value,
    turn_queries,
    turn_speaker,
    speaker_mask,
    shard_block,
    context_keys,
    context_values,
    context_length,
    decode_home,
    step_hidden,
    step_queries,
    row_speaker,
):
    steps = step_hidden.shape[1]
    tie = lax.optimization_barrier
    own, step_kv = project(turn_hidden, step_hidden, w_key, w_value)
    far, sib, xp, xm = from_x(own, 2), from_core(own), from_x(own, 1), from_x(own, 3)
    sib, row_speaker, shard_block = tie((sib, row_speaker, shard_block))
    packet = make_packet(row_speaker, step_queries)
    packets = [packet, from_y(packet, 1), None, from_y(packet, 3)]
    scalars, qf, kf_own, kf_other = prepare(
        shard_block, decode_home, context_length, speaker_mask, turn_speaker
    )
    near = list(prefill_near(scalars, turn_queries, qf, own, sib, kf_own, 0, 2))
    packets[0], packets[1], packets[3], near[0] = tie((packets[0], packets[1], packets[3], near[0]))
    packets[2] = from_y(packets[0], 2)
    near = list(prefill_near(scalars, turn_queries, qf, own, sib, kf_own, 2, 2, near))
    packets[0], packets[2], near[0] = tie((packets[0], packets[2], near[0]))
    ctx = context_part(scalars, packets[0], context_keys, context_values, step_kv, steps)
    far, xp, xm, _ = tie((far, xp, xm, ctx[1]))
    farsib, xps, xms = from_core(far), from_core(xp), from_core(xm)
    early = prefill_far(scalars, turn_queries, qf, far, farsib, kf_own, near, ())
    early, kf_other = tie((early, kf_other))
    moved = (own, sib, far, farsib, xp, xps, xm, xms)
    parts = turn_part(scalars, packets, moved, kf_own, kf_other, ())
    back = [parts[0]] + [from_y(parts[j], -j) for j in (1, 2, 3)]
    turn_attention = prefill_far(
        scalars, turn_queries, qf, far, farsib, kf_own, near, (parts[0],), early
    )
    step_attention = merge(scalars, *ctx, back, steps)
    return turn_attention, step_attention


def solution(mesh):
    heads = mesh.shape["head"]
    fine = Mesh(mesh.devices.reshape(2, 4, 2, 2, heads), ("xlo", "y", "xhi", "core", "head"))
    split = ("xlo", "y", "xhi", "core")
    return jax.shard_map(
        body,
        mesh=fine,
        in_specs=(
            P(split, None),
            P(None, "head"),
            P(None, "head"),
            P(split, "head"),
            P(),
            P(),
            P(),
            P(split, "head"),
            P(split, "head"),
            P(),
            P(),
            P(split, None, None),
            P(split, None, "head"),
            P(split),
        ),
        out_specs=(P(split, "head"), P(split, None, "head")),
        check_vma=False,
    )
```

```python
import functools
import math

import jax
import jax.numpy as jnp
from jax import lax
from jax.experimental import pallas as pl
from jax.experimental.pallas import tpu as pltpu
from jax.sharding import Mesh
from jax.sharding import PartitionSpec as P

HQ = 64
KVH = 8
HD = 128
SPK = 4
GQ = HQ // KVH

HIDE = -1e30
SCALE = math.log2(math.e) / math.sqrt(HD)
NT = (((1,), (1,)), ((), ()))
F32 = jnp.float32
BF16 = jnp.bfloat16

S_OWN, S_SIB, S_FAR, S_FARSIB, S_REL, S_WHICH, S_SEL, S_LEN, S_XP, S_EARLY = 0, 1, 2, 3, 4, 8, 12, 13, 14, 15


def params(mib):
    return pltpu.CompilerParams(vmem_limit_bytes=mib * 2**20)


def in_vmem(x):
    return pltpu.with_memory_space_constraint(x, pltpu.VMEM)


def in_hbm(x):
    return pltpu.with_memory_space_constraint(x, pltpu.HBM)


def with_ones(v):
    return jnp.concatenate([v, jnp.ones(v.shape, BF16)], 1)


def marks(table, speakers):
    row = lax.broadcasted_iota(jnp.int32, (8, HD), 0)
    hot = jnp.where(speakers == row, 1.0, 0.0).astype(BF16)
    out = lax.dot_general(hot, table, (((0,), (0,)), ((), ())), preferred_element_type=F32)
    return out.astype(BF16)


def prep_kernel(blocks, homes, lengths, mask, spk_ref, sc, qf_ref, kfo_ref, kfx_ref):
    xlo, y, xhi, core = (lax.axis_index(a) for a in ("xlo", "y", "xhi", "core"))
    own_at = xhi * 2 + core
    dialog = xlo * 4 + y
    here = blocks[dialog * 4 + own_at]
    sc[S_OWN] = own_at
    for i, at in ((1, S_SIB), (2, S_FAR), (3, S_FARSIB)):
        sc[at] = jnp.where(blocks[dialog * 4 + (own_at ^ i)] < here, 1, 0)
    for j in range(4):
        home = homes[xlo * 16 + (y + j) % 4 * 4 + own_at]
        sc[S_REL + j] = jnp.where(home % 4 == y, 1, 0)
        sc[S_WHICH + j] = jnp.where(home // 4 != xlo, 1, 0)
    home = homes[xlo * 16 + y * 4 + own_at]
    sc[S_SEL] = (y - home % 4 + 4) % 4
    sc[S_LEN] = lengths[home]
    sc[S_XP] = (xhi ^ xlo) * 2 + core

    most = jnp.int32(0)
    mine = jnp.int32(0)
    for c in range(8):
        rows_of = [homes[c // 4 * 16 + at * 4 + c % 4] % 4 for at in range(4)]
        for at in range(4):
            count = sum(jnp.where(r == at, 1, 0) for r in rows_of)
            most = jnp.maximum(most, count)
            mine = jnp.where((c == xlo * 4 + own_at) & (y == at), count, mine)
    sc[S_EARLY] = jnp.minimum((most - mine) * 2 // 3, 3)

    row = lax.broadcasted_iota(jnp.int32, (8, HD), 0)
    lane = lax.broadcasted_iota(jnp.int32, (8, HD), 1)
    for d, out in ((dialog, kfo_ref), ((1 - xlo) * 4 + y, kfx_ref)):
        table = jnp.zeros((8, HD), F32)
        for a in range(SPK):
            for b in range(SPK):
                add = jnp.where(mask[a, b, d] == 1, 0.0, HIDE)
                table = jnp.where((row == b) & (lane == a), add, table)
        table = table.astype(BF16)
        for i in range(16):
            out[i * HD : (i + 1) * HD, :] = marks(table, spk_ref[d * 2 + i // 8, i % 8 : i % 8 + 1, :])
    eye = jnp.where((row == lane) & (row < SPK), 1.0, 0.0).astype(BF16)
    for i in range(4):
        at = (dialog * 4 + own_at) * 4 + i
        qf_ref[i * HD : (i + 1) * HD, :] = marks(eye, spk_ref[at // 8, pl.ds(at % 8, 1), :])


def prepare(blocks, homes, lengths, mask, spk):
    rows = spk.size // 32
    smem = pl.BlockSpec(memory_space=pltpu.SMEM)
    vmem = pl.BlockSpec(memory_space=pltpu.VMEM)
    return pl.pallas_call(
        prep_kernel,
        in_specs=[smem] * 4 + [vmem],
        out_specs=[smem] + [vmem] * 3,
        out_shape=[
            jax.ShapeDtypeStruct((16,), jnp.int32),
            pltpu.VMEM((rows, HD), BF16),
            pltpu.VMEM((4 * rows, HD), BF16),
            pltpu.VMEM((4 * rows, HD), BF16),
        ],
        compiler_params=params(6),
        name="prepare",
    )(blocks, homes, lengths, mask.transpose(1, 2, 0), spk.reshape(-1, 8, HD))


def packet_kernel(row_spk, q_ref, pk_ref, wide):
    groups, steps, width = q_ref.shape
    srows = groups * steps
    for r in range(groups):
        wide[r * steps : (r + 1) * steps, :] = q_ref[r].astype(F32)
    pk_ref[:, :width] = wide[...].astype(BF16)
    row = lax.broadcasted_iota(jnp.int32, (srows, HD), 0)
    lane = lax.broadcasted_iota(jnp.int32, (srows, HD), 1)
    speaker = jnp.zeros((srows, HD), jnp.int32)
    for r in range(groups):
        speaker = jnp.where(row // steps == r, row_spk[r], speaker)
    pk_ref[:, width:] = jnp.where(lane == speaker, 1.0, 0.0).astype(BF16)


def make_packet(row_spk, queries):
    groups, steps, width = queries.shape
    return pl.pallas_call(
        packet_kernel,
        in_specs=[pl.BlockSpec(memory_space=pltpu.SMEM), pl.BlockSpec(memory_space=pltpu.VMEM)],
        out_specs=pl.BlockSpec(memory_space=pltpu.VMEM),
        out_shape=jax.ShapeDtypeStruct((groups * steps, width + HD), BF16),
        scratch_shapes=[pltpu.VMEM((groups * steps, width), F32)],
        compiler_params=params(4),
        name="packet",
    )(row_spk, queries)


def project_kernel(x_hbm, s_hbm, wk_hbm, wv_hbm, kv_ref, skv_ref, xb, sb, wkb, wvb, wide, sem, *, chunk):
    groups, steps, depth = s_hbm.shape
    copies = []
    for i in range(depth // chunk):
        c = pl.ds(i * chunk, chunk)
        pairs = [
            (x_hbm.at[:, c], xb.at[:, c]),
            (wk_hbm.at[c, :], wkb.at[c, :]),
            (wv_hbm.at[c, :], wvb.at[c, :]),
        ]
        copies.append([pltpu.make_async_copy(a, b, sem.at[i, n]) for n, (a, b) in enumerate(pairs)])
        for copy in copies[-1]:
            copy.start()
        if i == 0:
            step_copy = pltpu.make_async_copy(s_hbm, sb, sem.at[0, 3])
            step_copy.start()
    acc = None
    for i, these in enumerate(copies):
        for copy in these:
            copy.wait()
        c = slice(i * chunk, (i + 1) * chunk)
        w = jnp.concatenate([wkb[c, :], wvb[c, :]], 1)
        if i == 0:
            step_copy.wait()
        for r in range(groups):
            wide[r * steps : (r + 1) * steps, c] = sb[r, :, c].astype(F32)
        both = jnp.concatenate([xb[:, c], wide[:, c].astype(BF16)], 0)
        part = jnp.dot(both, w, preferred_element_type=F32)
        acc = part if acc is None else acc + part
    rows = xb.shape[0]
    for at, first in enumerate((0, 2 * HD, HD, 3 * HD)):
        kv_ref[at] = acc[:rows, first : first + HD].astype(BF16)
        skv_ref[at] = acc[rows:, first : first + HD].astype(BF16)


def project(x, steps, w_key, w_value):
    rows, depth = x.shape
    srows = steps.shape[0] * steps.shape[1]
    chunk = 1024
    hbm = pl.BlockSpec(memory_space=pl.ANY)
    vmem = pl.BlockSpec(memory_space=pltpu.VMEM)
    return pl.pallas_call(
        functools.partial(project_kernel, chunk=chunk),
        in_specs=[hbm] * 4,
        out_specs=[vmem] * 2,
        out_shape=[
            jax.ShapeDtypeStruct((4, rows, HD), BF16),
            jax.ShapeDtypeStruct((4, srows, HD), BF16),
        ],
        scratch_shapes=[
            pltpu.VMEM(x.shape, BF16),
            pltpu.VMEM(steps.shape, BF16),
            pltpu.VMEM(w_key.shape, BF16),
            pltpu.VMEM(w_value.shape, BF16),
            pltpu.VMEM((srows, depth), F32),
            pltpu.SemaphoreType.DMA((depth // chunk, 4)),
        ],
        compiler_params=params(28),
        cost_estimate=pl.CostEstimate(
            flops=2 * (rows + srows) * depth * 4 * HD,
            bytes_accessed=2 * depth * (rows + srows + 4 * HD),
            transcendentals=0,
        ),
        name="project",
    )(*map(in_hbm, (x, steps, w_key, w_value)))


def scores(q, k):
    return lax.dot_general(q, k, NT, preferred_element_type=F32)


def settle(s, v, state=None):
    m = jnp.max(s, axis=1, keepdims=True)
    if state is not None:
        m = jnp.maximum(m, state[0])
    p = jnp.exp2((s - m) * SCALE).astype(BF16)
    acc = jnp.dot(p, v, preferred_element_type=F32)
    if state is not None:
        acc = acc + state[1] * jnp.exp2((state[0] - m) * SCALE)
    return m, acc


def in_turn(items, score, finish):
    ahead = score(items[0])
    for i, item in enumerate(items):
        now = ahead
        if i + 1 < len(items):
            ahead = score(items[i + 1])
        finish(item, now)


def keys_of(k, kf):
    return jnp.concatenate([k, kf], 1)


def shown(marks_of_keys, flag):
    return marks_of_keys + jnp.where(flag != 0, 0.0, HIDE).astype(BF16)


def query_of(q_ref, qf_ref, h, first, count):
    q = q_ref[first : first + count, h * HD : (h + 1) * HD]
    return jnp.concatenate([q, qf_ref[first : first + count, :]], 1)


def near_kernel(sc, q_ref, qf_ref, own_ref, sib_ref, kf_ref, *refs, first):
    acc_ref, ml_ref = refs[-2:]
    group = pl.program_id(0) + first
    kvh = group * STATE // GQ
    rows = q_ref.shape[0]
    half = rows // 2
    own = pl.multiple_of(sc[S_OWN] * rows, rows)
    sib = pl.multiple_of((sc[S_OWN] ^ 1) * rows, rows)
    lane = lax.broadcasted_iota(jnp.int32, (half, HD), 1)

    k = keys_of(own_ref[2 * kvh], kf_ref[pl.ds(own, rows), :])
    v = with_ones(own_ref[2 * kvh + 1])
    late = keys_of(sib_ref[2 * kvh], shown(kf_ref[pl.ds(sib, rows), :], sc[S_SIB]))
    late_v = with_ones(sib_ref[2 * kvh + 1])
    ks = [jnp.concatenate([k[:half], late], 0), jnp.concatenate([k, late], 0)]
    vs = [jnp.concatenate([v[:half], late_v], 0), jnp.concatenate([v, late_v], 0)]
    ml = [jnp.zeros((half, HD), F32)] * 2

    def score(item):
        h, part = item
        q = [query_of(q_ref, qf_ref, h + i, part * half, half) for i in range(HN)]
        s = scores(jnp.concatenate(q, 0), ks[part])
        own_cols = (part + 1) * half
        at_row = lax.broadcasted_iota(jnp.int32, (HN * half, half), 0) % half
        at_col = lax.broadcasted_iota(jnp.int32, (HN * half, half), 1)
        corner = jnp.where(at_col <= at_row, s[:, own_cols - half : own_cols], HIDE)
        cut = [s[:, : own_cols - half]] * (part > 0) + [corner, s[:, own_cols:]]
        return jnp.concatenate(cut, 1)

    def finish(item, s):
        h0, part = item
        ms, accs = settle(s, vs[part])
        for i in range(HN):
            h = h0 + i
            m, acc = ms[i * half : (i + 1) * half], accs[i * half : (i + 1) * half]
            acc_ref[group, part * half : (part + 1) * half, h * HD : (h + 1) * HD] = acc[:, :HD]
            ml[part] = jnp.where(lane == h, m, jnp.where(lane == STATE + h, acc[:, HD:], ml[part]))

    in_turn([(h, part) for h in range(0, STATE, HN) for part in (0, 1)], score, finish)
    for part in (0, 1):
        ml_ref[group, part * half : (part + 1) * half, :] = ml[part]


def far_kernel(sc, q_ref, qf_ref, far_ref, fs_ref, kf_ref, acc_ref, ml_ref, *rest, early):
    group = pl.program_id(0)
    kvh = group * STATE // GQ
    o_ref = rest[-1]
    rows = q_ref.shape[0]
    half = rows // 2
    far = pl.multiple_of((sc[S_OWN] ^ 2) * rows, rows)
    farsib = pl.multiple_of((sc[S_OWN] ^ 3) * rows, rows)

    def run(seen):
        if seen:
            blocks = [(far_ref, far, S_FAR), (fs_ref, farsib, S_FARSIB)]
            k = [keys_of(x[2 * kvh], shown(kf_ref[pl.ds(at, rows), :], sc[flag])) for x, at, flag in blocks]
            k = jnp.concatenate(k, 0)
            v = jnp.concatenate([with_ones(x[2 * kvh + 1]) for x, _, _ in blocks], 0)

        def score(item):
            q = [query_of(q_ref, qf_ref, item + i, 0, rows) for i in range(HF)]
            return scores(jnp.concatenate(q, 0), k) if seen else None

        def finish(item, s):
            state = []
            for h in range(item, item + HF):
                ml = ml_ref[group]
                l = jnp.broadcast_to(ml[:, STATE + h : STATE + h + 1], (rows, HD))
                acc = jnp.concatenate([acc_ref[group, :, h * HD : (h + 1) * HD], l], 1)
                state.append((ml[:, h : h + 1], acc))
            m = jnp.concatenate([x[0] for x in state], 0)
            acc = jnp.concatenate([x[1] for x in state], 0)
            if seen:
                acc = settle(s, v, (m, acc))[1]
            out = (acc[:, :HD] / acc[:, HD:]).astype(BF16)
            for i in range(HF):
                o_ref[:, (item + i) * HD : (item + i + 1) * HD] = out[i * rows : (i + 1) * rows]

        in_turn(list(range(0, STATE, HF)), score, finish)

    mine = (group < sc[S_EARLY]) == early
    seen = (sc[S_FAR] != 0) | (sc[S_FARSIB] != 0)
    pl.when(mine & seen)(functools.partial(run, True))
    pl.when(mine & jnp.logical_not(seen))(functools.partial(run, False))


STATE = 4
HN = 2
HF = 1


def prefill_near(scalars, q, qf, own, sib, kf, first, count, state=()):
    rows, width = q.shape
    wide = STATE * HD
    groups = width // wide
    vmem = pl.BlockSpec(memory_space=pltpu.VMEM)
    return pl.pallas_call(
        functools.partial(near_kernel, first=first),
        grid_spec=pltpu.PrefetchScalarGridSpec(
            num_scalar_prefetch=1,
            grid=(count,),
            in_specs=[pl.BlockSpec((rows, wide), lambda g, sc: (0, first + g))] + [vmem] * (4 + len(state)),
            out_specs=[vmem, vmem],
        ),
        out_shape=[
            pltpu.VMEM((groups, rows, wide), F32),
            pltpu.VMEM((groups, rows, HD), F32),
        ],
        input_output_aliases={6: 0, 7: 1} if state else {},
        compiler_params=params(16),
        cost_estimate=pl.CostEstimate(
            flops=4 * GQ * rows * rows * 2 * 2 * HD, bytes_accessed=4 * 2**20, transcendentals=0
        ),
        name="prefill_near",
    )(scalars, *map(in_vmem, (q, qf, own, sib, kf, *state)))


def prefill_far(scalars, q, qf, far, farsib, kf, state, after, earlier=None):
    rows, width = q.shape
    wide = STATE * HD
    early = earlier is None
    if early:
        columns = pl.BlockSpec((rows, wide), lambda g, sc: (0, jnp.minimum(g, jnp.maximum(sc[S_EARLY], 1) - 1)))
    else:
        columns = pl.BlockSpec((rows, wide), lambda g, sc: (0, jnp.maximum(g, sc[S_EARLY])))
    vmem = pl.BlockSpec(memory_space=pltpu.VMEM)
    hbm = pl.BlockSpec(memory_space=pl.ANY)
    extra = list(after) + ([] if early else [earlier])
    return pl.pallas_call(
        functools.partial(far_kernel, early=early),
        grid_spec=pltpu.PrefetchScalarGridSpec(
            num_scalar_prefetch=1,
            grid=(width // wide,),
            in_specs=[columns] + [vmem] * 6 + [hbm] * len(extra),
            out_specs=columns,
        ),
        out_shape=pltpu.HBM(q.shape, BF16),
        input_output_aliases={} if early else {7 + len(extra): 0},
        compiler_params=params(16),
        cost_estimate=pl.CostEstimate(
            flops=4 * GQ * rows * rows * 2 * 2 * HD, bytes_accessed=4 * 2**20, transcendentals=0
        ),
        name="prefill_far",
    )(scalars, *map(in_vmem, (q, qf, far, farsib, kf, *state)), *extra)


def context_kernel(sc, q_ref, ck_ref, cv_ref, own_ref, acc_ref, ml_ref, *, steps):
    srows = q_ref.shape[0]
    n = ck_ref.shape[0]
    block = 1024
    live = sc[S_LEN]
    lane = lax.broadcasted_iota(jnp.int32, (srows, HD), 1)
    q_mark = jnp.where(lane == 0, 1.0, 0.0).astype(BF16)
    zero = jnp.zeros((srows, HD), BF16)
    at_row = lax.broadcasted_iota(jnp.int32, (DEC * srows, srows), 0) % srows
    at_col = lax.broadcasted_iota(jnp.int32, (DEC * srows, srows), 1)
    own_mask = (at_row // steps == at_col // steps) & (at_col <= at_row)
    keys = {}
    for first in range(0, n, block):
        pos = lax.broadcasted_iota(jnp.int32, (block, HD), 0) + first
        col = lax.broadcasted_iota(jnp.int32, (block, HD), 1)
        mark = jnp.where((pos >= live) & (col == 0), HIDE, 0.0).astype(BF16)
        for kvh in (0, 1):
            r, c = slice(first, first + block), slice(kvh * HD, (kvh + 1) * HD)
            keys[kvh, first] = jnp.concatenate([ck_ref[r, c], mark], 1), with_ones(cv_ref[r, c])
    state = {}
    ml = [jnp.zeros((srows, HD), F32)]

    def query(g):
        cut = [q_ref[:, h * HD : (h + 1) * HD] for h in range(g * DEC, (g + 1) * DEC)]
        return jnp.concatenate([jnp.concatenate([q, q_mark], 1) for q in cut], 0)

    def score(item):
        g, first = item
        kvh = g * DEC // GQ
        if first < 0:
            s = scores(query(g), jnp.concatenate([own_ref[2 * kvh], zero], 1))
            return jnp.where(own_mask, s, HIDE)
        return scores(query(g), keys[kvh, first][0])

    def finish(item, s):
        g, first = item
        kvh = g * DEC // GQ
        v = with_ones(own_ref[2 * kvh + 1]) if first < 0 else keys[kvh, first][1]
        state[g] = settle(s, v, state.get(g))
        if first == n - block:
            m, acc = state[g]
            for i in range(DEC):
                at = g * DEC + i
                a = acc[i * srows : (i + 1) * srows]
                acc_ref[:, at * HD : (at + 1) * HD] = a[:, :HD]
                ml[0] = jnp.where(lane == at, m[i * srows : (i + 1) * srows], ml[0])
                ml[0] = jnp.where(lane == 2 * GQ + at, a[:, HD:], ml[0])

    groups = 2 * GQ // DEC
    in_turn([(g, first) for g in range(groups) for first in [-1, *range(0, n, block)]], score, finish)
    ml_ref[...] = ml[0]


def context_part(scalars, q, ck, cv, own, steps):
    srows, width = q.shape[0], q.shape[1] - HD
    return pl.pallas_call(
        functools.partial(context_kernel, steps=steps),
        grid_spec=pltpu.PrefetchScalarGridSpec(
            num_scalar_prefetch=1,
            grid=(1,),
            in_specs=[pl.BlockSpec(memory_space=pltpu.VMEM)] * 4,
            out_specs=[
                pl.BlockSpec((srows, width), lambda i, sc: (0, 0)),
                pl.BlockSpec((srows, HD), lambda i, sc: (0, 0)),
            ],
        ),
        out_shape=[
            jax.ShapeDtypeStruct((srows, width), F32),
            jax.ShapeDtypeStruct((srows, HD), F32),
        ],
        compiler_params=params(12),
        name="context_part",
    )(scalars, q, in_vmem(ck), in_vmem(cv), own)


DEC = 8


def pieces(x):
    hi = x.astype(BF16)
    rest = x - hi.astype(F32)
    mid = rest.astype(BF16)
    return hi, mid, (rest - mid.astype(F32)).astype(BF16)


def turn_kernel(sc, p0, p1, p2, p3, own, sib, far, fs, xp, xps, xm, xms, kfo, kfx, o0, o1, o2, o3, ks, vs, qs, os):
    head = pl.program_id(0)
    srows = p0.shape[0]
    rows = own.shape[1]
    keys = 4 * rows
    wide = GQ * HD
    for which, refs, first, kf in ((0, (own, sib, far, fs), S_OWN, kfo), (1, (xp, xps, xm, xms), S_XP, kfx)):
        wanted = [(sc[S_REL + j] != 0) & (sc[S_WHICH + j] == which) for j in range(4)]

        @pl.when(wanted[0] | wanted[1] | wanted[2] | wanted[3])
        def _():
            ks[which, :, HD:] = kf[...]
            vs[which, :, HD:] = jnp.ones((keys, HD), BF16)
            for i, ref in enumerate(refs):
                at = pl.multiple_of((sc[first] ^ i) * rows, rows)
                ks[which, pl.ds(at, rows), :HD] = ref[2 * head]
                vs[which, pl.ds(at, rows), :HD] = ref[2 * head + 1]

    for j, p in enumerate((p0, p1, p2, p3)):

        @pl.when(sc[S_REL + j] != 0)
        def _():
            qs[j, :, :wide] = p[:, pl.ds(pl.multiple_of(head * wide, wide), wide)]
            qs[j, :, wide:] = p[:, 2 * wide :]

    lane = lax.broadcasted_iota(jnp.int32, (srows, HD), 1)
    block = 1024

    def one(j, carry):
        @pl.when(sc[S_REL + j] != 0)
        def _():
            which = sc[S_WHICH + j]
            feat = qs[j, :, wide:]
            state = {}
            ml = [jnp.zeros((srows, HD), F32)] * 2

            def score(item):
                g, first = item
                cut = [qs[j, :, h * HD : (h + 1) * HD] for h in range(g * DEC, (g + 1) * DEC)]
                q = jnp.concatenate([jnp.concatenate([q, feat], 1) for q in cut], 0)
                return scores(q, ks[which, first : first + block, :])

            def finish(item, s):
                g, first = item
                state[g] = settle(s, vs[which, first : first + block, :], state.get(g))
                if first == keys - block:
                    m, acc = state[g]
                    for i in range(DEC):
                        h = g * DEC + i
                        r = slice(i * srows, (i + 1) * srows)
                        os[j, :, h * HD : (h + 1) * HD] = acc[r, :HD].astype(BF16)
                        for part in range(3):
                            ml[0] = jnp.where(lane == part * GQ + h, m[r], ml[0])
                            ml[1] = jnp.where(lane == (part + 3) * GQ + h, acc[r, HD:], ml[1])

            in_turn([(g, first) for first in range(0, keys, block) for g in range(GQ // DEC)], score, finish)
            m3, l3 = pieces(ml[0]), pieces(ml[1])
            ext = jnp.zeros((srows, HD), F32)
            for part in range(3):
                ext = jnp.where(lane // GQ == part, m3[part].astype(F32), ext)
                ext = jnp.where(lane // GQ == part + 3, l3[part].astype(F32), ext)
            os[j, :, wide:] = ext.astype(BF16)

        return carry

    lax.fori_loop(0, 4, one, 0)
    for j, o in enumerate((o0, o1, o2, o3)):
        o[...] = os[j]


def turn_part(scalars, packets, kvs, kf_own, kf_other, after):
    srows = packets[0].shape[0]
    rows = kvs[0].shape[1]
    wide = GQ * HD + HD

    def kernel(*refs):
        turn_kernel(*refs[:15], *refs[15 + len(after) :])

    return pl.pallas_call(
        kernel,
        grid_spec=pltpu.PrefetchScalarGridSpec(
            num_scalar_prefetch=1,
            grid=(2,),
            in_specs=[pl.BlockSpec(memory_space=pltpu.VMEM)] * 14
            + [pl.BlockSpec(memory_space=pl.ANY)] * len(after),
            out_specs=[pl.BlockSpec((srows, wide), lambda g, sc: (0, g))] * 4,
            scratch_shapes=[
                pltpu.VMEM((2, 4 * rows, 2 * HD), BF16),
                pltpu.VMEM((2, 4 * rows, 2 * HD), BF16),
                pltpu.VMEM((4, srows, wide), BF16),
                pltpu.VMEM((4, srows, wide), BF16),
            ],
        ),
        out_shape=[jax.ShapeDtypeStruct((srows, 2 * wide), BF16)] * 4,
        compiler_params=params(20),
        cost_estimate=pl.CostEstimate(
            flops=4 * 4 * srows * GQ * 4 * rows * 2 * HD, bytes_accessed=4 * 2**20, transcendentals=0
        ),
        name="turn_part",
    )(scalars, *map(in_vmem, packets), *map(in_vmem, kvs), in_vmem(kf_own), in_vmem(kf_other), *after)


def merge_kernel(sc, acc_ref, ml_ref, *refs):
    o_ref, wide = refs[-2:]
    sel = sc[S_SEL]
    groups, steps, _ = o_ref.shape
    ml = ml_ref[...]
    width = GQ * HD
    for kvh in range(2):
        first = kvh * (width + HD)

        def pick(cols):
            cols = slice(first + cols.start, first + cols.stop)
            x = refs[0][:, cols]
            for j in (1, 2, 3):
                x = jnp.where(sel == j, refs[j][:, cols], x)
            return x.astype(F32)

        ext = pick(slice(width, width + HD))
        whole = [
            ext[:, i * GQ : (i + 1) * GQ]
            + ext[:, (i + 1) * GQ : (i + 2) * GQ]
            + ext[:, (i + 2) * GQ : (i + 3) * GQ]
            for i in (0, 3)
        ]
        m2, l2 = whole
        m1 = ml[:, kvh * GQ : (kvh + 1) * GQ]
        l1 = ml[:, (2 + kvh) * GQ : (3 + kvh) * GQ]
        m = jnp.maximum(m1, m2)
        w1, w2 = jnp.exp2((m1 - m) * SCALE), jnp.exp2((m2 - m) * SCALE)
        total = l1 * w1 + l2 * w2
        w1, w2 = w1 / total, w2 / total
        for h in range(GQ):
            at = kvh * GQ + h
            a1 = acc_ref[:, at * HD : (at + 1) * HD]
            a2 = pick(slice(h * HD, (h + 1) * HD))
            wide[:, at * HD : (at + 1) * HD] = a1 * w1[:, h : h + 1] + a2 * w2[:, h : h + 1]
    for r in range(groups):
        o_ref[r] = wide[r * steps : (r + 1) * steps, :].astype(BF16)


def merge(scalars, acc, ml, back, steps):
    args = (acc, ml, *back)
    shape = (acc.shape[0] // steps, steps, acc.shape[1])
    return pl.pallas_call(
        merge_kernel,
        grid_spec=pltpu.PrefetchScalarGridSpec(
            num_scalar_prefetch=1,
            grid=(1,),
            in_specs=[pl.BlockSpec(a.shape, lambda i, sc: (0, 0)) for a in args],
            out_specs=pl.BlockSpec(shape, lambda i, sc: (0, 0, 0)),
            scratch_shapes=[pltpu.VMEM(acc.shape, F32)],
        ),
        out_shape=jax.ShapeDtypeStruct(shape, BF16),
        compiler_params=params(8),
        name="merge",
    )(scalars, *args)


ROW = ("xlo", "xhi")


def row_index(x):
    return x % 2 * 2 + x // 2


def from_x(a, shift):
    return lax.ppermute(a, ROW, [(row_index((x + shift) % 4), row_index(x)) for x in range(4)])


def from_y(a, shift):
    return lax.ppermute(a, "y", [((y + shift) % 4, y) for y in range(4)])


def from_core(a):
    return lax.ppermute(a, "core", [(0, 1), (1, 0)])


def body(
    turn_hidden,
    w_key,
    w_value,
    turn_queries,
    turn_speaker,
    speaker_mask,
    shard_block,
    context_keys,
    context_values,
    context_length,
    decode_home,
    step_hidden,
    step_queries,
    row_speaker,
):
    steps = step_hidden.shape[1]
    tie = lax.optimization_barrier
    own, step_kv = project(turn_hidden, step_hidden, w_key, w_value)
    far, sib, xp, xm = from_x(own, 2), from_core(own), from_x(own, 1), from_x(own, 3)
    sib, row_speaker, shard_block = tie((sib, row_speaker, shard_block))
    packet = make_packet(row_speaker, step_queries)
    packets = [packet, from_y(packet, 1), None, from_y(packet, 3)]
    scalars, qf, kf_own, kf_other = prepare(
        shard_block, decode_home, context_length, speaker_mask, turn_speaker
    )
    near = list(prefill_near(scalars, turn_queries, qf, own, sib, kf_own, 0, 2))
    packets[0], packets[1], packets[3], near[0] = tie((packets[0], packets[1], packets[3], near[0]))
    packets[2] = from_y(packets[0], 2)
    near = list(prefill_near(scalars, turn_queries, qf, own, sib, kf_own, 2, 2, near))
    packets[0], packets[2], near[0] = tie((packets[0], packets[2], near[0]))
    ctx = context_part(scalars, packets[0], context_keys, context_values, step_kv, steps)
    far, xp, xm, _ = tie((far, xp, xm, ctx[1]))
    farsib, xps, xms = from_core(far), from_core(xp), from_core(xm)
    early = prefill_far(scalars, turn_queries, qf, far, farsib, kf_own, near, ())
    early, kf_other = tie((early, kf_other))
    moved = (own, sib, far, farsib, xp, xps, xm, xms)
    parts = turn_part(scalars, packets, moved, kf_own, kf_other, ())
    back = [parts[0]] + [from_y(parts[j], -j) for j in (1, 2, 3)]
    turn_attention = prefill_far(
        scalars, turn_queries, qf, far, farsib, kf_own, near, (parts[0],), early
    )
    step_attention = merge(scalars, *ctx, back, steps)
    return turn_attention, step_attention


def solution(mesh):
    heads = mesh.shape["head"]
    fine = Mesh(mesh.devices.reshape(2, 4, 2, 2, heads), ("xlo", "y", "xhi", "core", "head"))
    split = ("xlo", "y", "xhi", "core")
    return jax.shard_map(
        body,
        mesh=fine,
        in_specs=(
            P(split, None),
            P(None, "head"),
            P(None, "head"),
            P(split, "head"),
            P(),
            P(),
            P(),
            P(split, "head"),
            P(split, "head"),
            P(),
            P(),
            P(split, None, None),
            P(split, None, "head"),
            P(split),
        ),
        out_specs=(P(split, "head"), P(split, None, "head")),
        check_vma=False,
    )
```

```python
import functools
import math

import jax
import jax.numpy as jnp
from jax import lax
from jax.experimental import pallas as pl
from jax.experimental.pallas import tpu as pltpu
from jax.sharding import Mesh
from jax.sharding import PartitionSpec as P

HQ = 64
KVH = 8
HD = 128
SPK = 4
GQ = HQ // KVH

HIDE = -1e30
SCALE = math.log2(math.e) / math.sqrt(HD)
NT = (((1,), (1,)), ((), ()))
F32 = jnp.float32
BF16 = jnp.bfloat16

S_OWN, S_SIB, S_FAR, S_FARSIB, S_REL, S_WHICH, S_SEL, S_LEN, S_XP, S_EARLY = 0, 1, 2, 3, 4, 8, 12, 13, 14, 15


def params(mib):
    return pltpu.CompilerParams(vmem_limit_bytes=mib * 2**20)


def in_vmem(x):
    return pltpu.with_memory_space_constraint(x, pltpu.VMEM)


def in_hbm(x):
    return pltpu.with_memory_space_constraint(x, pltpu.HBM)


def with_ones(v):
    return jnp.concatenate([v, jnp.ones(v.shape, BF16)], 1)


def marks(table, speakers):
    row = lax.broadcasted_iota(jnp.int32, (8, HD), 0)
    hot = jnp.where(speakers == row, 1.0, 0.0).astype(BF16)
    out = lax.dot_general(hot, table, (((0,), (0,)), ((), ())), preferred_element_type=F32)
    return out.astype(BF16)


def mark_columns(blocks, homes, lengths, mask, spk_ref, sc, qf_ref, kfo_ref, kfx_ref):
    xlo, y, xhi, core = (lax.axis_index(a) for a in ("xlo", "y", "xhi", "core"))
    own_at = xhi * 2 + core
    dialog = xlo * 4 + y
    here = blocks[dialog * 4 + own_at]
    sc[S_OWN] = own_at
    for i, at in ((1, S_SIB), (2, S_FAR), (3, S_FARSIB)):
        sc[at] = jnp.where(blocks[dialog * 4 + (own_at ^ i)] < here, 1, 0)
    for j in range(4):
        home = homes[xlo * 16 + (y + j) % 4 * 4 + own_at]
        sc[S_REL + j] = jnp.where(home % 4 == y, 1, 0)
        sc[S_WHICH + j] = jnp.where(home // 4 != xlo, 1, 0)
    home = homes[xlo * 16 + y * 4 + own_at]
    sc[S_SEL] = (y - home % 4 + 4) % 4
    sc[S_LEN] = lengths[home]
    sc[S_XP] = (xhi ^ xlo) * 2 + core

    most = jnp.int32(0)
    mine = jnp.int32(0)
    for c in range(8):
        rows_of = [homes[c // 4 * 16 + at * 4 + c % 4] % 4 for at in range(4)]
        for at in range(4):
            count = sum(jnp.where(r == at, 1, 0) for r in rows_of)
            most = jnp.maximum(most, count)
            mine = jnp.where((c == xlo * 4 + own_at) & (y == at), count, mine)
    sc[S_EARLY] = jnp.minimum((most - mine) * 2 // 3, 3)

    row = lax.broadcasted_iota(jnp.int32, (8, HD), 0)
    lane = lax.broadcasted_iota(jnp.int32, (8, HD), 1)
    for d, out in ((dialog, kfo_ref), ((1 - xlo) * 4 + y, kfx_ref)):
        table = jnp.zeros((8, HD), F32)
        for a in range(SPK):
            for b in range(SPK):
                add = jnp.where(mask[a, b, d] == 1, 0.0, HIDE)
                table = jnp.where((row == b) & (lane == a), add, table)
        table = table.astype(BF16)
        for i in range(16):
            out[i * HD : (i + 1) * HD, :] = marks(table, spk_ref[d * 2 + i // 8, i % 8 : i % 8 + 1, :])
    eye = jnp.where((row == lane) & (row < SPK), 1.0, 0.0).astype(BF16)
    for i in range(4):
        at = (dialog * 4 + own_at) * 4 + i
        qf_ref[i * HD : (i + 1) * HD, :] = marks(eye, spk_ref[at // 8, pl.ds(at % 8, 1), :])


def fill_packet(row_spk, q_ref, pk_ref, wide):
    groups, steps, width = q_ref.shape
    srows = groups * steps
    for r in range(groups):
        wide[r * steps : (r + 1) * steps, :] = q_ref[r].astype(F32)
    pk_ref[:, :width] = wide[...].astype(BF16)
    row = lax.broadcasted_iota(jnp.int32, (srows, HD), 0)
    lane = lax.broadcasted_iota(jnp.int32, (srows, HD), 1)
    speaker = jnp.zeros((srows, HD), jnp.int32)
    for r in range(groups):
        speaker = jnp.where(row // steps == r, row_spk[r], speaker)
    pk_ref[:, width:] = jnp.where(lane == speaker, 1.0, 0.0).astype(BF16)


def project_kernel(
    x_hbm, s_hbm, wk_hbm, wv_hbm, blocks_hbm, homes_hbm, lengths_hbm, mask_hbm, row_spk_hbm, spk_hbm, q_hbm,
    kv_ref, skv_ref, sc, qf_ref, kfo_ref, kfx_ref, pk_ref,
    xb, sb, wkb, wvb, wide, wide_q, blocks, homes, lengths, mask, row_spk, spk_ref, q_ref, sem, small_sem, *, chunk
):
    groups, steps, depth = s_hbm.shape
    small = [
        (blocks_hbm, blocks),
        (homes_hbm, homes),
        (lengths_hbm, lengths),
        (mask_hbm, mask),
        (row_spk_hbm, row_spk),
        (spk_hbm, spk_ref),
        (q_hbm, q_ref),
    ]
    small = [pltpu.make_async_copy(a, b, small_sem.at[n]) for n, (a, b) in enumerate(small)]
    for copy in small:
        copy.start()
    copies = []
    for i in range(depth // chunk):
        c = pl.ds(i * chunk, chunk)
        pairs = [
            (x_hbm.at[:, c], xb.at[:, c]),
            (wk_hbm.at[c, :], wkb.at[c, :]),
            (wv_hbm.at[c, :], wvb.at[c, :]),
        ]
        copies.append([pltpu.make_async_copy(a, b, sem.at[i, n]) for n, (a, b) in enumerate(pairs)])
        for copy in copies[-1]:
            copy.start()
        if i == 0:
            step_copy = pltpu.make_async_copy(s_hbm, sb, sem.at[0, 3])
            step_copy.start()
    for copy in small:
        copy.wait()
    mark_columns(blocks, homes, lengths, mask, spk_ref, sc, qf_ref, kfo_ref, kfx_ref)
    fill_packet(row_spk, q_ref, pk_ref, wide_q)
    acc = None
    for i, these in enumerate(copies):
        for copy in these:
            copy.wait()
        c = slice(i * chunk, (i + 1) * chunk)
        w = jnp.concatenate([wkb[c, :], wvb[c, :]], 1)
        if i == 0:
            step_copy.wait()
        for r in range(groups):
            wide[r * steps : (r + 1) * steps, c] = sb[r, :, c].astype(F32)
        both = jnp.concatenate([xb[:, c], wide[:, c].astype(BF16)], 0)
        part = jnp.dot(both, w, preferred_element_type=F32)
        acc = part if acc is None else acc + part
    rows = xb.shape[0]
    for at, first in enumerate((0, 2 * HD, HD, 3 * HD)):
        kv_ref[at] = acc[:rows, first : first + HD].astype(BF16)
        skv_ref[at] = acc[rows:, first : first + HD].astype(BF16)


def project(x, steps, w_key, w_value, blocks, homes, lengths, mask, row_spk, spk, queries):
    rows, depth = x.shape
    srows = steps.shape[0] * steps.shape[1]
    chunk = 1024
    hbm = pl.BlockSpec(memory_space=pl.ANY)
    vmem = pl.BlockSpec(memory_space=pltpu.VMEM)
    smem = pl.BlockSpec(memory_space=pltpu.SMEM)
    width = queries.shape[2]
    table = (blocks, homes, lengths, mask.transpose(1, 2, 0), row_spk)
    spk = spk.reshape(-1, 8, HD)
    return pl.pallas_call(
        functools.partial(project_kernel, chunk=chunk),
        in_specs=[hbm] * 11,
        out_specs=[vmem] * 2 + [smem] + [vmem] * 4,
        out_shape=[
            jax.ShapeDtypeStruct((4, rows, HD), BF16),
            jax.ShapeDtypeStruct((4, srows, HD), BF16),
            jax.ShapeDtypeStruct((16,), jnp.int32),
            pltpu.VMEM((rows, HD), BF16),
            pltpu.VMEM((4 * rows, HD), BF16),
            pltpu.VMEM((4 * rows, HD), BF16),
            pltpu.VMEM((srows, width + HD), BF16),
        ],
        scratch_shapes=[
            pltpu.VMEM(x.shape, BF16),
            pltpu.VMEM(steps.shape, BF16),
            pltpu.VMEM(w_key.shape, BF16),
            pltpu.VMEM(w_value.shape, BF16),
            pltpu.VMEM((srows, depth), F32),
            pltpu.VMEM((srows, width), F32),
            *(pltpu.SMEM(x.shape, jnp.int32) for x in table),
            pltpu.VMEM(spk.shape, jnp.int32),
            pltpu.VMEM(queries.shape, BF16),
            pltpu.SemaphoreType.DMA((depth // chunk, 4)),
            pltpu.SemaphoreType.DMA((7,)),
        ],
        compiler_params=params(30),
        cost_estimate=pl.CostEstimate(
            flops=2 * (rows + srows) * depth * 4 * HD,
            bytes_accessed=2 * depth * (rows + srows + 4 * HD),
            transcendentals=0,
        ),
        name="project",
    )(
        *map(in_hbm, (x, steps, w_key, w_value, *table, spk, queries)),
    )


def scores(q, k):
    return lax.dot_general(q, k, NT, preferred_element_type=F32)


def settle(s, v, state=None):
    m = jnp.max(s, axis=1, keepdims=True)
    if state is not None:
        m = jnp.maximum(m, state[0])
    p = jnp.exp2((s - m) * SCALE).astype(BF16)
    acc = jnp.dot(p, v, preferred_element_type=F32)
    if state is not None:
        acc = acc + state[1] * jnp.exp2((state[0] - m) * SCALE)
    return m, acc


def in_turn(items, score, finish):
    ahead = score(items[0])
    for i, item in enumerate(items):
        now = ahead
        if i + 1 < len(items):
            ahead = score(items[i + 1])
        finish(item, now)


def keys_of(k, kf):
    return jnp.concatenate([k, kf], 1)


def shown(marks_of_keys, flag):
    return marks_of_keys + jnp.where(flag != 0, 0.0, HIDE).astype(BF16)


def query_of(q_ref, qf_ref, group, h, first, count):
    q = q_ref[first : first + count, pl.ds(pl.multiple_of(group * STATE * HD, HD) + h * HD, HD)]
    return jnp.concatenate([q, qf_ref[first : first + count, :]], 1)


def near_kernel(sc, q_ref, qf_ref, own_ref, sib_ref, kf_ref, *refs, first):
    acc_ref, ml_ref = refs[-2:]
    group = pl.program_id(0) + first
    kvh = group * STATE // GQ
    rows = q_ref.shape[0]
    half = rows // 2
    own = pl.multiple_of(sc[S_OWN] * rows, rows)
    sib = pl.multiple_of((sc[S_OWN] ^ 1) * rows, rows)
    lane = lax.broadcasted_iota(jnp.int32, (half, HD), 1)

    k = keys_of(own_ref[2 * kvh], kf_ref[pl.ds(own, rows), :])
    v = with_ones(own_ref[2 * kvh + 1])
    late = keys_of(sib_ref[2 * kvh], shown(kf_ref[pl.ds(sib, rows), :], sc[S_SIB]))
    late_v = with_ones(sib_ref[2 * kvh + 1])
    ks = [jnp.concatenate([k[:half], late], 0), jnp.concatenate([k, late], 0)]
    vs = [jnp.concatenate([v[:half], late_v], 0), jnp.concatenate([v, late_v], 0)]
    ml = [jnp.zeros((half, HD), F32)] * 2

    def score(item):
        h, part = item
        q = [query_of(q_ref, qf_ref, group, h + i, part * half, half) for i in range(HN)]
        s = scores(jnp.concatenate(q, 0), ks[part])
        own_cols = (part + 1) * half
        at_row = lax.broadcasted_iota(jnp.int32, (HN * half, half), 0) % half
        at_col = lax.broadcasted_iota(jnp.int32, (HN * half, half), 1)
        corner = jnp.where(at_col <= at_row, s[:, own_cols - half : own_cols], HIDE)
        cut = [s[:, : own_cols - half]] * (part > 0) + [corner, s[:, own_cols:]]
        return jnp.concatenate(cut, 1)

    def finish(item, s):
        h0, part = item
        ms, accs = settle(s, vs[part])
        for i in range(HN):
            h = h0 + i
            m, acc = ms[i * half : (i + 1) * half], accs[i * half : (i + 1) * half]
            acc_ref[group, part * half : (part + 1) * half, h * HD : (h + 1) * HD] = acc[:, :HD]
            ml[part] = jnp.where(lane == h, m, jnp.where(lane == STATE + h, acc[:, HD:], ml[part]))

    in_turn([(h, part) for h in range(0, STATE, HN) for part in (0, 1)], score, finish)
    for part in (0, 1):
        ml_ref[group, part * half : (part + 1) * half, :] = ml[part]


def far_kernel(sc, q_ref, qf_ref, far_ref, fs_ref, kf_ref, acc_ref, ml_ref, *rest, early):
    group = pl.program_id(0)
    kvh = group * STATE // GQ
    o_ref = rest[-1]
    rows = q_ref.shape[0]
    half = rows // 2
    far = pl.multiple_of((sc[S_OWN] ^ 2) * rows, rows)
    farsib = pl.multiple_of((sc[S_OWN] ^ 3) * rows, rows)

    def run(seen):
        if seen:
            blocks = [(far_ref, far, S_FAR), (fs_ref, farsib, S_FARSIB)]
            k = [keys_of(x[2 * kvh], shown(kf_ref[pl.ds(at, rows), :], sc[flag])) for x, at, flag in blocks]
            k = jnp.concatenate(k, 0)
            v = jnp.concatenate([with_ones(x[2 * kvh + 1]) for x, _, _ in blocks], 0)

        def score(item):
            q = [query_of(q_ref, qf_ref, group, item + i, 0, rows) for i in range(HF)]
            return scores(jnp.concatenate(q, 0), k) if seen else None

        def finish(item, s):
            state = []
            for h in range(item, item + HF):
                ml = ml_ref[group]
                l = jnp.broadcast_to(ml[:, STATE + h : STATE + h + 1], (rows, HD))
                acc = jnp.concatenate([acc_ref[group, :, h * HD : (h + 1) * HD], l], 1)
                state.append((ml[:, h : h + 1], acc))
            m = jnp.concatenate([x[0] for x in state], 0)
            acc = jnp.concatenate([x[1] for x in state], 0)
            if seen:
                acc = settle(s, v, (m, acc))[1]
            out = (acc[:, :HD] / acc[:, HD:]).astype(BF16)
            for i in range(HF):
                o_ref[:, (item + i) * HD : (item + i + 1) * HD] = out[i * rows : (i + 1) * rows]

        in_turn(list(range(0, STATE, HF)), score, finish)

    mine = (group < sc[S_EARLY]) == early
    seen = (sc[S_FAR] != 0) | (sc[S_FARSIB] != 0)
    pl.when(mine & seen)(functools.partial(run, True))
    pl.when(mine & jnp.logical_not(seen))(functools.partial(run, False))


STATE = 4
HN = 2
HF = 1


def prefill_near(scalars, q, qf, own, sib, kf, first, count, state=()):
    rows, width = q.shape
    wide = STATE * HD
    groups = width // wide
    vmem = pl.BlockSpec(memory_space=pltpu.VMEM)
    return pl.pallas_call(
        functools.partial(near_kernel, first=first),
        grid_spec=pltpu.PrefetchScalarGridSpec(
            num_scalar_prefetch=1,
            grid=(count,),
            in_specs=[vmem] * (5 + len(state)),
            out_specs=[vmem, vmem],
        ),
        out_shape=[
            pltpu.VMEM((groups, rows, wide), F32),
            pltpu.VMEM((groups, rows, HD), F32),
        ],
        input_output_aliases={6: 0, 7: 1} if state else {},
        compiler_params=params(16),
        cost_estimate=pl.CostEstimate(
            flops=4 * GQ * rows * rows * 2 * 2 * HD, bytes_accessed=4 * 2**20, transcendentals=0
        ),
        name="prefill_near",
    )(scalars, *map(in_vmem, (q, qf, own, sib, kf, *state)))


def prefill_far(scalars, q, qf, far, farsib, kf, state, after, earlier=None):
    rows, width = q.shape
    wide = STATE * HD
    early = earlier is None
    if early:
        columns = pl.BlockSpec((rows, wide), lambda g, sc: (0, jnp.minimum(g, jnp.maximum(sc[S_EARLY], 1) - 1)))
    else:
        columns = pl.BlockSpec((rows, wide), lambda g, sc: (0, jnp.maximum(g, sc[S_EARLY])))
    vmem = pl.BlockSpec(memory_space=pltpu.VMEM)
    hbm = pl.BlockSpec(memory_space=pl.ANY)
    extra = list(after) + ([] if early else [earlier])
    return pl.pallas_call(
        functools.partial(far_kernel, early=early),
        grid_spec=pltpu.PrefetchScalarGridSpec(
            num_scalar_prefetch=1,
            grid=(width // wide,),
            in_specs=[vmem] * 7 + [hbm] * len(extra),
            out_specs=columns,
        ),
        out_shape=pltpu.HBM(q.shape, BF16),
        input_output_aliases={} if early else {7 + len(extra): 0},
        compiler_params=params(16),
        cost_estimate=pl.CostEstimate(
            flops=4 * GQ * rows * rows * 2 * 2 * HD, bytes_accessed=4 * 2**20, transcendentals=0
        ),
        name="prefill_far",
    )(scalars, *map(in_vmem, (q, qf, far, farsib, kf, *state)), *extra)


def context_kernel(sc, q_ref, ck_ref, cv_ref, own_ref, acc_ref, ml_ref, *, steps):
    srows = q_ref.shape[0]
    n = ck_ref.shape[0]
    block = 1024
    live = sc[S_LEN]
    lane = lax.broadcasted_iota(jnp.int32, (srows, HD), 1)
    q_mark = jnp.where(lane == 0, 1.0, 0.0).astype(BF16)
    zero = jnp.zeros((srows, HD), BF16)
    at_row = lax.broadcasted_iota(jnp.int32, (DEC * srows, srows), 0) % srows
    at_col = lax.broadcasted_iota(jnp.int32, (DEC * srows, srows), 1)
    own_mask = (at_row // steps == at_col // steps) & (at_col <= at_row)
    keys = {}
    for first in range(0, n, block):
        pos = lax.broadcasted_iota(jnp.int32, (block, HD), 0) + first
        col = lax.broadcasted_iota(jnp.int32, (block, HD), 1)
        mark = jnp.where((pos >= live) & (col == 0), HIDE, 0.0).astype(BF16)
        for kvh in (0, 1):
            r, c = slice(first, first + block), slice(kvh * HD, (kvh + 1) * HD)
            keys[kvh, first] = jnp.concatenate([ck_ref[r, c], mark], 1), with_ones(cv_ref[r, c])
    state = {}
    ml = [jnp.zeros((srows, HD), F32)]

    def query(g):
        cut = [q_ref[:, h * HD : (h + 1) * HD] for h in range(g * DEC, (g + 1) * DEC)]
        return jnp.concatenate([jnp.concatenate([q, q_mark], 1) for q in cut], 0)

    def score(item):
        g, first = item
        kvh = g * DEC // GQ
        if first < 0:
            s = scores(query(g), jnp.concatenate([own_ref[2 * kvh], zero], 1))
            return jnp.where(own_mask, s, HIDE)
        return scores(query(g), keys[kvh, first][0])

    def finish(item, s):
        g, first = item
        kvh = g * DEC // GQ
        v = with_ones(own_ref[2 * kvh + 1]) if first < 0 else keys[kvh, first][1]
        state[g] = settle(s, v, state.get(g))
        if first == n - block:
            m, acc = state[g]
            for i in range(DEC):
                at = g * DEC + i
                a = acc[i * srows : (i + 1) * srows]
                acc_ref[:, at * HD : (at + 1) * HD] = a[:, :HD]
                ml[0] = jnp.where(lane == at, m[i * srows : (i + 1) * srows], ml[0])
                ml[0] = jnp.where(lane == 2 * GQ + at, a[:, HD:], ml[0])

    groups = 2 * GQ // DEC
    in_turn([(g, first) for g in range(groups) for first in [-1, *range(0, n, block)]], score, finish)
    ml_ref[...] = ml[0]


def context_part(scalars, q, ck, cv, own, steps):
    srows, width = q.shape[0], q.shape[1] - HD
    return pl.pallas_call(
        functools.partial(context_kernel, steps=steps),
        grid_spec=pltpu.PrefetchScalarGridSpec(
            num_scalar_prefetch=1,
            grid=(1,),
            in_specs=[pl.BlockSpec(memory_space=pltpu.VMEM)] * 4,
            out_specs=[
                pl.BlockSpec((srows, width), lambda i, sc: (0, 0)),
                pl.BlockSpec((srows, HD), lambda i, sc: (0, 0)),
            ],
        ),
        out_shape=[
            jax.ShapeDtypeStruct((srows, width), F32),
            jax.ShapeDtypeStruct((srows, HD), F32),
        ],
        compiler_params=params(12),
        name="context_part",
    )(scalars, q, in_vmem(ck), in_vmem(cv), own)


DEC = 8


def pieces(x):
    hi = x.astype(BF16)
    rest = x - hi.astype(F32)
    mid = rest.astype(BF16)
    return hi, mid, (rest - mid.astype(F32)).astype(BF16)


def turn_kernel(sc, p0, p1, p2, p3, own, sib, far, fs, xp, xps, xm, xms, kfo, kfx, o0, o1, o2, o3, ks, vs, qs, os):
    head = pl.program_id(0)
    srows = p0.shape[0]
    rows = own.shape[1]
    keys = 4 * rows
    wide = GQ * HD
    for which, refs, first, kf in ((0, (own, sib, far, fs), S_OWN, kfo), (1, (xp, xps, xm, xms), S_XP, kfx)):
        wanted = [(sc[S_REL + j] != 0) & (sc[S_WHICH + j] == which) for j in range(4)]

        @pl.when(wanted[0] | wanted[1] | wanted[2] | wanted[3])
        def _():
            ks[which, :, HD:] = kf[...]
            vs[which, :, HD:] = jnp.ones((keys, HD), BF16)
            for i, ref in enumerate(refs):
                at = pl.multiple_of((sc[first] ^ i) * rows, rows)
                ks[which, pl.ds(at, rows), :HD] = ref[2 * head]
                vs[which, pl.ds(at, rows), :HD] = ref[2 * head + 1]

    for j, p in enumerate((p0, p1, p2, p3)):

        @pl.when(sc[S_REL + j] != 0)
        def _():
            qs[j, :, :wide] = p[:, pl.ds(pl.multiple_of(head * wide, wide), wide)]
            qs[j, :, wide:] = p[:, 2 * wide :]

    lane = lax.broadcasted_iota(jnp.int32, (srows, HD), 1)
    block = 1024

    def one(j, carry):
        @pl.when(sc[S_REL + j] != 0)
        def _():
            which = sc[S_WHICH + j]
            feat = qs[j, :, wide:]
            state = {}
            ml = [jnp.zeros((srows, HD), F32)] * 2

            def score(item):
                g, first = item
                cut = [qs[j, :, h * HD : (h + 1) * HD] for h in range(g * DEC, (g + 1) * DEC)]
                q = jnp.concatenate([jnp.concatenate([q, feat], 1) for q in cut], 0)
                return scores(q, ks[which, first : first + block, :])

            def finish(item, s):
                g, first = item
                state[g] = settle(s, vs[which, first : first + block, :], state.get(g))
                if first == keys - block:
                    m, acc = state[g]
                    for i in range(DEC):
                        h = g * DEC + i
                        r = slice(i * srows, (i + 1) * srows)
                        os[j, :, h * HD : (h + 1) * HD] = acc[r, :HD].astype(BF16)
                        for part in range(3):
                            ml[0] = jnp.where(lane == part * GQ + h, m[r], ml[0])
                            ml[1] = jnp.where(lane == (part + 3) * GQ + h, acc[r, HD:], ml[1])

            in_turn([(g, first) for first in range(0, keys, block) for g in range(GQ // DEC)], score, finish)
            m3, l3 = pieces(ml[0]), pieces(ml[1])
            ext = jnp.zeros((srows, HD), F32)
            for part in range(3):
                ext = jnp.where(lane // GQ == part, m3[part].astype(F32), ext)
                ext = jnp.where(lane // GQ == part + 3, l3[part].astype(F32), ext)
            os[j, :, wide:] = ext.astype(BF16)

        return carry

    lax.fori_loop(0, 4, one, 0)
    for j, o in enumerate((o0, o1, o2, o3)):
        o[...] = os[j]


def turn_part(scalars, packets, kvs, kf_own, kf_other, after):
    srows = packets[0].shape[0]
    rows = kvs[0].shape[1]
    wide = GQ * HD + HD

    def kernel(*refs):
        turn_kernel(*refs[:15], *refs[15 + len(after) :])

    return pl.pallas_call(
        kernel,
        grid_spec=pltpu.PrefetchScalarGridSpec(
            num_scalar_prefetch=1,
            grid=(2,),
            in_specs=[pl.BlockSpec(memory_space=pltpu.VMEM)] * 14
            + [pl.BlockSpec(memory_space=pl.ANY)] * len(after),
            out_specs=[pl.BlockSpec((srows, wide), lambda g, sc: (0, g))] * 4,
            scratch_shapes=[
                pltpu.VMEM((2, 4 * rows, 2 * HD), BF16),
                pltpu.VMEM((2, 4 * rows, 2 * HD), BF16),
                pltpu.VMEM((4, srows, wide), BF16),
                pltpu.VMEM((4, srows, wide), BF16),
            ],
        ),
        out_shape=[jax.ShapeDtypeStruct((srows, 2 * wide), BF16)] * 4,
        compiler_params=params(20),
        cost_estimate=pl.CostEstimate(
            flops=4 * 4 * srows * GQ * 4 * rows * 2 * HD, bytes_accessed=4 * 2**20, transcendentals=0
        ),
        name="turn_part",
    )(scalars, *map(in_vmem, packets), *map(in_vmem, kvs), in_vmem(kf_own), in_vmem(kf_other), *after)


def merge_kernel(sc, acc_ref, ml_ref, *refs):
    o_ref, wide = refs[-2:]
    sel = sc[S_SEL]
    groups, steps, _ = o_ref.shape
    ml = ml_ref[...]
    width = GQ * HD
    for kvh in range(2):
        first = kvh * (width + HD)

        def pick(cols):
            cols = slice(first + cols.start, first + cols.stop)
            x = refs[0][:, cols]
            for j in (1, 2, 3):
                x = jnp.where(sel == j, refs[j][:, cols], x)
            return x.astype(F32)

        ext = pick(slice(width, width + HD))
        whole = [
            ext[:, i * GQ : (i + 1) * GQ]
            + ext[:, (i + 1) * GQ : (i + 2) * GQ]
            + ext[:, (i + 2) * GQ : (i + 3) * GQ]
            for i in (0, 3)
        ]
        m2, l2 = whole
        m1 = ml[:, kvh * GQ : (kvh + 1) * GQ]
        l1 = ml[:, (2 + kvh) * GQ : (3 + kvh) * GQ]
        m = jnp.maximum(m1, m2)
        w1, w2 = jnp.exp2((m1 - m) * SCALE), jnp.exp2((m2 - m) * SCALE)
        total = l1 * w1 + l2 * w2
        w1, w2 = w1 / total, w2 / total
        for h in range(GQ):
            at = kvh * GQ + h
            a1 = acc_ref[:, at * HD : (at + 1) * HD]
            a2 = pick(slice(h * HD, (h + 1) * HD))
            wide[:, at * HD : (at + 1) * HD] = a1 * w1[:, h : h + 1] + a2 * w2[:, h : h + 1]
    for r in range(groups):
        o_ref[r] = wide[r * steps : (r + 1) * steps, :].astype(BF16)


def merge(scalars, acc, ml, back, steps):
    args = (acc, ml, *back)
    shape = (acc.shape[0] // steps, steps, acc.shape[1])
    return pl.pallas_call(
        merge_kernel,
        grid_spec=pltpu.PrefetchScalarGridSpec(
            num_scalar_prefetch=1,
            grid=(1,),
            in_specs=[pl.BlockSpec(a.shape, lambda i, sc: (0, 0)) for a in args],
            out_specs=pl.BlockSpec(shape, lambda i, sc: (0, 0, 0)),
            scratch_shapes=[pltpu.VMEM(acc.shape, F32)],
        ),
        out_shape=jax.ShapeDtypeStruct(shape, BF16),
        compiler_params=params(8),
        name="merge",
    )(scalars, *args)


ROW = ("xlo", "xhi")


def row_index(x):
    return x % 2 * 2 + x // 2


def from_x(a, shift):
    return lax.ppermute(a, ROW, [(row_index((x + shift) % 4), row_index(x)) for x in range(4)])


def from_y(a, shift):
    return lax.ppermute(a, "y", [((y + shift) % 4, y) for y in range(4)])


def from_core(a):
    return lax.ppermute(a, "core", [(0, 1), (1, 0)])


def body(
    turn_hidden,
    w_key,
    w_value,
    turn_queries,
    turn_speaker,
    speaker_mask,
    shard_block,
    context_keys,
    context_values,
    context_length,
    decode_home,
    step_hidden,
    step_queries,
    row_speaker,
):
    steps = step_hidden.shape[1]
    tie = lax.optimization_barrier
    own, step_kv, scalars, qf, kf_own, kf_other, packet = project(
        turn_hidden,
        step_hidden,
        w_key,
        w_value,
        shard_block,
        decode_home,
        context_length,
        speaker_mask,
        row_speaker,
        turn_speaker,
        step_queries,
    )
    far, sib, xp, xm = from_x(own, 2), from_core(own), from_x(own, 1), from_x(own, 3)
    sib, packet = tie((sib, packet))
    packets = [packet, from_y(packet, 1), None, from_y(packet, 3)]
    near = list(prefill_near(scalars, turn_queries, qf, own, sib, kf_own, 0, 2))
    packets[0], packets[1], packets[3], near[0] = tie((packets[0], packets[1], packets[3], near[0]))
    packets[2] = from_y(packets[0], 2)
    near = list(prefill_near(scalars, turn_queries, qf, own, sib, kf_own, 2, 2, near))
    packets[0], packets[2], near[0] = tie((packets[0], packets[2], near[0]))
    ctx = context_part(scalars, packets[0], context_keys, context_values, step_kv, steps)
    far, xp, xm, _ = tie((far, xp, xm, ctx[1]))
    farsib, xps, xms = from_core(far), from_core(xp), from_core(xm)
    early = prefill_far(scalars, turn_queries, qf, far, farsib, kf_own, near, ())
    early, kf_other = tie((early, kf_other))
    moved = (own, sib, far, farsib, xp, xps, xm, xms)
    parts = turn_part(scalars, packets, moved, kf_own, kf_other, ())
    back = [parts[0]] + [from_y(parts[j], -j) for j in (1, 2, 3)]
    turn_attention = prefill_far(
        scalars, turn_queries, qf, far, farsib, kf_own, near, (parts[0],), early
    )
    step_attention = merge(scalars, *ctx, back, steps)
    return turn_attention, step_attention


def solution(mesh):
    heads = mesh.shape["head"]
    fine = Mesh(mesh.devices.reshape(2, 4, 2, 2, heads), ("xlo", "y", "xhi", "core", "head"))
    split = ("xlo", "y", "xhi", "core")
    return jax.shard_map(
        body,
        mesh=fine,
        in_specs=(
            P(split, None),
            P(None, "head"),
            P(None, "head"),
            P(split, "head"),
            P(),
            P(),
            P(),
            P(split, "head"),
            P(split, "head"),
            P(),
            P(),
            P(split, None, None),
            P(split, None, "head"),
            P(split),
        ),
        out_specs=(P(split, "head"), P(split, None, "head")),
        check_vma=False,
    )
```

```python
import functools
import math

import jax
import jax.numpy as jnp
from jax import lax
from jax.experimental import pallas as pl
from jax.experimental.pallas import tpu as pltpu
from jax.sharding import Mesh
from jax.sharding import PartitionSpec as P

HQ = 64
KVH = 8
HD = 128
SPK = 4
GQ = HQ // KVH

HIDE = -1e30
SCALE = math.log2(math.e) / math.sqrt(HD)
NT = (((1,), (1,)), ((), ()))
F32 = jnp.float32
BF16 = jnp.bfloat16

S_OWN, S_SIB, S_FAR, S_FARSIB, S_REL, S_WHICH, S_SEL, S_LEN, S_XP, S_EARLY = 0, 1, 2, 3, 4, 8, 12, 13, 14, 15


def params(mib):
    return pltpu.CompilerParams(vmem_limit_bytes=mib * 2**20)


def in_vmem(x):
    return pltpu.with_memory_space_constraint(x, pltpu.VMEM)


def in_hbm(x):
    return pltpu.with_memory_space_constraint(x, pltpu.HBM)


def over(x, y):
    r = pl.reciprocal(y, approx=True)
    return x * (r * (2.0 - y * r))


def with_ones(v):
    return jnp.concatenate([v, jnp.ones(v.shape, BF16)], 1)


def marks(table, speakers):
    row = lax.broadcasted_iota(jnp.int32, (8, HD), 0)
    hot = jnp.where(speakers == row, 1.0, 0.0).astype(BF16)
    out = lax.dot_general(hot, table, (((0,), (0,)), ((), ())), preferred_element_type=F32)
    return out.astype(BF16)


def prep_kernel(blocks, homes, lengths, mask, row_spk, spk_ref, q_ref, sc, qf_ref, kfo_ref, kfx_ref, pk_ref, wide):
    fill_packet(row_spk, q_ref, pk_ref, wide)
    xlo, y, xhi, core = (lax.axis_index(a) for a in ("xlo", "y", "xhi", "core"))
    own_at = xhi * 2 + core
    dialog = xlo * 4 + y
    here = blocks[dialog * 4 + own_at]
    sc[S_OWN] = own_at
    for i, at in ((1, S_SIB), (2, S_FAR), (3, S_FARSIB)):
        sc[at] = jnp.where(blocks[dialog * 4 + (own_at ^ i)] < here, 1, 0)
    for j in range(4):
        home = homes[xlo * 16 + (y + j) % 4 * 4 + own_at]
        sc[S_REL + j] = jnp.where(home % 4 == y, 1, 0)
        sc[S_WHICH + j] = jnp.where(home // 4 != xlo, 1, 0)
    home = homes[xlo * 16 + y * 4 + own_at]
    sc[S_SEL] = (y - home % 4 + 4) % 4
    sc[S_LEN] = lengths[home]
    sc[S_XP] = (xhi ^ xlo) * 2 + core

    most = jnp.int32(0)
    mine = jnp.int32(0)
    for c in range(8):
        rows_of = [homes[c // 4 * 16 + at * 4 + c % 4] % 4 for at in range(4)]
        for at in range(4):
            count = sum(jnp.where(r == at, 1, 0) for r in rows_of)
            most = jnp.maximum(most, count)
            mine = jnp.where((c == xlo * 4 + own_at) & (y == at), count, mine)
    sc[S_EARLY] = jnp.minimum((most - mine) * 2 // 3, EARLY_MOST)

    row = lax.broadcasted_iota(jnp.int32, (8, HD), 0)
    lane = lax.broadcasted_iota(jnp.int32, (8, HD), 1)
    for d, out in ((dialog, kfo_ref), ((1 - xlo) * 4 + y, kfx_ref)):
        table = jnp.zeros((8, HD), F32)
        for a in range(SPK):
            for b in range(SPK):
                add = jnp.where(mask[a, b, d] == 1, 0.0, HIDE)
                table = jnp.where((row == b) & (lane == a), add, table)
        table = table.astype(BF16)
        for i in range(16):
            out[i * HD : (i + 1) * HD, :] = marks(table, spk_ref[d * 2 + i // 8, i % 8 : i % 8 + 1, :])
    eye = jnp.where((row == lane) & (row < SPK), 1.0, 0.0).astype(BF16)
    for i in range(4):
        at = (dialog * 4 + own_at) * 4 + i
        qf_ref[i * HD : (i + 1) * HD, :] = marks(eye, spk_ref[at // 8, pl.ds(at % 8, 1), :])


def prepare(blocks, homes, lengths, mask, row_spk, spk, queries):
    groups, steps, width = queries.shape
    rows = spk.size // 32
    smem = pl.BlockSpec(memory_space=pltpu.SMEM)
    vmem = pl.BlockSpec(memory_space=pltpu.VMEM)
    return pl.pallas_call(
        prep_kernel,
        in_specs=[smem] * 5 + [vmem] * 2,
        out_specs=[smem] + [vmem] * 4,
        out_shape=[
            jax.ShapeDtypeStruct((16,), jnp.int32),
            pltpu.VMEM((rows, HD), BF16),
            pltpu.VMEM((4 * rows, HD), BF16),
            pltpu.VMEM((4 * rows, HD), BF16),
            pltpu.VMEM((groups * steps, width + HD), BF16),
        ],
        scratch_shapes=[pltpu.VMEM((groups * steps, width), F32)],
        compiler_params=params(8),
        name="prepare",
    )(blocks, homes, lengths, mask.transpose(1, 2, 0), row_spk, spk.reshape(-1, 8, HD), queries)


def fill_packet(row_spk, q_ref, pk_ref, wide):
    groups, steps, width = q_ref.shape
    srows = groups * steps
    for r in range(groups):
        wide[r * steps : (r + 1) * steps, :] = q_ref[r].astype(F32)
    pk_ref[:, :width] = wide[...].astype(BF16)
    row = lax.broadcasted_iota(jnp.int32, (srows, HD), 0)
    lane = lax.broadcasted_iota(jnp.int32, (srows, HD), 1)
    speaker = jnp.zeros((srows, HD), jnp.int32)
    for r in range(groups):
        speaker = jnp.where(row // steps == r, row_spk[r], speaker)
    pk_ref[:, width:] = jnp.where(lane == speaker, 1.0, 0.0).astype(BF16)


def project_kernel(x_hbm, s_hbm, wk_hbm, wv_hbm, kv_ref, skv_ref, xb, sb, wkb, wvb, wide, sem, *, chunk):
    groups, steps, depth = s_hbm.shape
    copies = []
    for i in range(depth // chunk):
        c = pl.ds(i * chunk, chunk)
        pairs = [
            (x_hbm.at[:, c], xb.at[:, c]),
            (wk_hbm.at[c, :], wkb.at[c, :]),
            (wv_hbm.at[c, :], wvb.at[c, :]),
        ]
        copies.append([pltpu.make_async_copy(a, b, sem.at[i, n]) for n, (a, b) in enumerate(pairs)])
        for copy in copies[-1]:
            copy.start()
        if i == 0:
            step_copy = pltpu.make_async_copy(s_hbm, sb, sem.at[0, 3])
            step_copy.start()
    acc = None
    for i, these in enumerate(copies):
        for copy in these:
            copy.wait()
        c = slice(i * chunk, (i + 1) * chunk)
        w = jnp.concatenate([wkb[c, :], wvb[c, :]], 1)
        if i == 0:
            step_copy.wait()
        for r in range(groups):
            wide[r * steps : (r + 1) * steps, c] = sb[r, :, c].astype(F32)
        both = jnp.concatenate([xb[:, c], wide[:, c].astype(BF16)], 0)
        part = jnp.dot(both, w, preferred_element_type=F32)
        acc = part if acc is None else acc + part
    rows = xb.shape[0]
    for at, first in enumerate((0, 2 * HD, HD, 3 * HD)):
        kv_ref[at] = acc[:rows, first : first + HD].astype(BF16)
        skv_ref[at] = acc[rows:, first : first + HD].astype(BF16)


def project(x, steps, w_key, w_value):
    rows, depth = x.shape
    srows = steps.shape[0] * steps.shape[1]
    chunk = 1024
    hbm = pl.BlockSpec(memory_space=pl.ANY)
    vmem = pl.BlockSpec(memory_space=pltpu.VMEM)
    return pl.pallas_call(
        functools.partial(project_kernel, chunk=chunk),
        in_specs=[hbm] * 4,
        out_specs=[vmem] * 2,
        out_shape=[
            jax.ShapeDtypeStruct((4, rows, HD), BF16),
            jax.ShapeDtypeStruct((4, srows, HD), BF16),
        ],
        scratch_shapes=[
            pltpu.VMEM(x.shape, BF16),
            pltpu.VMEM(steps.shape, BF16),
            pltpu.VMEM(w_key.shape, BF16),
            pltpu.VMEM(w_value.shape, BF16),
            pltpu.VMEM((srows, depth), F32),
            pltpu.SemaphoreType.DMA((depth // chunk, 4)),
        ],
        compiler_params=params(28),
        cost_estimate=pl.CostEstimate(
            flops=2 * (rows + srows) * depth * 4 * HD,
            bytes_accessed=2 * depth * (rows + srows + 4 * HD),
            transcendentals=0,
        ),
        name="project",
    )(*map(in_hbm, (x, steps, w_key, w_value)))


def scores(q, k):
    return lax.dot_general(q, k, NT, preferred_element_type=F32)


def settle(s, v, state=None):
    m = jnp.max(s, axis=1, keepdims=True)
    if state is not None:
        m = jnp.maximum(m, state[0])
    p = jnp.exp2((s - m) * SCALE).astype(BF16)
    acc = jnp.dot(p, v, preferred_element_type=F32)
    if state is not None:
        acc = acc + state[1] * jnp.exp2((state[0] - m) * SCALE)
    return m, acc


def in_turn(items, score, finish):
    ahead = score(items[0])
    for i, item in enumerate(items):
        now = ahead
        if i + 1 < len(items):
            ahead = score(items[i + 1])
        finish(item, now)


def keys_of(k, kf):
    return jnp.concatenate([k, kf], 1)


def shown(marks_of_keys, flag):
    return marks_of_keys + jnp.where(flag != 0, 0.0, HIDE).astype(BF16)


def query_of(q_ref, qf_ref, group, h, first, count):
    q = q_ref[first : first + count, pl.ds(pl.multiple_of(group * STATE * HD, HD) + h * HD, HD)]
    return jnp.concatenate([q, qf_ref[first : first + count, :]], 1)


def near_kernel(sc, q_ref, qf_ref, own_ref, sib_ref, kf_ref, *refs, first):
    acc_ref, ml_ref = refs[-2:]
    group = pl.program_id(0) + first
    kvh = group * STATE // GQ
    rows = q_ref.shape[0]
    half = rows // 2
    own = pl.multiple_of(sc[S_OWN] * rows, rows)
    sib = pl.multiple_of((sc[S_OWN] ^ 1) * rows, rows)
    lane = lax.broadcasted_iota(jnp.int32, (half, HD), 1)

    k = keys_of(own_ref[2 * kvh], kf_ref[pl.ds(own, rows), :])
    v = with_ones(own_ref[2 * kvh + 1])
    late = keys_of(sib_ref[2 * kvh], shown(kf_ref[pl.ds(sib, rows), :], sc[S_SIB]))
    late_v = with_ones(sib_ref[2 * kvh + 1])
    ks = [jnp.concatenate([k[:half], late], 0), jnp.concatenate([k, late], 0)]
    vs = [jnp.concatenate([v[:half], late_v], 0), jnp.concatenate([v, late_v], 0)]
    ml = [jnp.zeros((half, HD), F32)] * 2

    def score(item):
        h, part = item
        q = [query_of(q_ref, qf_ref, group, h + i, part * half, half) for i in range(HN)]
        s = scores(jnp.concatenate(q, 0), ks[part])
        own_cols = (part + 1) * half
        at_row = lax.broadcasted_iota(jnp.int32, (HN * half, half), 0) % half
        at_col = lax.broadcasted_iota(jnp.int32, (HN * half, half), 1)
        corner = jnp.where(at_col <= at_row, s[:, own_cols - half : own_cols], HIDE)
        cut = [s[:, : own_cols - half]] * (part > 0) + [corner, s[:, own_cols:]]
        return jnp.concatenate(cut, 1)

    def finish(item, s):
        h0, part = item
        ms, accs = settle(s, vs[part])
        for i in range(HN):
            h = h0 + i
            m, acc = ms[i * half : (i + 1) * half], accs[i * half : (i + 1) * half]
            acc_ref[group, part * half : (part + 1) * half, h * HD : (h + 1) * HD] = acc[:, :HD]
            ml[part] = jnp.where(lane == h, m, jnp.where(lane == STATE + h, acc[:, HD:], ml[part]))

    in_turn([(h, part) for h in range(0, STATE, HN) for part in (0, 1)], score, finish)
    for part in (0, 1):
        ml_ref[group, part * half : (part + 1) * half, :] = ml[part]


def far_kernel(sc, q_ref, qf_ref, far_ref, fs_ref, kf_ref, acc_ref, ml_ref, *rest, early):
    group = pl.program_id(0)
    kvh = group * STATE // GQ
    o_ref = rest[-1]
    rows = q_ref.shape[0]
    half = rows // 2
    far = pl.multiple_of((sc[S_OWN] ^ 2) * rows, rows)
    farsib = pl.multiple_of((sc[S_OWN] ^ 3) * rows, rows)

    def run(seen):
        if seen:
            blocks = [(far_ref, far, S_FAR), (fs_ref, farsib, S_FARSIB)]
            k = [keys_of(x[2 * kvh], shown(kf_ref[pl.ds(at, rows), :], sc[flag])) for x, at, flag in blocks]
            k = jnp.concatenate(k, 0)
            v = jnp.concatenate([with_ones(x[2 * kvh + 1]) for x, _, _ in blocks], 0)

        def score(item):
            q = [query_of(q_ref, qf_ref, group, item + i, 0, rows) for i in range(HF)]
            return scores(jnp.concatenate(q, 0), k) if seen else None

        def finish(item, s):
            state = []
            for h in range(item, item + HF):
                ml = ml_ref[group]
                l = jnp.broadcast_to(ml[:, STATE + h : STATE + h + 1], (rows, HD))
                acc = jnp.concatenate([acc_ref[group, :, h * HD : (h + 1) * HD], l], 1)
                state.append((ml[:, h : h + 1], acc))
            m = jnp.concatenate([x[0] for x in state], 0)
            acc = jnp.concatenate([x[1] for x in state], 0)
            if seen:
                acc = settle(s, v, (m, acc))[1]
            out = over(acc[:, :HD], acc[:, HD:]).astype(BF16)
            for i in range(HF):
                o_ref[:, (item + i) * HD : (item + i + 1) * HD] = out[i * rows : (i + 1) * rows]

        in_turn(list(range(0, STATE, HF)), score, finish)

    mine = (group < sc[S_EARLY]) == early
    seen = (sc[S_FAR] != 0) | (sc[S_FARSIB] != 0)
    pl.when(mine & seen)(functools.partial(run, True))
    pl.when(mine & jnp.logical_not(seen))(functools.partial(run, False))


STATE = 4
EARLY_MOST = 2
HN = 2
HF = 1


def prefill_near(scalars, q, qf, own, sib, kf, first, count, state=()):
    rows, width = q.shape
    wide = STATE * HD
    groups = width // wide
    vmem = pl.BlockSpec(memory_space=pltpu.VMEM)
    return pl.pallas_call(
        functools.partial(near_kernel, first=first),
        grid_spec=pltpu.PrefetchScalarGridSpec(
            num_scalar_prefetch=1,
            grid=(count,),
            in_specs=[vmem] * (5 + len(state)),
            out_specs=[vmem, vmem],
        ),
        out_shape=[
            pltpu.VMEM((groups, rows, wide), F32),
            pltpu.VMEM((groups, rows, HD), F32),
        ],
        input_output_aliases={6: 0, 7: 1} if state else {},
        compiler_params=params(16),
        cost_estimate=pl.CostEstimate(
            flops=4 * GQ * rows * rows * 2 * 2 * HD, bytes_accessed=4 * 2**20, transcendentals=0
        ),
        name="prefill_near",
    )(scalars, *map(in_vmem, (q, qf, own, sib, kf, *state)))


def prefill_far(scalars, q, qf, far, farsib, kf, state, after, earlier=None):
    rows, width = q.shape
    wide = STATE * HD
    early = earlier is None
    if early:
        columns = pl.BlockSpec((rows, wide), lambda g, sc: (0, jnp.minimum(g, jnp.maximum(sc[S_EARLY], 1) - 1)))
    else:
        columns = pl.BlockSpec((rows, wide), lambda g, sc: (0, jnp.maximum(g, sc[S_EARLY])))
    vmem = pl.BlockSpec(memory_space=pltpu.VMEM)
    hbm = pl.BlockSpec(memory_space=pl.ANY)
    extra = list(after) + ([] if early else [earlier])
    return pl.pallas_call(
        functools.partial(far_kernel, early=early),
        grid_spec=pltpu.PrefetchScalarGridSpec(
            num_scalar_prefetch=1,
            grid=(EARLY_MOST if early else width // wide,),
            in_specs=[vmem] * 7 + [hbm] * len(extra),
            out_specs=columns,
        ),
        out_shape=pltpu.HBM(q.shape, BF16),
        input_output_aliases={} if early else {7 + len(extra): 0},
        compiler_params=params(16),
        cost_estimate=pl.CostEstimate(
            flops=4 * GQ * rows * rows * 2 * 2 * HD, bytes_accessed=4 * 2**20, transcendentals=0
        ),
        name="prefill_far",
    )(scalars, *map(in_vmem, (q, qf, far, farsib, kf, *state)), *extra)


def context_kernel(sc, q_ref, ck_ref, cv_ref, own_ref, acc_ref, ml_ref, *, steps):
    srows = q_ref.shape[0]
    n = ck_ref.shape[0]
    block = 1024
    live = sc[S_LEN]
    lane = lax.broadcasted_iota(jnp.int32, (srows, HD), 1)
    q_mark = jnp.where(lane == 0, 1.0, 0.0).astype(BF16)
    zero = jnp.zeros((srows, HD), BF16)
    at_row = lax.broadcasted_iota(jnp.int32, (DEC * srows, srows), 0) % srows
    at_col = lax.broadcasted_iota(jnp.int32, (DEC * srows, srows), 1)
    own_mask = (at_row // steps == at_col // steps) & (at_col <= at_row)
    keys = {}
    for first in range(0, n, block):
        pos = lax.broadcasted_iota(jnp.int32, (block, HD), 0) + first
        col = lax.broadcasted_iota(jnp.int32, (block, HD), 1)
        mark = jnp.where((pos >= live) & (col == 0), HIDE, 0.0).astype(BF16)
        for kvh in (0, 1):
            r, c = slice(first, first + block), slice(kvh * HD, (kvh + 1) * HD)
            keys[kvh, first] = jnp.concatenate([ck_ref[r, c], mark], 1), with_ones(cv_ref[r, c])
    state = {}
    ml = [jnp.zeros((srows, HD), F32)]

    def query(g):
        cut = [q_ref[:, h * HD : (h + 1) * HD] for h in range(g * DEC, (g + 1) * DEC)]
        return jnp.concatenate([jnp.concatenate([q, q_mark], 1) for q in cut], 0)

    def score(item):
        g, first = item
        kvh = g * DEC // GQ
        if first < 0:
            s = scores(query(g), jnp.concatenate([own_ref[2 * kvh], zero], 1))
            return jnp.where(own_mask, s, HIDE)
        return scores(query(g), keys[kvh, first][0])

    def finish(item, s):
        g, first = item
        kvh = g * DEC // GQ
        v = with_ones(own_ref[2 * kvh + 1]) if first < 0 else keys[kvh, first][1]
        state[g] = settle(s, v, state.get(g))
        if first == n - block:
            m, acc = state[g]
            for i in range(DEC):
                at = g * DEC + i
                a = acc[i * srows : (i + 1) * srows]
                acc_ref[:, at * HD : (at + 1) * HD] = a[:, :HD]
                ml[0] = jnp.where(lane == at, m[i * srows : (i + 1) * srows], ml[0])
                ml[0] = jnp.where(lane == 2 * GQ + at, a[:, HD:], ml[0])

    groups = 2 * GQ // DEC
    in_turn([(g, first) for g in range(groups) for first in [-1, *range(0, n, block)]], score, finish)
    ml_ref[...] = ml[0]


def context_part(scalars, q, ck, cv, own, steps):
    srows, width = q.shape[0], q.shape[1] - HD
    return pl.pallas_call(
        functools.partial(context_kernel, steps=steps),
        grid_spec=pltpu.PrefetchScalarGridSpec(
            num_scalar_prefetch=1,
            grid=(1,),
            in_specs=[pl.BlockSpec(memory_space=pltpu.VMEM)] * 4,
            out_specs=[
                pl.BlockSpec((srows, width), lambda i, sc: (0, 0)),
                pl.BlockSpec((srows, HD), lambda i, sc: (0, 0)),
            ],
        ),
        out_shape=[
            jax.ShapeDtypeStruct((srows, width), F32),
            jax.ShapeDtypeStruct((srows, HD), F32),
        ],
        compiler_params=params(12),
        name="context_part",
    )(scalars, q, in_vmem(ck), in_vmem(cv), own)


DEC = 8


def pieces(x):
    hi = x.astype(BF16)
    rest = x - hi.astype(F32)
    mid = rest.astype(BF16)
    return hi, mid, (rest - mid.astype(F32)).astype(BF16)


def turn_kernel(sc, p0, p1, p2, p3, own, sib, far, fs, xp, xps, xm, xms, kfo, kfx, o0, o1, o2, o3, ks, vs, qs, os):
    head = pl.program_id(0)
    srows = p0.shape[0]
    rows = own.shape[1]
    keys = 4 * rows
    wide = GQ * HD
    for which, refs, first, kf in ((0, (own, sib, far, fs), S_OWN, kfo), (1, (xp, xps, xm, xms), S_XP, kfx)):
        wanted = [(sc[S_REL + j] != 0) & (sc[S_WHICH + j] == which) for j in range(4)]

        @pl.when(wanted[0] | wanted[1] | wanted[2] | wanted[3])
        def _():
            ks[which, :, HD:] = kf[...]
            vs[which, :, HD:] = jnp.ones((keys, HD), BF16)
            for i, ref in enumerate(refs):
                at = pl.multiple_of((sc[first] ^ i) * rows, rows)
                ks[which, pl.ds(at, rows), :HD] = ref[2 * head]
                vs[which, pl.ds(at, rows), :HD] = ref[2 * head + 1]

    for j, p in enumerate((p0, p1, p2, p3)):

        @pl.when(sc[S_REL + j] != 0)
        def _():
            qs[j, :, :wide] = p[:, pl.ds(pl.multiple_of(head * wide, wide), wide)]
            qs[j, :, wide:] = p[:, 2 * wide :]

    lane = lax.broadcasted_iota(jnp.int32, (srows, HD), 1)
    block = 1024

    def one(j, carry):
        @pl.when(sc[S_REL + j] != 0)
        def _():
            which = sc[S_WHICH + j]
            feat = qs[j, :, wide:]
            state = {}
            ml = [jnp.zeros((srows, HD), F32)] * 2

            def score(item):
                g, first = item
                cut = [qs[j, :, h * HD : (h + 1) * HD] for h in range(g * DEC, (g + 1) * DEC)]
                q = jnp.concatenate([jnp.concatenate([q, feat], 1) for q in cut], 0)
                return scores(q, ks[which, first : first + block, :])

            def finish(item, s):
                g, first = item
                state[g] = settle(s, vs[which, first : first + block, :], state.get(g))
                if first == keys - block:
                    m, acc = state[g]
                    for i in range(DEC):
                        h = g * DEC + i
                        r = slice(i * srows, (i + 1) * srows)
                        os[j, :, h * HD : (h + 1) * HD] = acc[r, :HD].astype(BF16)
                        for part in range(3):
                            ml[0] = jnp.where(lane == part * GQ + h, m[r], ml[0])
                            ml[1] = jnp.where(lane == (part + 3) * GQ + h, acc[r, HD:], ml[1])

            in_turn([(g, first) for first in range(0, keys, block) for g in range(GQ // DEC)], score, finish)
            m3, l3 = pieces(ml[0]), pieces(ml[1])
            ext = jnp.zeros((srows, HD), F32)
            for part in range(3):
                ext = jnp.where(lane // GQ == part, m3[part].astype(F32), ext)
                ext = jnp.where(lane // GQ == part + 3, l3[part].astype(F32), ext)
            os[j, :, wide:] = ext.astype(BF16)

        return carry

    lax.fori_loop(0, 4, one, 0)
    for j, o in enumerate((o0, o1, o2, o3)):
        o[...] = os[j]


def turn_part(scalars, packets, kvs, kf_own, kf_other, after):
    srows = packets[0].shape[0]
    rows = kvs[0].shape[1]
    wide = GQ * HD + HD

    def kernel(*refs):
        turn_kernel(*refs[:15], *refs[15 + len(after) :])

    return pl.pallas_call(
        kernel,
        grid_spec=pltpu.PrefetchScalarGridSpec(
            num_scalar_prefetch=1,
            grid=(2,),
            in_specs=[pl.BlockSpec(memory_space=pltpu.VMEM)] * 14
            + [pl.BlockSpec(memory_space=pl.ANY)] * len(after),
            out_specs=[pl.BlockSpec((srows, wide), lambda g, sc: (0, g))] * 4,
            scratch_shapes=[
                pltpu.VMEM((2, 4 * rows, 2 * HD), BF16),
                pltpu.VMEM((2, 4 * rows, 2 * HD), BF16),
                pltpu.VMEM((4, srows, wide), BF16),
                pltpu.VMEM((4, srows, wide), BF16),
            ],
        ),
        out_shape=[jax.ShapeDtypeStruct((srows, 2 * wide), BF16)] * 4,
        compiler_params=params(20),
        cost_estimate=pl.CostEstimate(
            flops=4 * 4 * srows * GQ * 4 * rows * 2 * HD, bytes_accessed=4 * 2**20, transcendentals=0
        ),
        name="turn_part",
    )(scalars, *map(in_vmem, packets), *map(in_vmem, kvs), in_vmem(kf_own), in_vmem(kf_other), *after)


def merge_kernel(sc, acc_ref, ml_ref, *refs):
    o_ref, wide = refs[-2:]
    sel = sc[S_SEL]
    groups, steps, _ = o_ref.shape
    ml = ml_ref[...]
    width = GQ * HD
    for kvh in range(2):
        first = kvh * (width + HD)

        def pick(cols):
            cols = slice(first + cols.start, first + cols.stop)
            x = refs[0][:, cols]
            for j in (1, 2, 3):
                x = jnp.where(sel == j, refs[j][:, cols], x)
            return x.astype(F32)

        ext = pick(slice(width, width + HD))
        whole = [
            ext[:, i * GQ : (i + 1) * GQ]
            + ext[:, (i + 1) * GQ : (i + 2) * GQ]
            + ext[:, (i + 2) * GQ : (i + 3) * GQ]
            for i in (0, 3)
        ]
        m2, l2 = whole
        m1 = ml[:, kvh * GQ : (kvh + 1) * GQ]
        l1 = ml[:, (2 + kvh) * GQ : (3 + kvh) * GQ]
        m = jnp.maximum(m1, m2)
        w1, w2 = jnp.exp2((m1 - m) * SCALE), jnp.exp2((m2 - m) * SCALE)
        total = l1 * w1 + l2 * w2
        w1, w2 = w1 / total, w2 / total
        for h in range(GQ):
            at = kvh * GQ + h
            a1 = acc_ref[:, at * HD : (at + 1) * HD]
            a2 = pick(slice(h * HD, (h + 1) * HD))
            wide[:, at * HD : (at + 1) * HD] = a1 * w1[:, h : h + 1] + a2 * w2[:, h : h + 1]
    for r in range(groups):
        o_ref[r] = wide[r * steps : (r + 1) * steps, :].astype(BF16)


def merge(scalars, acc, ml, back, steps):
    args = (acc, ml, *back)
    shape = (acc.shape[0] // steps, steps, acc.shape[1])
    return pl.pallas_call(
        merge_kernel,
        grid_spec=pltpu.PrefetchScalarGridSpec(
            num_scalar_prefetch=1,
            grid=(1,),
            in_specs=[pl.BlockSpec(a.shape, lambda i, sc: (0, 0)) for a in args],
            out_specs=pl.BlockSpec(shape, lambda i, sc: (0, 0, 0)),
            scratch_shapes=[pltpu.VMEM(acc.shape, F32)],
        ),
        out_shape=jax.ShapeDtypeStruct(shape, BF16),
        compiler_params=params(8),
        name="merge",
    )(scalars, *args)


ROW = ("xlo", "xhi")


def row_index(x):
    return x % 2 * 2 + x // 2


def from_x(a, shift):
    return lax.ppermute(a, ROW, [(row_index((x + shift) % 4), row_index(x)) for x in range(4)])


def from_y(a, shift):
    return lax.ppermute(a, "y", [((y + shift) % 4, y) for y in range(4)])


def from_core(a):
    return lax.ppermute(a, "core", [(0, 1), (1, 0)])


def body(
    turn_hidden,
    w_key,
    w_value,
    turn_queries,
    turn_speaker,
    speaker_mask,
    shard_block,
    context_keys,
    context_values,
    context_length,
    decode_home,
    step_hidden,
    step_queries,
    row_speaker,
):
    steps = step_hidden.shape[1]
    tie = lax.optimization_barrier
    own, step_kv = project(turn_hidden, step_hidden, w_key, w_value)
    far, sib, xp, xm = from_x(own, 2), from_core(own), from_x(own, 1), from_x(own, 3)
    sib, shard_block = tie((sib, shard_block))
    scalars, qf, kf_own, kf_other, packet = prepare(
        shard_block, decode_home, context_length, speaker_mask, row_speaker, turn_speaker, step_queries
    )
    packets = [packet, from_y(packet, 1), None, from_y(packet, 3)]
    near = list(prefill_near(scalars, turn_queries, qf, own, sib, kf_own, 0, 2))
    packets[0], packets[1], packets[3], near[0] = tie((packets[0], packets[1], packets[3], near[0]))
    packets[2] = from_y(packets[0], 2)
    near = list(prefill_near(scalars, turn_queries, qf, own, sib, kf_own, 2, 2, near))
    packets[0], packets[2], near[0] = tie((packets[0], packets[2], near[0]))
    ctx = context_part(scalars, packets[0], context_keys, context_values, step_kv, steps)
    far, xp, xm, _ = tie((far, xp, xm, ctx[1]))
    farsib, xps, xms = from_core(far), from_core(xp), from_core(xm)
    early = prefill_far(scalars, turn_queries, qf, far, farsib, kf_own, near, ())
    early, kf_other = tie((early, kf_other))
    moved = (own, sib, far, farsib, xp, xps, xm, xms)
    parts = turn_part(scalars, packets, moved, kf_own, kf_other, ())
    back = [parts[0]] + [from_y(parts[j], -j) for j in (1, 2, 3)]
    turn_attention = prefill_far(
        scalars, turn_queries, qf, far, farsib, kf_own, near, (parts[0],), early
    )
    step_attention = merge(scalars, *ctx, back, steps)
    return turn_attention, step_attention


def solution(mesh):
    heads = mesh.shape["head"]
    fine = Mesh(mesh.devices.reshape(2, 4, 2, 2, heads), ("xlo", "y", "xhi", "core", "head"))
    split = ("xlo", "y", "xhi", "core")
    return jax.shard_map(
        body,
        mesh=fine,
        in_specs=(
            P(split, None),
            P(None, "head"),
            P(None, "head"),
            P(split, "head"),
            P(),
            P(),
            P(),
            P(split, "head"),
            P(split, "head"),
            P(),
            P(),
            P(split, None, None),
            P(split, None, "head"),
            P(split),
        ),
        out_specs=(P(split, "head"), P(split, None, "head")),
        check_vma=False,
    )
```

```python
import functools
import math

import jax
import jax.numpy as jnp
from jax import lax
from jax.experimental import pallas as pl
from jax.experimental.pallas import tpu as pltpu
from jax.sharding import Mesh
from jax.sharding import PartitionSpec as P

HQ = 64
KVH = 8
HD = 128
SPK = 4
GQ = HQ // KVH

HIDE = -1e30
SCALE = math.log2(math.e) / math.sqrt(HD)
NT = (((1,), (1,)), ((), ()))
F32 = jnp.float32
BF16 = jnp.bfloat16

S_OWN, S_SIB, S_FAR, S_FARSIB, S_REL, S_WHICH, S_SEL, S_LEN, S_XP, S_EARLY = 0, 1, 2, 3, 4, 8, 12, 13, 14, 15


def params(mib):
    return pltpu.CompilerParams(vmem_limit_bytes=mib * 2**20)


def in_vmem(x):
    return pltpu.with_memory_space_constraint(x, pltpu.VMEM)


def in_hbm(x):
    return pltpu.with_memory_space_constraint(x, pltpu.HBM)


def over(x, y):
    r = pl.reciprocal(y, approx=True)
    return x * (r * (2.0 - y * r))


def with_ones(v):
    return jnp.concatenate([v, jnp.ones(v.shape, BF16)], 1)


def marks(table, speakers):
    row = lax.broadcasted_iota(jnp.int32, (8, HD), 0)
    hot = jnp.where(speakers == row, 1.0, 0.0).astype(BF16)
    out = lax.dot_general(hot, table, (((0,), (0,)), ((), ())), preferred_element_type=F32)
    return out.astype(BF16)


def prep_kernel(blocks, homes, lengths, mask, row_spk, spk_ref, q_ref, sc, qf_ref, kfo_ref, kfx_ref, pk_ref, wide):
    fill_packet(row_spk, q_ref, pk_ref, wide)
    xlo, y, xhi, core = (lax.axis_index(a) for a in ("xlo", "y", "xhi", "core"))
    own_at = xhi * 2 + core
    dialog = xlo * 4 + y
    here = blocks[dialog * 4 + own_at]
    sc[S_OWN] = own_at
    for i, at in ((1, S_SIB), (2, S_FAR), (3, S_FARSIB)):
        sc[at] = jnp.where(blocks[dialog * 4 + (own_at ^ i)] < here, 1, 0)
    for j in range(4):
        home = homes[xlo * 16 + (y + j) % 4 * 4 + own_at]
        sc[S_REL + j] = jnp.where(home % 4 == y, 1, 0)
        sc[S_WHICH + j] = jnp.where(home // 4 != xlo, 1, 0)
    home = homes[xlo * 16 + y * 4 + own_at]
    sc[S_SEL] = (y - home % 4 + 4) % 4
    sc[S_LEN] = lengths[home]
    sc[S_XP] = (xhi ^ xlo) * 2 + core

    most = jnp.int32(0)
    mine = jnp.int32(0)
    for c in range(8):
        rows_of = [homes[c // 4 * 16 + at * 4 + c % 4] % 4 for at in range(4)]
        for at in range(4):
            count = sum(jnp.where(r == at, 1, 0) for r in rows_of)
            most = jnp.maximum(most, count)
            mine = jnp.where((c == xlo * 4 + own_at) & (y == at), count, mine)
    sc[S_EARLY] = jnp.minimum(((most - mine) * 7 + 5) // 10, EARLY_MOST)

    row = lax.broadcasted_iota(jnp.int32, (8, HD), 0)
    lane = lax.broadcasted_iota(jnp.int32, (8, HD), 1)
    for d, out in ((dialog, kfo_ref), ((1 - xlo) * 4 + y, kfx_ref)):
        table = jnp.zeros((8, HD), F32)
        for a in range(SPK):
            for b in range(SPK):
                add = jnp.where(mask[a, b, d] == 1, 0.0, HIDE)
                table = jnp.where((row == b) & (lane == a), add, table)
        table = table.astype(BF16)
        for i in range(16):
            out[i * HD : (i + 1) * HD, :] = marks(table, spk_ref[d * 2 + i // 8, i % 8 : i % 8 + 1, :])
    eye = jnp.where((row == lane) & (row < SPK), 1.0, 0.0).astype(BF16)
    for i in range(4):
        at = (dialog * 4 + own_at) * 4 + i
        qf_ref[i * HD : (i + 1) * HD, :] = marks(eye, spk_ref[at // 8, pl.ds(at % 8, 1), :])


def prepare(blocks, homes, lengths, mask, row_spk, spk, queries):
    groups, steps, width = queries.shape
    rows = spk.size // 32
    smem = pl.BlockSpec(memory_space=pltpu.SMEM)
    vmem = pl.BlockSpec(memory_space=pltpu.VMEM)
    return pl.pallas_call(
        prep_kernel,
        in_specs=[smem] * 5 + [vmem] * 2,
        out_specs=[smem] + [vmem] * 4,
        out_shape=[
            jax.ShapeDtypeStruct((16,), jnp.int32),
            pltpu.VMEM((rows, HD), BF16),
            pltpu.VMEM((4 * rows, HD), BF16),
            pltpu.VMEM((4 * rows, HD), BF16),
            pltpu.VMEM((groups * steps, width + HD), BF16),
        ],
        scratch_shapes=[pltpu.VMEM((groups * steps, width), F32)],
        compiler_params=params(8),
        name="prepare",
    )(blocks, homes, lengths, mask.transpose(1, 2, 0), row_spk, spk.reshape(-1, 8, HD), queries)


def fill_packet(row_spk, q_ref, pk_ref, wide):
    groups, steps, width = q_ref.shape
    srows = groups * steps
    for r in range(groups):
        wide[r * steps : (r + 1) * steps, :] = q_ref[r].astype(F32)
    pk_ref[:, :width] = wide[...].astype(BF16)
    row = lax.broadcasted_iota(jnp.int32, (srows, HD), 0)
    lane = lax.broadcasted_iota(jnp.int32, (srows, HD), 1)
    speaker = jnp.zeros((srows, HD), jnp.int32)
    for r in range(groups):
        speaker = jnp.where(row // steps == r, row_spk[r], speaker)
    pk_ref[:, width:] = jnp.where(lane == speaker, 1.0, 0.0).astype(BF16)


def project_kernel(x_hbm, s_hbm, wk_hbm, wv_hbm, kv_ref, skv_ref, xb, sb, wkb, wvb, wide, sem, *, chunk):
    groups, steps, depth = s_hbm.shape
    copies = []
    for i in range(depth // chunk):
        c = pl.ds(i * chunk, chunk)
        pairs = [
            (x_hbm.at[:, c], xb.at[:, c]),
            (wk_hbm.at[c, :], wkb.at[c, :]),
            (wv_hbm.at[c, :], wvb.at[c, :]),
        ]
        copies.append([pltpu.make_async_copy(a, b, sem.at[i, n]) for n, (a, b) in enumerate(pairs)])
        for copy in copies[-1]:
            copy.start()
        if i == 0:
            step_copy = pltpu.make_async_copy(s_hbm, sb, sem.at[0, 3])
            step_copy.start()
    acc = None
    for i, these in enumerate(copies):
        for copy in these:
            copy.wait()
        c = slice(i * chunk, (i + 1) * chunk)
        w = jnp.concatenate([wkb[c, :], wvb[c, :]], 1)
        if i == 0:
            step_copy.wait()
        for r in range(groups):
            wide[r * steps : (r + 1) * steps, c] = sb[r, :, c].astype(F32)
        both = jnp.concatenate([xb[:, c], wide[:, c].astype(BF16)], 0)
        part = jnp.dot(both, w, preferred_element_type=F32)
        acc = part if acc is None else acc + part
    rows = xb.shape[0]
    for at, first in enumerate((0, 2 * HD, HD, 3 * HD)):
        kv_ref[at] = acc[:rows, first : first + HD].astype(BF16)
        skv_ref[at] = acc[rows:, first : first + HD].astype(BF16)


def project(x, steps, w_key, w_value):
    rows, depth = x.shape
    srows = steps.shape[0] * steps.shape[1]
    chunk = 1024
    hbm = pl.BlockSpec(memory_space=pl.ANY)
    vmem = pl.BlockSpec(memory_space=pltpu.VMEM)
    return pl.pallas_call(
        functools.partial(project_kernel, chunk=chunk),
        in_specs=[hbm] * 4,
        out_specs=[vmem] * 2,
        out_shape=[
            jax.ShapeDtypeStruct((4, rows, HD), BF16),
            jax.ShapeDtypeStruct((4, srows, HD), BF16),
        ],
        scratch_shapes=[
            pltpu.VMEM(x.shape, BF16),
            pltpu.VMEM(steps.shape, BF16),
            pltpu.VMEM(w_key.shape, BF16),
            pltpu.VMEM(w_value.shape, BF16),
            pltpu.VMEM((srows, depth), F32),
            pltpu.SemaphoreType.DMA((depth // chunk, 4)),
        ],
        compiler_params=params(28),
        cost_estimate=pl.CostEstimate(
            flops=2 * (rows + srows) * depth * 4 * HD,
            bytes_accessed=2 * depth * (rows + srows + 4 * HD),
            transcendentals=0,
        ),
        name="project",
    )(*map(in_hbm, (x, steps, w_key, w_value)))


def scores(q, k):
    return lax.dot_general(q, k, NT, preferred_element_type=F32)


def settle(s, v, state=None):
    m = jnp.max(s, axis=1, keepdims=True)
    if state is not None:
        m = jnp.maximum(m, state[0])
    p = jnp.exp2((s - m) * SCALE).astype(BF16)
    acc = jnp.dot(p, v, preferred_element_type=F32)
    if state is not None:
        acc = acc + state[1] * jnp.exp2((state[0] - m) * SCALE)
    return m, acc


def in_turn(items, score, finish):
    ahead = score(items[0])
    for i, item in enumerate(items):
        now = ahead
        if i + 1 < len(items):
            ahead = score(items[i + 1])
        finish(item, now)


def keys_of(k, kf):
    return jnp.concatenate([k, kf], 1)


def shown(marks_of_keys, flag):
    return marks_of_keys + jnp.where(flag != 0, 0.0, HIDE).astype(BF16)


def query_of(q_ref, qf_ref, group, h, first, count):
    q = q_ref[first : first + count, pl.ds(pl.multiple_of(group * STATE * HD, HD) + h * HD, HD)]
    return jnp.concatenate([q, qf_ref[first : first + count, :]], 1)


def near_kernel(sc, q_ref, qf_ref, own_ref, sib_ref, kf_ref, *refs, first):
    acc_ref, ml_ref = refs[-2:]
    group = pl.program_id(0) + first
    kvh = group * STATE // GQ
    rows = q_ref.shape[0]
    half = rows // 2
    own = pl.multiple_of(sc[S_OWN] * rows, rows)
    sib = pl.multiple_of((sc[S_OWN] ^ 1) * rows, rows)
    lane = lax.broadcasted_iota(jnp.int32, (half, HD), 1)

    k = keys_of(own_ref[2 * kvh], kf_ref[pl.ds(own, rows), :])
    v = with_ones(own_ref[2 * kvh + 1])
    late = keys_of(sib_ref[2 * kvh], shown(kf_ref[pl.ds(sib, rows), :], sc[S_SIB]))
    late_v = with_ones(sib_ref[2 * kvh + 1])
    ks = [jnp.concatenate([k[:half], late], 0), jnp.concatenate([k, late], 0)]
    vs = [jnp.concatenate([v[:half], late_v], 0), jnp.concatenate([v, late_v], 0)]
    ml = [jnp.zeros((half, HD), F32)] * 2

    def score(item):
        h, part = item
        q = [query_of(q_ref, qf_ref, group, h + i, part * half, half) for i in range(HN)]
        s = scores(jnp.concatenate(q, 0), ks[part])
        own_cols = (part + 1) * half
        at_row = lax.broadcasted_iota(jnp.int32, (HN * half, half), 0) % half
        at_col = lax.broadcasted_iota(jnp.int32, (HN * half, half), 1)
        corner = jnp.where(at_col <= at_row, s[:, own_cols - half : own_cols], HIDE)
        cut = [s[:, : own_cols - half]] * (part > 0) + [corner, s[:, own_cols:]]
        return jnp.concatenate(cut, 1)

    def finish(item, s):
        h0, part = item
        ms, accs = settle(s, vs[part])
        for i in range(HN):
            h = h0 + i
            m, acc = ms[i * half : (i + 1) * half], accs[i * half : (i + 1) * half]
            acc_ref[group, part * half : (part + 1) * half, h * HD : (h + 1) * HD] = acc[:, :HD]
            ml[part] = jnp.where(lane == h, m, jnp.where(lane == STATE + h, acc[:, HD:], ml[part]))

    in_turn([(h, part) for h in range(0, STATE, HN) for part in (0, 1)], score, finish)
    for part in (0, 1):
        ml_ref[group, part * half : (part + 1) * half, :] = ml[part]


def far_kernel(sc, q_ref, qf_ref, far_ref, fs_ref, kf_ref, acc_ref, ml_ref, *rest, early):
    group = pl.program_id(0)
    kvh = group * STATE // GQ
    o_ref = rest[-1]
    rows = q_ref.shape[0]
    half = rows // 2
    far = pl.multiple_of((sc[S_OWN] ^ 2) * rows, rows)
    farsib = pl.multiple_of((sc[S_OWN] ^ 3) * rows, rows)

    def run(seen):
        if seen == 1:
            take = sc[S_FAR] != 0
            at = pl.multiple_of(jnp.where(take, far, farsib), rows)
            k = keys_of(jnp.where(take, far_ref[2 * kvh], fs_ref[2 * kvh]), kf_ref[pl.ds(at, rows), :])
            v = with_ones(jnp.where(take, far_ref[2 * kvh + 1], fs_ref[2 * kvh + 1]))
        if seen == 2:
            blocks = [(far_ref, far, S_FAR), (fs_ref, farsib, S_FARSIB)]
            k = [keys_of(x[2 * kvh], shown(kf_ref[pl.ds(at, rows), :], sc[flag])) for x, at, flag in blocks]
            k = jnp.concatenate(k, 0)
            v = jnp.concatenate([with_ones(x[2 * kvh + 1]) for x, _, _ in blocks], 0)

        def score(item):
            q = [query_of(q_ref, qf_ref, group, item + i, 0, rows) for i in range(HF)]
            return scores(jnp.concatenate(q, 0), k) if seen else None

        def finish(item, s):
            state = []
            for h in range(item, item + HF):
                ml = ml_ref[group]
                l = jnp.broadcast_to(ml[:, STATE + h : STATE + h + 1], (rows, HD))
                acc = jnp.concatenate([acc_ref[group, :, h * HD : (h + 1) * HD], l], 1)
                state.append((ml[:, h : h + 1], acc))
            m = jnp.concatenate([x[0] for x in state], 0)
            acc = jnp.concatenate([x[1] for x in state], 0)
            if seen:
                acc = settle(s, v, (m, acc))[1]
            out = over(acc[:, :HD], acc[:, HD:]).astype(BF16)
            for i in range(HF):
                o_ref[:, (item + i) * HD : (item + i + 1) * HD] = out[i * rows : (i + 1) * rows]

        in_turn(list(range(0, STATE, HF)), score, finish)

    mine = (group < sc[S_EARLY]) == early
    count = sc[S_FAR] + sc[S_FARSIB]
    pl.when(mine & (count == 0))(functools.partial(run, 0))
    if early:
        pl.when(mine & (count != 0))(functools.partial(run, 2))
    else:
        pl.when(mine & (count == 1))(functools.partial(run, 1))
        pl.when(mine & (count == 2))(functools.partial(run, 2))


STATE = 4
EARLY_MOST = 2
HN = 2
HF = 1


def prefill_near(scalars, q, qf, own, sib, kf, first, count, state=()):
    rows, width = q.shape
    wide = STATE * HD
    groups = width // wide
    vmem = pl.BlockSpec(memory_space=pltpu.VMEM)
    return pl.pallas_call(
        functools.partial(near_kernel, first=first),
        grid_spec=pltpu.PrefetchScalarGridSpec(
            num_scalar_prefetch=1,
            grid=(count,),
            in_specs=[vmem] * (5 + len(state)),
            out_specs=[vmem, vmem],
        ),
        out_shape=[
            pltpu.VMEM((groups, rows, wide), F32),
            pltpu.VMEM((groups, rows, HD), F32),
        ],
        input_output_aliases={6: 0, 7: 1} if state else {},
        compiler_params=params(16),
        cost_estimate=pl.CostEstimate(
            flops=4 * GQ * rows * rows * 2 * 2 * HD, bytes_accessed=4 * 2**20, transcendentals=0
        ),
        name="prefill_near",
    )(scalars, *map(in_vmem, (q, qf, own, sib, kf, *state)))


def prefill_far(scalars, q, qf, far, farsib, kf, state, after, earlier=None):
    rows, width = q.shape
    wide = STATE * HD
    early = earlier is None
    if early:
        columns = pl.BlockSpec((rows, wide), lambda g, sc: (0, jnp.minimum(g, jnp.maximum(sc[S_EARLY], 1) - 1)))
    else:
        columns = pl.BlockSpec((rows, wide), lambda g, sc: (0, jnp.maximum(g, sc[S_EARLY])))
    vmem = pl.BlockSpec(memory_space=pltpu.VMEM)
    hbm = pl.BlockSpec(memory_space=pl.ANY)
    extra = list(after) + ([] if early else [earlier])
    return pl.pallas_call(
        functools.partial(far_kernel, early=early),
        grid_spec=pltpu.PrefetchScalarGridSpec(
            num_scalar_prefetch=1,
            grid=(EARLY_MOST if early else width // wide,),
            in_specs=[vmem] * 7 + [hbm] * len(extra),
            out_specs=columns,
        ),
        out_shape=pltpu.HBM(q.shape, BF16),
        input_output_aliases={} if early else {7 + len(extra): 0},
        compiler_params=params(16),
        cost_estimate=pl.CostEstimate(
            flops=4 * GQ * rows * rows * 2 * 2 * HD, bytes_accessed=4 * 2**20, transcendentals=0
        ),
        name="prefill_far",
    )(scalars, *map(in_vmem, (q, qf, far, farsib, kf, *state)), *extra)


def context_kernel(sc, q_ref, ck_ref, cv_ref, own_ref, acc_ref, ml_ref, *, steps):
    srows = q_ref.shape[0]
    n = ck_ref.shape[0]
    block = 1024
    live = sc[S_LEN]
    lane = lax.broadcasted_iota(jnp.int32, (srows, HD), 1)
    q_mark = jnp.where(lane == 0, 1.0, 0.0).astype(BF16)
    zero = jnp.zeros((srows, HD), BF16)
    at_row = lax.broadcasted_iota(jnp.int32, (DEC * srows, srows), 0) % srows
    at_col = lax.broadcasted_iota(jnp.int32, (DEC * srows, srows), 1)
    own_mask = (at_row // steps == at_col // steps) & (at_col <= at_row)
    keys = {}
    for first in range(0, n, block):
        pos = lax.broadcasted_iota(jnp.int32, (block, HD), 0) + first
        col = lax.broadcasted_iota(jnp.int32, (block, HD), 1)
        mark = jnp.where((pos >= live) & (col == 0), HIDE, 0.0).astype(BF16)
        for kvh in (0, 1):
            r, c = slice(first, first + block), slice(kvh * HD, (kvh + 1) * HD)
            keys[kvh, first] = jnp.concatenate([ck_ref[r, c], mark], 1), with_ones(cv_ref[r, c])
    state = {}
    ml = [jnp.zeros((srows, HD), F32)]

    def query(g):
        cut = [q_ref[:, h * HD : (h + 1) * HD] for h in range(g * DEC, (g + 1) * DEC)]
        return jnp.concatenate([jnp.concatenate([q, q_mark], 1) for q in cut], 0)

    def score(item):
        g, first = item
        kvh = g * DEC // GQ
        if first < 0:
            s = scores(query(g), jnp.concatenate([own_ref[2 * kvh], zero], 1))
            return jnp.where(own_mask, s, HIDE)
        return scores(query(g), keys[kvh, first][0])

    def finish(item, s):
        g, first = item
        kvh = g * DEC // GQ
        v = with_ones(own_ref[2 * kvh + 1]) if first < 0 else keys[kvh, first][1]
        state[g] = settle(s, v, state.get(g))
        if first == n - block:
            m, acc = state[g]
            for i in range(DEC):
                at = g * DEC + i
                a = acc[i * srows : (i + 1) * srows]
                acc_ref[:, at * HD : (at + 1) * HD] = a[:, :HD]
                ml[0] = jnp.where(lane == at, m[i * srows : (i + 1) * srows], ml[0])
                ml[0] = jnp.where(lane == 2 * GQ + at, a[:, HD:], ml[0])

    groups = 2 * GQ // DEC
    in_turn([(g, first) for g in range(groups) for first in [-1, *range(0, n, block)]], score, finish)
    ml_ref[...] = ml[0]


def context_part(scalars, q, ck, cv, own, steps):
    srows, width = q.shape[0], q.shape[1] - HD
    return pl.pallas_call(
        functools.partial(context_kernel, steps=steps),
        grid_spec=pltpu.PrefetchScalarGridSpec(
            num_scalar_prefetch=1,
            grid=(1,),
            in_specs=[pl.BlockSpec(memory_space=pltpu.VMEM)] * 4,
            out_specs=[
                pl.BlockSpec((srows, width), lambda i, sc: (0, 0)),
                pl.BlockSpec((srows, HD), lambda i, sc: (0, 0)),
            ],
        ),
        out_shape=[
            jax.ShapeDtypeStruct((srows, width), F32),
            jax.ShapeDtypeStruct((srows, HD), F32),
        ],
        compiler_params=params(12),
        name="context_part",
    )(scalars, q, in_vmem(ck), in_vmem(cv), own)


DEC = 8


def pieces(x):
    hi = x.astype(BF16)
    rest = x - hi.astype(F32)
    mid = rest.astype(BF16)
    return hi, mid, (rest - mid.astype(F32)).astype(BF16)


def turn_kernel(sc, p0, p1, p2, p3, own, sib, far, fs, xp, xps, xm, xms, kfo, kfx, o0, o1, o2, o3, ks, vs, qs, os):
    head = pl.program_id(0)
    srows = p0.shape[0]
    rows = own.shape[1]
    keys = 4 * rows
    wide = GQ * HD
    for which, refs, first, kf in ((0, (own, sib, far, fs), S_OWN, kfo), (1, (xp, xps, xm, xms), S_XP, kfx)):
        wanted = [(sc[S_REL + j] != 0) & (sc[S_WHICH + j] == which) for j in range(4)]

        @pl.when(wanted[0] | wanted[1] | wanted[2] | wanted[3])
        def _():
            ks[which, :, HD:] = kf[...]
            vs[which, :, HD:] = jnp.ones((keys, HD), BF16)
            for i, ref in enumerate(refs):
                at = pl.multiple_of((sc[first] ^ i) * rows, rows)
                ks[which, pl.ds(at, rows), :HD] = ref[2 * head]
                vs[which, pl.ds(at, rows), :HD] = ref[2 * head + 1]

    for j, p in enumerate((p0, p1, p2, p3)):

        @pl.when(sc[S_REL + j] != 0)
        def _():
            qs[j, :, :wide] = p[:, pl.ds(pl.multiple_of(head * wide, wide), wide)]
            qs[j, :, wide:] = p[:, 2 * wide :]

    lane = lax.broadcasted_iota(jnp.int32, (srows, HD), 1)
    block = 1024

    def one(j, carry):
        @pl.when(sc[S_REL + j] != 0)
        def _():
            which = sc[S_WHICH + j]
            feat = qs[j, :, wide:]
            state = {}
            ml = [jnp.zeros((srows, HD), F32)] * 2

            def score(item):
                g, first = item
                cut = [qs[j, :, h * HD : (h + 1) * HD] for h in range(g * DEC, (g + 1) * DEC)]
                q = jnp.concatenate([jnp.concatenate([q, feat], 1) for q in cut], 0)
                return scores(q, ks[which, first : first + block, :])

            def finish(item, s):
                g, first = item
                state[g] = settle(s, vs[which, first : first + block, :], state.get(g))
                if first == keys - block:
                    m, acc = state[g]
                    for i in range(DEC):
                        h = g * DEC + i
                        r = slice(i * srows, (i + 1) * srows)
                        os[j, :, h * HD : (h + 1) * HD] = acc[r, :HD].astype(BF16)
                        for part in range(3):
                            ml[0] = jnp.where(lane == part * GQ + h, m[r], ml[0])
                            ml[1] = jnp.where(lane == (part + 3) * GQ + h, acc[r, HD:], ml[1])

            in_turn([(g, first) for first in range(0, keys, block) for g in range(GQ // DEC)], score, finish)
            m3, l3 = pieces(ml[0]), pieces(ml[1])
            ext = jnp.zeros((srows, HD), F32)
            for part in range(3):
                ext = jnp.where(lane // GQ == part, m3[part].astype(F32), ext)
                ext = jnp.where(lane // GQ == part + 3, l3[part].astype(F32), ext)
            os[j, :, wide:] = ext.astype(BF16)

        return carry

    lax.fori_loop(0, 4, one, 0)
    for j, o in enumerate((o0, o1, o2, o3)):
        o[...] = os[j]


def turn_part(scalars, packets, kvs, kf_own, kf_other, after):
    srows = packets[0].shape[0]
    rows = kvs[0].shape[1]
    wide = GQ * HD + HD

    def kernel(*refs):
        turn_kernel(*refs[:15], *refs[15 + len(after) :])

    return pl.pallas_call(
        kernel,
        grid_spec=pltpu.PrefetchScalarGridSpec(
            num_scalar_prefetch=1,
            grid=(2,),
            in_specs=[pl.BlockSpec(memory_space=pltpu.VMEM)] * 14
            + [pl.BlockSpec(memory_space=pl.ANY)] * len(after),
            out_specs=[pl.BlockSpec((srows, wide), lambda g, sc: (0, g))] * 4,
            scratch_shapes=[
                pltpu.VMEM((2, 4 * rows, 2 * HD), BF16),
                pltpu.VMEM((2, 4 * rows, 2 * HD), BF16),
                pltpu.VMEM((4, srows, wide), BF16),
                pltpu.VMEM((4, srows, wide), BF16),
            ],
        ),
        out_shape=[jax.ShapeDtypeStruct((srows, 2 * wide), BF16)] * 4,
        compiler_params=params(20),
        cost_estimate=pl.CostEstimate(
            flops=4 * 4 * srows * GQ * 4 * rows * 2 * HD, bytes_accessed=4 * 2**20, transcendentals=0
        ),
        name="turn_part",
    )(scalars, *map(in_vmem, packets), *map(in_vmem, kvs), in_vmem(kf_own), in_vmem(kf_other), *after)


def merge_kernel(sc, acc_ref, ml_ref, *refs):
    o_ref, wide = refs[-2:]
    sel = sc[S_SEL]
    groups, steps, _ = o_ref.shape
    ml = ml_ref[...]
    width = GQ * HD
    for kvh in range(2):
        first = kvh * (width + HD)

        def pick(cols):
            cols = slice(first + cols.start, first + cols.stop)
            x = refs[0][:, cols]
            for j in (1, 2, 3):
                x = jnp.where(sel == j, refs[j][:, cols], x)
            return x.astype(F32)

        ext = pick(slice(width, width + HD))
        whole = [
            ext[:, i * GQ : (i + 1) * GQ]
            + ext[:, (i + 1) * GQ : (i + 2) * GQ]
            + ext[:, (i + 2) * GQ : (i + 3) * GQ]
            for i in (0, 3)
        ]
        m2, l2 = whole
        m1 = ml[:, kvh * GQ : (kvh + 1) * GQ]
        l1 = ml[:, (2 + kvh) * GQ : (3 + kvh) * GQ]
        m = jnp.maximum(m1, m2)
        w1, w2 = jnp.exp2((m1 - m) * SCALE), jnp.exp2((m2 - m) * SCALE)
        total = l1 * w1 + l2 * w2
        w1, w2 = w1 / total, w2 / total
        for h in range(GQ):
            at = kvh * GQ + h
            a1 = acc_ref[:, at * HD : (at + 1) * HD]
            a2 = pick(slice(h * HD, (h + 1) * HD))
            wide[:, at * HD : (at + 1) * HD] = a1 * w1[:, h : h + 1] + a2 * w2[:, h : h + 1]
    for r in range(groups):
        o_ref[r] = wide[r * steps : (r + 1) * steps, :].astype(BF16)


def merge(scalars, acc, ml, back, steps):
    args = (acc, ml, *back)
    shape = (acc.shape[0] // steps, steps, acc.shape[1])
    return pl.pallas_call(
        merge_kernel,
        grid_spec=pltpu.PrefetchScalarGridSpec(
            num_scalar_prefetch=1,
            grid=(1,),
            in_specs=[pl.BlockSpec(a.shape, lambda i, sc: (0, 0)) for a in args],
            out_specs=pl.BlockSpec(shape, lambda i, sc: (0, 0, 0)),
            scratch_shapes=[pltpu.VMEM(acc.shape, F32)],
        ),
        out_shape=jax.ShapeDtypeStruct(shape, BF16),
        compiler_params=params(8),
        name="merge",
    )(scalars, *args)


ROW = ("xlo", "xhi")


def row_index(x):
    return x % 2 * 2 + x // 2


def from_x(a, shift):
    return lax.ppermute(a, ROW, [(row_index((x + shift) % 4), row_index(x)) for x in range(4)])


def from_y(a, shift):
    return lax.ppermute(a, "y", [((y + shift) % 4, y) for y in range(4)])


def from_core(a):
    return lax.ppermute(a, "core", [(0, 1), (1, 0)])


def body(
    turn_hidden,
    w_key,
    w_value,
    turn_queries,
    turn_speaker,
    speaker_mask,
    shard_block,
    context_keys,
    context_values,
    context_length,
    decode_home,
    step_hidden,
    step_queries,
    row_speaker,
):
    steps = step_hidden.shape[1]
    tie = lax.optimization_barrier
    own, step_kv = project(turn_hidden, step_hidden, w_key, w_value)
    far, sib, xp, xm = from_x(own, 2), from_core(own), from_x(own, 1), from_x(own, 3)
    sib, shard_block = tie((sib, shard_block))
    scalars, qf, kf_own, kf_other, packet = prepare(
        shard_block, decode_home, context_length, speaker_mask, row_speaker, turn_speaker, step_queries
    )
    packets = [packet, from_y(packet, 1), None, from_y(packet, 3)]
    near = list(prefill_near(scalars, turn_queries, qf, own, sib, kf_own, 0, 2))
    packets[0], packets[1], packets[3], near[0] = tie((packets[0], packets[1], packets[3], near[0]))
    packets[2] = from_y(packets[0], 2)
    near = list(prefill_near(scalars, turn_queries, qf, own, sib, kf_own, 2, 2, near))
    packets[0], packets[2], near[0] = tie((packets[0], packets[2], near[0]))
    ctx = context_part(scalars, packets[0], context_keys, context_values, step_kv, steps)
    far, xp, xm, _ = tie((far, xp, xm, ctx[1]))
    farsib, xps, xms = from_core(far), from_core(xp), from_core(xm)
    early = prefill_far(scalars, turn_queries, qf, far, farsib, kf_own, near, ())
    early, kf_other = tie((early, kf_other))
    moved = (own, sib, far, farsib, xp, xps, xm, xms)
    parts = turn_part(scalars, packets, moved, kf_own, kf_other, ())
    back = [parts[0]] + [from_y(parts[j], -j) for j in (1, 2, 3)]
    turn_attention = prefill_far(
        scalars, turn_queries, qf, far, farsib, kf_own, near, (parts[0],), early
    )
    step_attention = merge(scalars, *ctx, back, steps)
    return turn_attention, step_attention


def solution(mesh):
    heads = mesh.shape["head"]
    fine = Mesh(mesh.devices.reshape(2, 4, 2, 2, heads), ("xlo", "y", "xhi", "core", "head"))
    split = ("xlo", "y", "xhi", "core")
    return jax.shard_map(
        body,
        mesh=fine,
        in_specs=(
            P(split, None),
            P(None, "head"),
            P(None, "head"),
            P(split, "head"),
            P(),
            P(),
            P(),
            P(split, "head"),
            P(split, "head"),
            P(),
            P(),
            P(split, None, None),
            P(split, None, "head"),
            P(split),
        ),
        out_specs=(P(split, "head"), P(split, None, "head")),
        check_vma=False,
    )
```
